128 devices in a mesh: ha: 16 (over y_hi, x, core), wa: 8 (over y_lo, z).
Axes of the slice: x: 4, y: 4 (y_hi: 2, y_lo: 2; y = y_hi * 2 + y_lo), z: 4, core: 2. Of those that a mesh axis runs over, the one named last changes fastest.
Arguments:
- hw_plane: bfloat16 [512, 1024, 128], P('ha', 'wa'), may hold values from -200 to 200
- zh_plane: bfloat16 [64, 512, 128], P(None, 'ha'), may hold values from -5 to 5
- wz_plane: bfloat16 [1024, 64, 128], P('wa'), may hold values from -5 to 5
- w_in: bfloat16 [128, 256], replicated, may hold values from -0.5 to 0.5
- b_in: float32 [256], replicated, may hold values from -3 to 3
- w_out: bfloat16 [256, 18], replicated, may hold values from -0.75 to 0.75
- b_out: float32 [18], replicated, may hold values from -3 to 3
- run_index: int32 [128, 512], P(('ha', 'wa')), may hold values from 0 to 2047, as said below
- run_count: int32 [128], P(('ha', 'wa')), may hold values from 1 to 511, as said below
- labels: int32 [128, 512, 128], P(('ha', 'wa')), may hold values from 0 to 17
Outputs:
- hw_grad: float32 [512, 1024, 128], P('ha', 'wa')
- zh_grad: float32 [64, 512, 128], P('wa', 'ha')
- wz_grad: float32 [1024, 64, 128], P('wa', 'ha')
- w_in_grad: float32 [128, 256], replicated
- b_in_grad: float32 [256], replicated
- w_out_grad: float32 [256, 18], replicated
- b_out_grad: float32 [18], replicated
The draws below stay inside these ranges and needn't reach their ends.
Inputs may be any that keep to these rules, and one draw needn't show every extreme that they name: `run_index`: each row holds 512 different run positions of one device block. `run_count`: the counts of block k and of block k + 16 * 8 / 2 (ha index differing by 8) sum to exactly 512.
All inputs are finite; a program needn't handle non-finite values.
Results may differ from the reference program's by a relative error of at most 0.00055.
The reference program's roundings to bfloat16 on the way (of `features`, `hidden`, `dlogits` and `dpreact`) count: a program that leaves them out, or rounds other values in their place, can miss the bound.
Values may be sent and summed in bfloat16 or wider, within the bound.
A program may use at most 192 MiB of HBM per device.

```python
import jax
import jax.numpy as jnp
from jax import lax

C = 128
HID = 256
NCLS = 18
Z = 64
HB = 32
WB = 128
RUN = 128
CAP = 512
H = 512
W = 1024
N_HA = 16
N_WA = 8


def draw_hw_plane(key, part):
    key = jax.random.fold_in(key, 11)
    draws = jnp.clip(jax.random.normal(key, (H, W, C), jnp.float32), -4.0, 4.0)
    return draws.astype(jnp.bfloat16)


def draw_run_index(key, part):
    key = jax.random.fold_in(key, 7)
    device_keys = jax.random.split(key, N_HA * N_WA)
    picked = jax.vmap(lambda one_key: jax.random.permutation(one_key, HB * WB // 2)[:CAP])(device_keys)
    return picked.astype(jnp.int32)


def draw_run_count(key, part):
    key = jax.random.fold_in(key, 5)
    lower_counts = jax.random.randint(key, (N_HA * N_WA // 2,), 1, CAP, dtype=jnp.int32)
    lower_counts = lower_counts.at[0].set(CAP - 1)
    return jnp.concatenate([lower_counts, CAP - lower_counts]).astype(jnp.int32)


def set_ends(result, stream_key, low, largest):
    shape = result.shape
    spot = [jax.random.randint(jax.random.fold_in(stream_key, axis), (), 0, shape[axis]) for axis in range(len(shape))]
    result = result.at[tuple(spot)].set(low)
    longest = shape.index(max(shape))
    spot[longest] = (spot[longest] + 1) % shape[longest]
    return result.at[tuple(spot)].set(largest)


def block_levels(key, extent, shards, low, high):
    level = 1.0
    for position, parts in shards:
        steps = jax.random.uniform(jax.random.fold_in(jax.random.fold_in(key, 6), position), (parts,), jnp.float32, low / len(shards), high / len(shards))
        level = level * jnp.repeat(jnp.exp(steps), extent[position] // parts).reshape((-1,) + (1,) * (len(extent) - 1 - position))
    return level


def normal_values(stream_key, shape, width, most, pieces=(), kind=jnp.bfloat16):
    array = jax.random.normal(stream_key, shape, jnp.float32) * width
    if len(pieces) > 0:
        array = block_levels(stream_key, shape, pieces, -0.22, 0.18) * array
    return jnp.clip(array, min=-most, max=most).astype(kind)


def setup_inputs(seed: int = 0) -> dict:
    seeds = jax.random.split(jax.random.key(seed), 11)
    hw_plane = draw_hw_plane(jax.random.fold_in(seeds[10], 71), 0)
    zh_plane = normal_values(seeds[1], (Z, H, C), 1.0, 5.0, ((1, 16),))
    wz_plane = normal_values(seeds[2], (W, Z, C), 1.0, 5.0, ((0, 8),))
    w_in = normal_values(seeds[3], (C, HID), C ** -0.5, 0.5)
    b_in = normal_values(seeds[4], (HID,), 0.5, 3.0, (), jnp.float32)
    w_out = normal_values(seeds[5], (HID, NCLS), (HID // 4) ** -0.5, 0.75)
    b_out = normal_values(seeds[6], (NCLS,), 0.5, 3.0, (), jnp.float32)
    run_index = draw_run_index(jax.random.fold_in(seeds[10], 71), 0)
    run_count = draw_run_count(jax.random.fold_in(seeds[10], 71), 0)
    labels = set_ends(jax.random.randint(seeds[9], (N_HA * N_WA, CAP, RUN), 0, NCLS), jax.random.fold_in(seeds[9], 1), 0, NCLS - 1).astype(jnp.int32)
    return dict(hw_plane=hw_plane, zh_plane=zh_plane, wz_plane=wz_plane, w_in=w_in, b_in=b_in, w_out=w_out, b_out=b_out, run_index=run_index, run_count=run_count, labels=labels)


grad_scale = 0.25


def silu_slope(preact):
    sigmoid_val = jax.nn.sigmoid(preact)
    return sigmoid_val * (1.0 + preact * (1.0 - sigmoid_val))


def contract_rows(left, right):
    return lax.dot_general(left, right, (((0,), (0,)), ((), ())), preferred_element_type=jnp.float32)


def contract_cols(left, right):
    return lax.dot_general(left, right, (((1,), (1,)), ((), ())), preferred_element_type=jnp.float32)


def sample_grads(features, labels_flat, validity, w_in, b_in, w_out, b_out):
    preact = jnp.dot(features, w_in, preferred_element_type=jnp.float32) + b_in
    hidden = jax.nn.silu(preact).astype(jnp.bfloat16)
    logits = jnp.dot(hidden, w_out, preferred_element_type=jnp.float32) + b_out
    row_top = jnp.max(logits, axis=1, keepdims=True)
    scores_exp = jnp.exp(logits - row_top)
    probability = scores_exp / jnp.sum(scores_exp, axis=1, keepdims=True)
    classes = jnp.arange(logits.shape[1], dtype=jnp.int32)
    onehot = (labels_flat[:, None] == classes[None, :]).astype(jnp.float32)
    dlogits = ((probability - onehot) * (grad_scale * validity[:, None])).astype(jnp.bfloat16)
    grad_w_out = contract_rows(hidden, dlogits)
    grad_b_out = jnp.sum(dlogits.astype(jnp.float32), axis=0)
    dhidden = contract_cols(dlogits, w_out)
    dpreact = (dhidden * silu_slope(preact)).astype(jnp.bfloat16)
    grad_w_in = contract_rows(features, dpreact)
    grad_b_in = jnp.sum(dpreact.astype(jnp.float32), axis=0)
    dfeatures = contract_cols(dpreact, w_in)
    return dfeatures, (grad_w_in, grad_b_in, grad_w_out, grad_b_out)


def run_features(hw_block, zh_rows, wz_block, run_ids):
    rows_blk, cols_blk, channels = hw_block.shape
    pair_cols = cols_blk // 2
    depth_z = wz_block.shape[1]
    run_row = run_ids // pair_cols
    run_pair = run_ids % pair_cols
    hw_part = hw_block.reshape(rows_blk * pair_cols, 2, channels)[run_ids].astype(jnp.float32)
    zh_part = zh_rows[run_row].astype(jnp.float32)
    wz_part = wz_block.reshape(pair_cols, 2, depth_z, channels)[run_pair].astype(jnp.float32)
    summed = hw_part[:, :, None, :] + zh_part[:, None, :, :] + wz_part
    return summed.astype(jnp.bfloat16)


def plane_grads(dfeatures, run_ids, rows_blk, cols_blk):
    slot_count, pair_count, depth_z, channels = dfeatures.shape
    pair_cols = cols_blk // 2
    run_row = run_ids // pair_cols
    run_pair = run_ids % pair_cols
    hw_local = jnp.zeros((rows_blk * pair_cols, 2, channels), jnp.float32)
    hw_local = hw_local.at[run_ids].add(jnp.sum(dfeatures, axis=2)).reshape(rows_blk, cols_blk, channels)
    zh_rows_grad = jnp.zeros((rows_blk, depth_z, channels), jnp.float32).at[run_row].add(jnp.sum(dfeatures, axis=1))
    zh_local = jnp.transpose(zh_rows_grad, (1, 0, 2))
    wz_local = jnp.zeros((pair_cols, 2, depth_z, channels), jnp.float32).at[run_pair].add(dfeatures)
    return hw_local, zh_local, wz_local.reshape(cols_blk, depth_z, channels)


def reference(hw_plane, zh_plane, wz_plane, w_in, b_in, w_out, b_out, run_index, run_count, labels):
    channels = hw_plane.shape[2]
    zh_all = jnp.transpose(zh_plane, (1, 0, 2))
    zero_init = (jnp.zeros(hw_plane.shape, jnp.float32), jnp.zeros(zh_plane.shape, jnp.float32),
                 jnp.zeros(wz_plane.shape, jnp.float32), jnp.zeros(w_in.shape, jnp.float32),
                 jnp.zeros(b_in.shape, jnp.float32), jnp.zeros(w_out.shape, jnp.float32),
                 jnp.zeros(b_out.shape, jnp.float32))
    slot_ids = jnp.arange(CAP, dtype=jnp.int32)

    def device_step(totals, device):
        row_start = ((device // N_WA) * HB).astype(jnp.int32)
        col_start = ((device % N_WA) * WB).astype(jnp.int32)
        zero_idx = jnp.zeros((), jnp.int32)
        hw_block = lax.dynamic_slice(hw_plane, (row_start, col_start, zero_idx), (HB, WB, channels))
        zh_rows = lax.dynamic_slice(zh_all, (row_start, zero_idx, zero_idx), (HB, Z, channels))
        wz_block = lax.dynamic_slice(wz_plane, (col_start, zero_idx, zero_idx), (WB, Z, channels))
        run_ids = run_index[device]
        features = run_features(hw_block, zh_rows, wz_block, run_ids)
        validity = jnp.repeat((slot_ids < run_count[device]).astype(jnp.float32), RUN)
        dfeat_flat, weight_grads = sample_grads(features.reshape(CAP * RUN, channels),
                                                labels[device].reshape(CAP * RUN), validity,
                                                w_in, b_in, w_out, b_out)
        hw_local, zh_local, wz_local = plane_grads(dfeat_flat.reshape(CAP, 2, Z, channels), run_ids, HB, WB)
        hw_total = lax.dynamic_update_slice(totals[0], hw_local, (row_start, col_start, zero_idx))
        zh_now = lax.dynamic_slice(totals[1], (zero_idx, row_start, zero_idx), (Z, HB, channels))
        zh_total = lax.dynamic_update_slice(totals[1], zh_now + zh_local, (zero_idx, row_start, zero_idx))
        wz_now = lax.dynamic_slice(totals[2], (col_start, zero_idx, zero_idx), (WB, Z, channels))
        wz_total = lax.dynamic_update_slice(totals[2], wz_now + wz_local, (col_start, zero_idx, zero_idx))
        return (hw_total, zh_total, wz_total, totals[3] + weight_grads[0], totals[4] + weight_grads[1],
                totals[5] + weight_grads[2], totals[6] + weight_grads[3]), None

    totals, ignored = lax.scan(device_step, zero_init, jnp.arange(N_HA * N_WA, dtype=jnp.int32))
    return (totals[0], totals[1], totals[2], totals[3], totals[4], totals[5], totals[6])
```

```python
import functools

import jax
import jax.numpy as jnp
from jax import lax
from jax.experimental import pallas as pl
from jax.experimental.pallas import tpu as pltpu
from jax.sharding import PartitionSpec as P

F32 = jnp.float32
BF16 = jnp.bfloat16
GRAD_SCALE = 0.25
GROUP = 16
CLS = 32


def dotg(left, right, dims):
    return lax.dot_general(left, right, ((dims[0], dims[1]), ((), ())), preferred_element_type=F32)


def decode_kernel(
    ids_ref, count_ref, hw_ref, zh_ref, wz_ref, labels_ref, win_ref, bin_ref, wout_ref, bout_ref,
    hw_out, zh_out, wz_out, gwi_ref, gwo_ref, gbo_ref,
    hw32,
):
    rows, depth, chans = zh_ref.shape
    pairs = wz_ref.shape[0]
    used = count_ref[0]
    hw32[...] = hw_ref[...].astype(F32)
    hw_out[...] = jnp.zeros_like(hw_out)
    zh_out[...] = jnp.zeros_like(zh_out)
    wz_out[...] = jnp.zeros_like(wz_out)
    gwi_ref[...] = jnp.zeros_like(gwi_ref)
    gwo_ref[...] = jnp.zeros_like(gwo_ref)
    gbo_ref[...] = jnp.zeros_like(gbo_ref)
    samples = GROUP * 2 * depth
    run = 2 * depth

    def body(step, carry):
        base = step * GROUP
        spots = []
        parts = []
        for g in range(GROUP):
            rid = ids_ref[base + g]
            row = rid // pairs
            pair = rid % pairs
            spots.append((rid, row, pair))
            zh = zh_ref[row].astype(F32)
            for p in range(2):
                hw = hw32[pl.ds(2 * rid + p, 1), :]
                wz = wz_ref[pair, p * depth:(p + 1) * depth, :].astype(F32)
                parts.append(((hw + zh) + wz).astype(BF16))
        feats = jnp.concatenate(parts, axis=0)
        u = jnp.dot(feats, win_ref[...] * 0.5, preferred_element_type=F32) + bin_ref[...]
        a = jnp.tanh(u) + 1.0
        h = u * a
        hid = h.astype(BF16)
        logits = dotg(wout_ref[...], hid, ((1,), (1,)))
        dparts = []
        for g in range(GROUP):
            lt = logits[:, g * run:(g + 1) * run] + bout_ref[...]
            top = jnp.max(lt, axis=0, keepdims=True)
            e = jnp.exp(lt - top)
            inv = 1.0 / jnp.sum(e, axis=0, keepdims=True)
            lab = labels_ref[pl.ds(base + g, 1), :]
            cls = lax.broadcasted_iota(jnp.int32, lt.shape, 0)
            hot = jnp.where(cls == lab, 1.0, 0.0)
            scale = jnp.where(base + g < used, GRAD_SCALE, 0.0)
            dparts.append(((e * inv - hot) * scale).astype(BF16))
        dlt = jnp.concatenate(dparts, axis=1)
        gwo_ref[...] += jnp.dot(dlt, hid, preferred_element_type=F32)
        tot = dparts[0].astype(F32)
        for g in range(1, GROUP):
            tot += dparts[g].astype(F32)
        gbo_ref[...] += tot
        dhh = dotg(dlt, wout_ref[...] * 0.5, ((0,), (0,)))
        q = (u + u + 1.0) - h
        dpre = (dhh * a * q).astype(BF16)
        lhs = jnp.concatenate([feats.T, jnp.ones((16, samples), BF16)], axis=0)
        gwi_ref[...] += jnp.dot(lhs, dpre, preferred_element_type=F32)
        df = dotg(dpre, win_ref[...], ((1,), (1,)))
        for g in range(GROUP):
            rid, row, pair = spots[g]
            d = df[g * run:(g + 1) * run]
            wz_out[pair] += d
            zh_out[row] += d[:depth] + d[depth:]
            for p in range(2):
                hw_out[pl.ds(2 * rid + p, 1), :] = jnp.sum(d[p * depth:(p + 1) * depth], axis=0, keepdims=True)
        return carry

    lax.fori_loop(0, pl.cdiv(used, GROUP), body, 0)


def decode_runs(ids, count, hw, zh, wz, labels, w_in, b_in, w_out, b_out):
    rows, depth, chans = zh.shape
    pairs = wz.shape[0]
    hid, ncls = w_out.shape
    hw_rows = hw.shape[0]
    wout = jnp.zeros((CLS, hid), BF16).at[:ncls].set(w_out.T)
    bout = jnp.full((CLS, 1), -1e30, F32).at[:ncls, 0].set(b_out)
    smem = pl.BlockSpec(memory_space=pltpu.SMEM)
    vmem = pl.BlockSpec(memory_space=pltpu.VMEM)
    return pl.pallas_call(
        decode_kernel,
        out_shape=(
            jax.ShapeDtypeStruct((hw_rows, chans), F32),
            jax.ShapeDtypeStruct((rows, depth, chans), F32),
            jax.ShapeDtypeStruct((pairs, 2 * depth, chans), F32),
            jax.ShapeDtypeStruct((chans + 16, hid), F32),
            jax.ShapeDtypeStruct((CLS, hid), F32),
            jax.ShapeDtypeStruct((CLS, 2 * depth), F32),
        ),
        in_specs=[smem, smem] + [vmem] * 8,
        out_specs=[vmem] * 6,
        scratch_shapes=[pltpu.VMEM((hw_rows, chans), F32)],
        compiler_params=pltpu.CompilerParams(vmem_limit_bytes=48 * 1024 * 1024),
    )(ids, count, hw, zh, wz, labels, w_in, (0.5 * b_in).reshape(1, hid), wout, bout)


def local(hw_plane, zh_plane, wz_plane, w_in, b_in, w_out, b_out, run_index, run_count, labels):
    rows, cols, chans = hw_plane.shape
    depth = zh_plane.shape[0]
    ncls = w_out.shape[1]
    zh_rows = jnp.transpose(zh_plane, (1, 0, 2))
    hw, zh, wz, gwi, gwo, gbo = decode_runs(
        run_index[0], run_count, hw_plane.reshape(rows * cols, chans), zh_rows,
        wz_plane.reshape(cols // 2, 2 * depth, chans), labels[0], w_in, b_in, w_out, b_out,
    )
    zh_grad = lax.psum_scatter(jnp.transpose(zh, (1, 0, 2)), "wa", scatter_dimension=0, tiled=True)
    wz_grad = lax.psum_scatter(wz.reshape(cols, depth, chans), "ha", scatter_dimension=1, tiled=True)
    gwi, gwo, gbo = lax.psum((gwi, gwo, jnp.sum(gbo, axis=1)), ("ha", "wa"))
    return (hw.reshape(rows, cols, chans), zh_grad, wz_grad, gwi[:chans], gwi[chans], gwo[:ncls].T, gbo[:ncls])


def solution(mesh):
    placed = (
        P("ha", "wa", None),
        P(None, "ha", None),
        P("wa", None, None),
        P(),
        P(),
        P(),
        P(),
        P(("ha", "wa"), None),
        P(("ha", "wa")),
        P(("ha", "wa"), None, None),
    )
    return jax.shard_map(
        local,
        mesh=mesh,
        in_specs=placed,
        out_specs=(P("ha", "wa", None), P("wa", "ha", None), P("wa", "ha", None), P(), P(), P(), P()),
        check_vma=False,
    )
```

```python
import functools

import jax
import jax.numpy as jnp
from jax import lax
from jax.experimental import pallas as pl
from jax.experimental.pallas import tpu as pltpu
from jax.sharding import PartitionSpec as P

F32 = jnp.float32
BF16 = jnp.bfloat16
GRAD_SCALE = 0.25
GROUP = 16
CLS = 32
CHUNKS = 4
MESH = pl.DeviceIdType.MESH


def dotg(left, right, dims):
    return lax.dot_general(left, right, ((dims[0], dims[1]), ((), ())), preferred_element_type=F32)


def decode_kernel(
    ids_ref, count_ref, hw_ref, zh_ref, wz_ref, labels_ref, win_ref, bin_ref, wout_ref, bout_ref,
    hw_out, zh_out, wz_out, wt_out,
    hw32, gwi_ref, gwo_ref, gbo_ref,
):
    rows, depth, chans = zh_ref.shape
    pairs = wz_ref.shape[0]
    used = count_ref[0]
    hw32[...] = hw_ref[...].astype(F32)
    hw_out[...] = jnp.zeros_like(hw_out)
    zh_out[...] = jnp.zeros_like(zh_out)
    wz_out[...] = jnp.zeros_like(wz_out)
    gwi_ref[...] = jnp.zeros_like(gwi_ref)
    gwo_ref[...] = jnp.zeros_like(gwo_ref)
    gbo_ref[...] = jnp.zeros_like(gbo_ref)
    samples = GROUP * 2 * depth
    run = 2 * depth

    def body(step, carry):
        base = step * GROUP
        spots = []
        parts = []
        for g in range(GROUP):
            rid = ids_ref[base + g]
            row = rid // pairs
            pair = rid % pairs
            spots.append((rid, row, pair))
            zh = zh_ref[row].astype(F32)
            for p in range(2):
                hw = hw32[pl.ds(2 * rid + p, 1), :]
                wz = wz_ref[pair, p * depth:(p + 1) * depth, :].astype(F32)
                parts.append(((hw + zh) + wz).astype(BF16))
        feats = jnp.concatenate(parts, axis=0)
        u = jnp.dot(feats, win_ref[...] * 0.5, preferred_element_type=F32) + bin_ref[...]
        a = jnp.tanh(u) + 1.0
        h = u * a
        hid = h.astype(BF16)
        logits = dotg(wout_ref[...], hid, ((1,), (1,)))
        dparts = []
        for g in range(GROUP):
            lt = logits[:, g * run:(g + 1) * run] + bout_ref[...]
            top = jnp.max(lt, axis=0, keepdims=True)
            e = jnp.exp(lt - top)
            inv = 1.0 / jnp.sum(e, axis=0, keepdims=True)
            lab = labels_ref[pl.ds(base + g, 1), :]
            cls = lax.broadcasted_iota(jnp.int32, lt.shape, 0)
            hot = jnp.where(cls == lab, 1.0, 0.0)
            scale = jnp.where(base + g < used, GRAD_SCALE, 0.0)
            dparts.append(((e * inv - hot) * scale).astype(BF16))
        dlt = jnp.concatenate(dparts, axis=1)
        gwo_ref[...] += jnp.dot(dlt, hid, preferred_element_type=F32)
        tot = dparts[0].astype(F32)
        for g in range(1, GROUP):
            tot += dparts[g].astype(F32)
        gbo_ref[...] += tot
        dhh = dotg(dlt, wout_ref[...] * 0.5, ((0,), (0,)))
        q = (u + u + 1.0) - h
        dpre = (dhh * a * q).astype(BF16)
        lhs = jnp.concatenate([feats.T, jnp.ones((16, samples), BF16)], axis=0)
        gwi_ref[...] += jnp.dot(lhs, dpre, preferred_element_type=F32)
        df = dotg(dpre, win_ref[...], ((1,), (1,)))
        for g in range(GROUP):
            rid, row, pair = spots[g]
            d = df[g * run:(g + 1) * run]
            zh_out[:, row] += (d[:depth] + d[depth:]).reshape(depth // 8, 8, chans)
            for p in range(2):
                wz_out[:, 2 * pair + p] += d[p * depth:(p + 1) * depth].reshape(depth // 8, 8, chans)
                hw_out[pl.ds(2 * rid + p, 1), :] = jnp.sum(d[p * depth:(p + 1) * depth], axis=0, keepdims=True)
        return carry

    lax.fori_loop(0, pl.cdiv(used, GROUP), body, 0)
    top = chans + 16
    wt_out[0:top] = gwi_ref[:, :128]
    wt_out[top:2 * top] = gwi_ref[:, 128:]
    wt_out[2 * top:2 * top + CLS] = gwo_ref[:, :128]
    wt_out[2 * top + CLS:2 * top + 2 * CLS] = gwo_ref[:, 128:]
    wt_out[2 * top + 2 * CLS:] = gbo_ref[...]


def decode_runs(ids, count, hw, zh, wz, labels, w_in, b_in, w_out, b_out):
    rows, depth, chans = zh.shape
    pairs = wz.shape[0]
    hid, ncls = w_out.shape
    hw_rows = hw.shape[0]
    wout = jnp.zeros((CLS, hid), BF16).at[:ncls].set(w_out.T)
    bout = jnp.full((CLS, 1), -1e30, F32).at[:ncls, 0].set(b_out)
    smem = pl.BlockSpec(memory_space=pltpu.SMEM)
    vmem = pl.BlockSpec(memory_space=pltpu.VMEM)
    return pl.pallas_call(
        decode_kernel,
        out_shape=(
            jax.ShapeDtypeStruct((hw_rows, chans), F32),
            jax.ShapeDtypeStruct((depth // 8, rows, 8, chans), F32),
            jax.ShapeDtypeStruct((depth // 8, 2 * pairs, 8, chans), F32),
            jax.ShapeDtypeStruct((2 * (chans + 16) + 3 * CLS, chans), F32),
        ),
        in_specs=[smem, smem] + [vmem] * 8,
        out_specs=[vmem] * 4,
        scratch_shapes=[
            pltpu.VMEM((hw_rows, chans), F32),
            pltpu.VMEM((chans + 16, hid), F32),
            pltpu.VMEM((CLS, hid), F32),
            pltpu.VMEM((CLS, 2 * depth), F32),
        ],
        compiler_params=pltpu.CompilerParams(vmem_limit_bytes=48 * 1024 * 1024),
    )(ids, count, hw, zh, wz, labels, w_in, (0.5 * b_in).reshape(1, hid), wout, bout)


def ring_copies(src, chain_p, chain_m, final, sems, axis, me, size, span, at):
    plus, minus, far = lax.rem(me + 1, size), lax.rem(me + 3, size), lax.rem(me + 2, size)
    half = span // 2
    lo, hi = pl.ds(at, half), pl.ds(at + half, half)

    def copy(i, source, dest, to):
        return pltpu.make_async_remote_copy(
            src_ref=source, dst_ref=dest, send_sem=sems.at[0, i], recv_sem=sems.at[1, i],
            device_id=axis(to), device_id_type=MESH)

    first = [
        copy(0, src.at[:, far, lo], chain_p, plus),
        copy(1, src.at[:, far, hi], chain_m, minus),
        copy(2, src.at[:, minus, lo], final.at[1, :, 0:half], minus),
        copy(3, src.at[:, plus, hi], final.at[1, :, half:span], plus),
    ]
    second = [
        copy(4, chain_p, final.at[0, :, 0:half], plus),
        copy(5, chain_m, final.at[0, :, half:span], minus),
    ]

    def relay():
        first[0].wait_recv()
        chain_p[...] += src[:, plus, lo]
        second[0].start()
        first[1].wait_recv()
        chain_m[...] += src[:, minus, hi]
        second[1].start()

    def finish():
        for c in (first[2], first[3], second[0], second[1]):
            c.wait_recv()
        return final[0] + final[1] + src[:, me, pl.ds(at, span)]

    def done():
        for c in first + second:
            c.wait_send()

    return first, relay, finish, done


def reduce_kernel(
    wz_ref, zh_ref, wt_ref, wz_out, zh_out, wt_out,
    core_in, xchain_p, xchain_m, xfinal, xsum, yin, swap,
    zchain_p, zchain_m, zfinal, zsum, zin, zres, wt_in, wt_mid,
    core_sem, x_sem, y_sem, swap_sem, z_sem, yl_sem, wa_sem, wb_sem, wc_sem,
):
    ha, wa = lax.axis_index("ha"), lax.axis_index("wa")
    yh, x, c = ha // 8, lax.rem(ha // 2, 4), lax.rem(ha, 2)
    yl, z = wa // 4, lax.rem(wa, 4)
    half_w = wz_ref.shape[2] // 2
    span = half_w // CHUNKS
    n_ha, n_wa = wt_ref.shape[0], 8

    def on_x(to):
        return (yh * 8 + to * 2 + c, wa)

    def on_z(to):
        return (ha, yl * 4 + to)

    sibling = (ha + 1 - 2 * c, wa)
    across = (lax.rem(ha + 8, 16), wa)
    beside = (ha, lax.rem(wa + 4, 8))

    barrier = pltpu.get_barrier_semaphore()

    def greet_ha(i, carry):
        pl.semaphore_signal(barrier, inc=1, device_id=(lax.rem(ha + i, n_ha), wa), device_id_type=MESH)
        return carry

    def greet_wa(i, carry):
        pl.semaphore_signal(barrier, inc=1, device_id=(ha, lax.rem(wa + i, n_wa)), device_id_type=MESH)
        return carry

    lax.fori_loop(1, n_ha, greet_ha, 0)
    lax.fori_loop(1, n_wa, greet_wa, 0)
    pl.semaphore_wait(barrier, n_ha + n_wa - 2)

    def send(source, dest, sems, to):
        return pltpu.make_async_remote_copy(
            src_ref=source, dst_ref=dest, send_sem=sems.at[0], recv_sem=sems.at[1],
            device_id=to, device_id_type=MESH)

    core = [
        send(wz_ref.at[:, :, pl.ds((1 - c) * half_w + k * span, span)], core_in.at[:, :, pl.ds(k * span, span)],
             core_sem.at[k], sibling)
        for k in range(CHUNKS)
    ]
    for k in range(CHUNKS):
        core[k].start()
    zring = ring_copies(zh_ref, zchain_p, zchain_m, zfinal, z_sem, on_z, z, 4, zh_ref.shape[2], 0)
    for cp in zring[0]:
        cp.start()

    def wt_first(i):
        to = lax.rem(ha + i, n_ha)
        return pltpu.make_async_remote_copy(
            src_ref=wt_ref.at[to], dst_ref=wt_in.at[ha], send_sem=wa_sem.at[0, to], recv_sem=wa_sem.at[1, ha],
            device_id=(to, wa), device_id_type=MESH)

    def wt_second(i):
        to = lax.rem(wa + i, n_wa)
        return pltpu.make_async_remote_copy(
            src_ref=wt_mid.at[wa], dst_ref=wt_mid.at[wa], send_sem=wb_sem.at[0, to], recv_sem=wb_sem.at[1, wa],
            device_id=(ha, to), device_id_type=MESH)

    def wt_third(i):
        to = lax.rem(ha + i, n_ha)
        return pltpu.make_async_remote_copy(
            src_ref=wt_out.at[ha], dst_ref=wt_out.at[ha], send_sem=wc_sem.at[0, to], recv_sem=wc_sem.at[1, ha],
            device_id=(to, wa), device_id_type=MESH)

    def start(make, n):
        def go(i, carry):
            make(i).start()
            return carry
        lax.fori_loop(1, n, go, 0)

    def wait_send(make, n):
        def go(i, carry):
            make(i).wait_send()
            return carry
        lax.fori_loop(1, n, go, 0)

    def wait_slot(buf, sems, me, n, own):
        def go(i, carry):
            frm = lax.rem(me + i, n)
            pltpu.make_async_remote_copy(
                src_ref=buf.at[frm], dst_ref=buf.at[frm], send_sem=sems.at[0, frm], recv_sem=sems.at[1, frm],
                device_id=own, device_id_type=MESH).wait_recv()
            return carry
        lax.fori_loop(1, n, go, 0)

    start(wt_first, n_ha)
    rings = []
    for k in range(CHUNKS):
        rows = pl.ds(k * span, span)
        core[k].wait_recv()
        core_in[:, :, rows] += wz_ref[:, :, pl.ds(c * half_w + k * span, span)]
        ring = ring_copies(core_in, xchain_p.at[k], xchain_m.at[k], xfinal.at[k], x_sem.at[k], on_x, x, 4, span, k * span)
        for cp in ring[0]:
            cp.start()
        rings.append(ring)
    zring[1]()
    wait_slot(wt_in, wa_sem, ha, n_ha, sibling)
    wt_in[ha] = wt_ref[ha]
    tot = wt_in[0]
    for i in range(1, n_ha):
        tot += wt_in[i]
    wt_mid[wa] = tot
    start(wt_second, n_wa)
    for k in range(CHUNKS):
        rings[k][1]()
    zsum[...] = zring[2]()
    to_beside = send(zsum.at[1 - yl], zin, yl_sem, beside)
    to_beside.start()
    ys = []
    for k in range(CHUNKS):
        rows = pl.ds(k * span, span)
        xsum[:, rows] = rings[k][2]()
        ys.append(send(xsum.at[1 - yh, rows], yin.at[rows], y_sem.at[k], across))
        ys[k].start()
    wait_slot(wt_mid, wb_sem, wa, n_wa, beside)
    tot = wt_mid[0]
    for i in range(1, n_wa):
        tot += wt_mid[i]
    wt_out[ha] = tot
    start(wt_third, n_ha)
    to_beside.wait_recv()
    zres[...] = zsum[yl] + zin[...]
    for i in range(8):
        zh_out[i] = zres[:, i, :]
    swaps = []
    for k in range(CHUNKS):
        rows = pl.ds(k * span, span)
        ys[k].wait_recv()
        r = xsum[yh, rows] + yin[rows]
        mine = pl.ds(c * half_w + k * span, span)
        wz_out[mine] = jnp.where(c == 0, r[:, :4], r[:, 4:])
        swap[rows] = jnp.where(c == 0, r[:, 4:], r[:, :4])
        swaps.append(send(swap.at[rows], wz_out.at[mine], swap_sem.at[k], sibling))
        swaps[k].start()
    for k in range(CHUNKS):
        swaps[k].wait_recv()
    wait_slot(wt_out, wc_sem, ha, n_ha, sibling)
    for k in range(CHUNKS):
        core[k].wait_send()
        rings[k][3]()
        ys[k].wait_send()
        swaps[k].wait_send()
    zring[3]()
    to_beside.wait_send()
    wait_send(wt_first, n_ha)
    wait_send(wt_second, n_wa)
    wait_send(wt_third, n_ha)


def reduce_all(wz, zh, wt):
    width, chans = wz.shape[2], wz.shape[4]
    rows = zh.shape[2]
    half_w = width // 2
    span = half_w // CHUNKS
    vmem = pl.BlockSpec(memory_space=pltpu.VMEM)
    buf = lambda *s: pltpu.VMEM(s, F32)
    dma = lambda *s: pltpu.SemaphoreType.DMA(s)
    return pl.pallas_call(
        reduce_kernel,
        out_shape=(
            jax.ShapeDtypeStruct((width, 4, chans), F32),
            jax.ShapeDtypeStruct((8, rows, chans), F32),
            jax.ShapeDtypeStruct(wt.shape, F32),
        ),
        in_specs=[vmem] * 3,
        out_specs=[vmem] * 3,
        scratch_shapes=[
            buf(2, 4, half_w, 8, chans),
            buf(CHUNKS, 2, span // 2, 8, chans),
            buf(CHUNKS, 2, span // 2, 8, chans),
            buf(CHUNKS, 2, 2, span, 8, chans),
            buf(2, half_w, 8, chans),
            buf(half_w, 8, chans),
            buf(half_w, 4, chans),
            buf(2, rows // 2, 8, chans),
            buf(2, rows // 2, 8, chans),
            buf(2, 2, rows, 8, chans),
            buf(2, rows, 8, chans),
            buf(rows, 8, chans),
            buf(rows, 8, chans),
            buf(*wt.shape),
            buf(8, *wt.shape[1:]),
            dma(CHUNKS, 2), dma(CHUNKS, 2, 6), dma(CHUNKS, 2), dma(CHUNKS, 2), dma(2, 6), dma(2),
            dma(2, 16), dma(2, 8), dma(2, 16),
        ],
        compiler_params=pltpu.CompilerParams(
            collective_id=0, has_side_effects=True, vmem_limit_bytes=48 * 1024 * 1024),
    )(wz, zh, wt)


def local(hw_plane, zh_plane, wz_plane, w_in, b_in, w_out, b_out, run_index, run_count, labels):
    rows, cols, chans = hw_plane.shape
    depth = zh_plane.shape[0]
    ncls = w_out.shape[1]
    zh_rows = jnp.transpose(zh_plane, (1, 0, 2))
    hw, zh, wz, wt = decode_runs(
        run_index[0], run_count, hw_plane.reshape(rows * cols, chans), zh_rows,
        wz_plane.reshape(cols // 2, 2 * depth, chans), labels[0], w_in, b_in, w_out, b_out,
    )
    wz_grad, zh_grad, wt = reduce_all(
        wz.reshape(2, 4, cols, 8, chans), zh.reshape(2, 4, rows, 8, chans), wt.reshape(16, -1, chans))
    wt = wt.reshape(-1, chans)
    top = chans + 16
    gwi = jnp.concatenate([wt[:chans], wt[top:top + chans]], axis=1)
    gbi = jnp.concatenate([wt[chans], wt[top + chans]])
    gwo = jnp.concatenate([wt[2 * top:2 * top + ncls], wt[2 * top + CLS:2 * top + CLS + ncls]], axis=1).T
    gbo = jnp.sum(wt[2 * top + 2 * CLS:2 * top + 2 * CLS + ncls], axis=1)
    return (hw.reshape(rows, cols, chans), zh_grad, wz_grad, gwi, gbi, gwo, gbo)


def solution(mesh):
    placed = (
        P("ha", "wa", None),
        P(None, "ha", None),
        P("wa", None, None),
        P(),
        P(),
        P(),
        P(),
        P(("ha", "wa"), None),
        P(("ha", "wa")),
        P(("ha", "wa"), None, None),
    )
    return jax.shard_map(
        local,
        mesh=mesh,
        in_specs=placed,
        out_specs=(P("ha", "wa", None), P("wa", "ha", None), P("wa", "ha", None), P(), P(), P(), P()),
        check_vma=False,
    )
```

```python
import functools

import jax
import jax.numpy as jnp
from jax import lax
from jax.experimental import pallas as pl
from jax.experimental.pallas import tpu as pltpu
from jax.sharding import PartitionSpec as P

F32 = jnp.float32
BF16 = jnp.bfloat16
GRAD_SCALE = 0.25
GROUP = 16
CLS = 32
CHUNKS = 4
MESH = pl.DeviceIdType.MESH


def dotg(left, right, dims):
    return lax.dot_general(left, right, ((dims[0], dims[1]), ((), ())), preferred_element_type=F32)


def exchange_kernel(
    ids_ref, idrow_ref, hw_ref, zh_ref, labels_ref,
    ids_out, hw_out, zh_out, lab_out,
    hw32, rows32, rows16, lab16, sem, z_sem,
):
    ha, wa = lax.axis_index("ha"), lax.axis_index("wa")
    z, base = lax.rem(wa, 4), wa - lax.rem(wa, 4)
    cap = labels_ref.shape[0]
    half = cap // 2
    own_rows = zh_ref.shape[0]
    part = own_rows // 4
    across = (lax.rem(ha + 8, 16), wa)
    corner = (lax.rem(ha + 8, 16), lax.rem(wa + 4, 8))
    up, down, far = base + lax.rem(z + 1, 4), base + lax.rem(z + 3, 4), lax.rem(z + 2, 4)
    barrier = pltpu.get_barrier_semaphore()
    for to in (across, corner, (ha, up), (ha, down)):
        pl.semaphore_signal(barrier, inc=1, device_id=to, device_id_type=MESH)
    pl.semaphore_wait(barrier, 4)

    def send(source, dest, sems, to):
        return pltpu.make_async_remote_copy(
            src_ref=source, dst_ref=dest, send_sem=sems.at[0], recv_sem=sems.at[1],
            device_id=to, device_id_type=MESH)

    got = own_rows + z * part
    fetch = send(zh_ref.at[pl.ds(z * part, part)], zh_out.at[pl.ds(got, part)], z_sem.at[0], corner)
    fetch.start()
    keep = pltpu.make_async_copy(zh_ref, zh_out.at[pl.ds(0, own_rows)], sem.at[3, 0])
    keep.start()
    lab16[...] = labels_ref[half:].astype(F32).astype(BF16)
    to_lab = send(lab16, lab_out, sem.at[0], across)
    to_lab.start()
    to_ids = send(idrow_ref, ids_out, sem.at[1], across)
    to_ids.start()
    hw32[...] = hw_ref[...].astype(F32)

    def pick(i, carry):
        for k in range(8):
            s = i * 8 + k
            at = 2 * ids_ref[0, half + s]
            for p in range(2):
                rows32[pl.ds(2 * s + p, 1), :] = hw32[pl.ds(at + p, 1), :]
        return carry

    lax.fori_loop(0, half // 8, pick, 0)
    rows16[...] = rows32[...].astype(BF16)
    to_hw = send(rows16, hw_out, sem.at[2], across)
    to_hw.start()
    fetch.wait_recv()
    mine = zh_out.at[pl.ds(got, part)]
    to_up = send(mine, mine, z_sem.at[1], (ha, up))
    to_down = send(mine, mine, z_sem.at[2], (ha, down))
    to_up.start()
    to_down.start()
    from_down = own_rows + lax.rem(z + 3, 4) * part
    from_up = own_rows + lax.rem(z + 1, 4) * part
    to_up.wait_recv()
    piece = zh_out.at[pl.ds(from_down, part // 2)]
    on_up = send(piece, piece, z_sem.at[3], (ha, up))
    on_up.start()
    to_down.wait_recv()
    piece = zh_out.at[pl.ds(from_up + part // 2, part // 2)]
    on_down = send(piece, piece, z_sem.at[4], (ha, down))
    on_down.start()
    keep.wait()
    for cp in (to_lab, to_ids, to_hw, on_up, on_down):
        cp.wait()
    for cp in (fetch, to_up, to_down):
        cp.wait_send()


def exchange(ids, hw, zh, labels):
    vmem = pl.BlockSpec(memory_space=pltpu.VMEM)
    half = labels.shape[0] // 2
    dma = lambda *s: pltpu.SemaphoreType.DMA(s)
    return pl.pallas_call(
        exchange_kernel,
        out_shape=(
            jax.ShapeDtypeStruct(ids.shape, jnp.int32),
            jax.ShapeDtypeStruct((2 * half, hw.shape[1]), BF16),
            jax.ShapeDtypeStruct((2 * zh.shape[0],) + zh.shape[1:], BF16),
            jax.ShapeDtypeStruct((half, labels.shape[1]), BF16),
        ),
        in_specs=[pl.BlockSpec(memory_space=pltpu.SMEM)] + [vmem] * 4,
        out_specs=[vmem] * 4,
        scratch_shapes=[
            pltpu.VMEM(hw.shape, F32), pltpu.VMEM((2 * half, hw.shape[1]), F32),
            pltpu.VMEM((2 * half, hw.shape[1]), BF16), pltpu.VMEM((half, labels.shape[1]), BF16),
            dma(4, 2), dma(5, 2),
        ],
        compiler_params=pltpu.CompilerParams(
            collective_id=1, has_side_effects=True, vmem_limit_bytes=32 * 1024 * 1024),
    )(ids, ids, hw, zh, labels)


def decode_kernel(
    ids_ref, idx_ref, count_ref, hw_ref, hwx_ref, zh_ref, wz_ref, labels_ref, labx_ref, win_ref, bin_ref, wout_ref, bout_ref,
    hw_out, zh_out, wz_out, wt_out,
    hw32, labs, gwi_ref, gwo_ref, gbo_ref,
):
    rows, depth, chans = zh_ref.shape
    pairs = wz_ref.shape[0]
    half = labx_ref.shape[0]
    own_hw = hw_ref.shape[0]
    own_n = jnp.minimum(count_ref[0], half)
    hw32[:own_hw] = hw_ref[...].astype(F32)
    hw32[own_hw:] = hwx_ref[...].astype(F32)
    labs[:half] = labels_ref[:half]
    labs[half:] = labx_ref[...].astype(F32).astype(jnp.int32)
    hw_out[...] = jnp.zeros_like(hw_out)
    zh_out[...] = jnp.zeros_like(zh_out)
    wz_out[...] = jnp.zeros_like(wz_out)
    gwi_ref[...] = jnp.zeros_like(gwi_ref)
    gwo_ref[...] = jnp.zeros_like(gwo_ref)
    gbo_ref[...] = jnp.zeros_like(gbo_ref)
    samples = GROUP * 2 * depth
    run = 2 * depth

    def body(step, carry):
        base = step * GROUP
        spots = []
        parts = []
        for g in range(GROUP):
            i = base + g
            own = i < own_n
            j = jnp.maximum(i - own_n, 0)
            rid = jnp.where(own, ids_ref[0, i], idx_ref[0, half + j])
            row = rid // pairs + jnp.where(own, 0, rows // 2)
            pair = rid % pairs
            hw_at = jnp.where(own, 2 * rid, own_hw + 2 * j)
            slot = jnp.where(own, i, half + j)
            spots.append((slot, row, pair))
            zh = zh_ref[row].astype(F32)
            for p in range(2):
                hw = hw32[pl.ds(hw_at + p, 1), :]
                wz = wz_ref[pair, p * depth:(p + 1) * depth, :].astype(F32)
                parts.append(((hw + zh) + wz).astype(BF16))
        feats = jnp.concatenate(parts, axis=0)
        u = jnp.dot(feats, win_ref[...] * 0.5, preferred_element_type=F32) + bin_ref[...] * 0.5
        a = jnp.tanh(u) + 1.0
        h = u * a
        hid = h.astype(BF16)
        logits = dotg(wout_ref[...], hid, ((1,), (1,)))
        dparts = []
        for g in range(GROUP):
            lt = logits[:, g * run:(g + 1) * run] + bout_ref[...]
            top = jnp.max(lt, axis=0, keepdims=True)
            e = jnp.exp(lt - top)
            inv = GRAD_SCALE / jnp.sum(e, axis=0, keepdims=True)
            lab = labs[pl.ds(spots[g][0], 1), :]
            cls = lax.broadcasted_iota(jnp.int32, lt.shape, 0)
            hot = jnp.where(cls == lab, GRAD_SCALE, 0.0)
            dparts.append((e * inv - hot).astype(BF16))
        dlt = jnp.concatenate(dparts, axis=1)
        gwo_ref[...] += jnp.dot(dlt, hid, preferred_element_type=F32)
        tot = dparts[0].astype(F32)
        for g in range(1, GROUP):
            tot += dparts[g].astype(F32)
        gbo_ref[...] += tot
        dhh = dotg(dlt, wout_ref[...] * 0.5, ((0,), (0,)))
        q = (u + u + 1.0) - h
        dpre = (dhh * a * q).astype(BF16)
        lhs = jnp.concatenate([feats.T, jnp.ones((16, samples), BF16)], axis=0)
        gwi_ref[...] += jnp.dot(lhs, dpre, preferred_element_type=F32)
        df = dotg(dpre, win_ref[...], ((1,), (1,)))
        for g in range(GROUP):
            slot, row, pair = spots[g]
            d = df[g * run:(g + 1) * run]
            zh_out[:, row] += (d[:depth] + d[depth:]).reshape(depth // 8, 8, chans)
            for p in range(2):
                wz_out[:, 2 * pair + p] += d[p * depth:(p + 1) * depth].reshape(depth // 8, 8, chans)
                hw_out[pl.ds(2 * slot + p, 1), :] = jnp.sum(d[p * depth:(p + 1) * depth], axis=0, keepdims=True)
        return carry

    lax.fori_loop(0, half // GROUP, body, 0)
    top = chans + 16
    wt_out[0:top] = gwi_ref[:, :128]
    wt_out[top:2 * top] = gwi_ref[:, 128:]
    wt_out[2 * top:2 * top + CLS] = gwo_ref[:, :128]
    wt_out[2 * top + CLS:2 * top + 2 * CLS] = gwo_ref[:, 128:]
    wt_out[2 * top + 2 * CLS:] = gbo_ref[...]


def decode_runs(ids, idx, count, hw, hwx, zh, wz, labels, labx, w_in, b_in, w_out, b_out):
    rows, depth, chans = zh.shape
    pairs = wz.shape[0]
    hid, ncls = w_out.shape
    wout = jnp.pad(w_out.T, ((0, CLS - ncls), (0, 0)))
    bout = jnp.pad(b_out, (0, CLS - ncls), constant_values=-1e30).reshape(CLS, 1)
    smem = pl.BlockSpec(memory_space=pltpu.SMEM)
    vmem = pl.BlockSpec(memory_space=pltpu.VMEM)
    return pl.pallas_call(
        decode_kernel,
        out_shape=(
            jax.ShapeDtypeStruct((2 * labels.shape[0], chans), F32),
            jax.ShapeDtypeStruct((depth // 8, rows, 8, chans), F32),
            jax.ShapeDtypeStruct((depth // 8, 2 * pairs, 8, chans), F32),
            jax.ShapeDtypeStruct((2 * (chans + 16) + 3 * CLS, chans), F32),
        ),
        in_specs=[smem] * 3 + [vmem] * 10,
        out_specs=[vmem] * 4,
        scratch_shapes=[
            pltpu.VMEM((hw.shape[0] + hwx.shape[0], chans), F32),
            pltpu.VMEM(labels.shape, jnp.int32),
            pltpu.VMEM((chans + 16, hid), F32),
            pltpu.VMEM((CLS, hid), F32),
            pltpu.VMEM((CLS, 2 * depth), F32),
        ],
        compiler_params=pltpu.CompilerParams(vmem_limit_bytes=48 * 1024 * 1024),
    )(ids, idx, count, hw, hwx, zh, wz, labels, labx, w_in, b_in.reshape(1, hid), wout, bout)


def finish_kernel(
    ids_ref, count_ref, own_ref, back_ref, wz_ref, zh_ref, wt_ref,
    hw_out, wz_out, zh_out, gwi_out, gbi_out, gwo_out, gbo_out,
):
    cap = ids_ref.shape[1]
    half = cap // 2
    used = count_ref[0]
    chans = hw_out.shape[1]
    ncls = gwo_out.shape[1]
    hw_out[...] = jnp.zeros_like(hw_out)

    def put(source, start):
        def go(s, carry):
            for p in range(2):
                hw_out[pl.ds(2 * ids_ref[0, start + s] + p, 1), :] = source[pl.ds(2 * s + p, 1), :]
            return carry
        return go

    lax.fori_loop(0, jnp.minimum(used, half), put(own_ref, 0), 0)
    lax.fori_loop(0, jnp.maximum(used - half, 0), put(back_ref, half), 0)
    wz_out[...] = wz_ref[...]
    for i in range(8):
        zh_out[i] = zh_ref[:, i, :]
    top = chans + 16
    gwi_out[:, :128] = wt_ref[:chans]
    gwi_out[:, 128:] = wt_ref[top:top + chans]
    gbi_out[:, :128] = wt_ref[chans:chans + 1]
    gbi_out[:, 128:] = wt_ref[top + chans:top + chans + 1]
    at = 2 * top
    gwo_out[:128] = wt_ref[at:at + CLS].T[:, :ncls]
    gwo_out[128:] = wt_ref[at + CLS:at + 2 * CLS].T[:, :ncls]
    gbo_out[...] = jnp.sum(wt_ref[at + 2 * CLS:at + 3 * CLS].T, axis=0, keepdims=True)[:, :ncls]


def finish(ids, count, own, back, wz, zh, wt, hw_rows, hid, ncls):
    smem = pl.BlockSpec(memory_space=pltpu.SMEM)
    vmem = pl.BlockSpec(memory_space=pltpu.VMEM)
    chans = own.shape[1]
    return pl.pallas_call(
        finish_kernel,
        out_shape=(
            jax.ShapeDtypeStruct((hw_rows, chans), F32),
            jax.ShapeDtypeStruct(wz.shape, F32),
            jax.ShapeDtypeStruct((8, zh.shape[0], chans), F32),
            jax.ShapeDtypeStruct((chans, hid), F32),
            jax.ShapeDtypeStruct((1, hid), F32),
            jax.ShapeDtypeStruct((hid, ncls), F32),
            jax.ShapeDtypeStruct((1, ncls), F32),
        ),
        in_specs=[smem] * 2 + [vmem] * 5,
        out_specs=[vmem] * 7,
        compiler_params=pltpu.CompilerParams(vmem_limit_bytes=32 * 1024 * 1024),
    )(ids, count, own, back, wz, zh, wt)


def ring_copies(src, chain_p, chain_m, final, sems, axis, me, size, span, at):
    plus, minus, far = lax.rem(me + 1, size), lax.rem(me + 3, size), lax.rem(me + 2, size)
    half = span // 2
    lo, hi = pl.ds(at, half), pl.ds(at + half, half)

    def copy(i, source, dest, to):
        return pltpu.make_async_remote_copy(
            src_ref=source, dst_ref=dest, send_sem=sems.at[0, i], recv_sem=sems.at[1, i],
            device_id=axis(to), device_id_type=MESH)

    first = [
        copy(0, src.at[:, far, lo], chain_p, plus),
        copy(1, src.at[:, far, hi], chain_m, minus),
        copy(2, src.at[:, minus, lo], final.at[1, :, 0:half], minus),
        copy(3, src.at[:, plus, hi], final.at[1, :, half:span], plus),
    ]
    second = [
        copy(4, chain_p, final.at[0, :, 0:half], plus),
        copy(5, chain_m, final.at[0, :, half:span], minus),
    ]

    def relay():
        first[0].wait_recv()
        chain_p[...] += src[:, plus, lo]
        second[0].start()
        first[1].wait_recv()
        chain_m[...] += src[:, minus, hi]
        second[1].start()

    def finish():
        for c in (first[2], first[3], second[0], second[1]):
            c.wait_recv()
        return final[0] + final[1] + src[:, me, pl.ds(at, span)]

    def done():
        for c in first + second:
            c.wait_send()

    return first, relay, finish, done


def reduce_kernel(
    wz_ref, zh_ref, wt_ref, hw_ref, wz_out, zh_out, wt_out, hw_out,
    core_in, xchain_p, xchain_m, xfinal, xsum, yin, swap,
    zchain_p, zchain_m, zfinal, zsum, zin, wt_in, wt_mid,
    core_sem, x_sem, y_sem, swap_sem, hw_sem, z_sem, yl_sem, wa_sem, wb_sem, wc_sem,
):
    ha, wa = lax.axis_index("ha"), lax.axis_index("wa")
    yh, x, c = ha // 8, lax.rem(ha // 2, 4), lax.rem(ha, 2)
    yl, z = wa // 4, lax.rem(wa, 4)
    half_w = wz_ref.shape[2] // 2
    span = half_w // CHUNKS
    n_ha, n_wa = wt_ref.shape[0], 8

    def on_x(to):
        return (yh * 8 + to * 2 + c, wa)

    def on_z(to):
        return (ha, yl * 4 + to)

    sibling = (ha + 1 - 2 * c, wa)
    across = (lax.rem(ha + 8, 16), wa)
    beside = (ha, lax.rem(wa + 4, 8))
    corner = (lax.rem(ha + 8, 16), lax.rem(wa + 4, 8))
    rows_own = zh_ref.shape[2] // 2

    barrier = pltpu.get_barrier_semaphore()

    def greet_ha(i, carry):
        pl.semaphore_signal(barrier, inc=1, device_id=(lax.rem(ha + i, n_ha), wa), device_id_type=MESH)
        return carry

    def greet_wa(i, carry):
        pl.semaphore_signal(barrier, inc=1, device_id=(ha, lax.rem(wa + i, n_wa)), device_id_type=MESH)
        return carry

    lax.fori_loop(1, n_ha, greet_ha, 0)
    lax.fori_loop(1, n_wa, greet_wa, 0)
    pl.semaphore_signal(barrier, inc=1, device_id=corner, device_id_type=MESH)
    pl.semaphore_wait(barrier, n_ha + n_wa - 1)

    def send(source, dest, sems, to):
        return pltpu.make_async_remote_copy(
            src_ref=source, dst_ref=dest, send_sem=sems.at[0], recv_sem=sems.at[1],
            device_id=to, device_id_type=MESH)

    core = [
        send(wz_ref.at[:, :, pl.ds((1 - c) * half_w + k * span, span)], core_in.at[:, :, pl.ds(k * span, span)],
             core_sem.at[k], sibling)
        for k in range(CHUNKS)
    ]
    for k in range(CHUNKS):
        core[k].start()
    zring = ring_copies(zh_ref, zchain_p, zchain_m, zfinal, z_sem, on_z, z, 4, zh_ref.shape[2], 0)
    for cp in zring[0]:
        cp.start()

    def wt_first(i):
        to = lax.rem(ha + i, n_ha)
        return pltpu.make_async_remote_copy(
            src_ref=wt_ref.at[to], dst_ref=wt_in.at[ha], send_sem=wa_sem.at[0, to], recv_sem=wa_sem.at[1, ha],
            device_id=(to, wa), device_id_type=MESH)

    def wt_second(i):
        to = lax.rem(wa + i, n_wa)
        return pltpu.make_async_remote_copy(
            src_ref=wt_mid.at[wa], dst_ref=wt_mid.at[wa], send_sem=wb_sem.at[0, to], recv_sem=wb_sem.at[1, wa],
            device_id=(ha, to), device_id_type=MESH)

    def wt_third(i):
        to = lax.rem(ha + i, n_ha)
        return pltpu.make_async_remote_copy(
            src_ref=wt_out.at[ha], dst_ref=wt_out.at[ha], send_sem=wc_sem.at[0, to], recv_sem=wc_sem.at[1, ha],
            device_id=(to, wa), device_id_type=MESH)

    def start(make, n):
        def go(i, carry):
            make(i).start()
            return carry
        lax.fori_loop(1, n, go, 0)

    def wait_send(make, n):
        def go(i, carry):
            make(i).wait_send()
            return carry
        lax.fori_loop(1, n, go, 0)

    def wait_slot(buf, sems, me, n, own):
        def go(i, carry):
            frm = lax.rem(me + i, n)
            pltpu.make_async_remote_copy(
                src_ref=buf.at[frm], dst_ref=buf.at[frm], send_sem=sems.at[0, frm], recv_sem=sems.at[1, frm],
                device_id=own, device_id_type=MESH).wait_recv()
            return carry
        lax.fori_loop(1, n, go, 0)

    start(wt_first, n_ha)
    back = send(hw_ref.at[pl.ds(hw_out.shape[0], hw_out.shape[0])], hw_out, hw_sem, across)
    back.start()
    rings = []
    for k in range(CHUNKS):
        rows = pl.ds(k * span, span)
        core[k].wait_recv()
        core_in[:, :, rows] += wz_ref[:, :, pl.ds(c * half_w + k * span, span)]
        ring = ring_copies(core_in, xchain_p.at[k], xchain_m.at[k], xfinal.at[k], x_sem.at[k], on_x, x, 4, span, k * span)
        for cp in ring[0]:
            cp.start()
        rings.append(ring)
    zring[1]()
    wait_slot(wt_in, wa_sem, ha, n_ha, sibling)
    wt_in[ha] = wt_ref[ha]
    tot = wt_in[0]
    for i in range(1, n_ha):
        tot += wt_in[i]
    wt_mid[wa] = tot
    start(wt_second, n_wa)
    for k in range(CHUNKS):
        rings[k][1]()
    zsum[...] = zring[2]()
    own_part, far_part = pl.ds(0, rows_own), pl.ds(rows_own, rows_own)
    zys = [
        send(zsum.at[1 - yl, own_part], zin.at[0], yl_sem.at[0], beside),
        send(zsum.at[1 - yl, far_part], zin.at[1], yl_sem.at[1], corner),
        send(zsum.at[yl, far_part], zin.at[2], yl_sem.at[2], across),
    ]
    for cp in zys:
        cp.start()
    ys = []
    for k in range(CHUNKS):
        rows = pl.ds(k * span, span)
        xsum[:, rows] = rings[k][2]()
        ys.append(send(xsum.at[1 - yh, rows], yin.at[rows], y_sem.at[k], across))
        ys[k].start()
    wait_slot(wt_mid, wb_sem, wa, n_wa, beside)
    tot = wt_mid[0]
    for i in range(1, n_wa):
        tot += wt_mid[i]
    wt_out[ha] = tot
    start(wt_third, n_ha)
    for cp in zys:
        cp.wait_recv()
    zh_out[...] = (zsum[yl, own_part] + zin[0]) + (zin[1] + zin[2])
    swaps = []
    for k in range(CHUNKS):
        rows = pl.ds(k * span, span)
        ys[k].wait_recv()
        r = xsum[yh, rows] + yin[rows]
        mine = pl.ds(c * half_w + k * span, span)
        wz_out[mine] = jnp.where(c == 0, r[:, :4], r[:, 4:])
        swap[rows] = jnp.where(c == 0, r[:, 4:], r[:, :4])
        swaps.append(send(swap.at[rows], wz_out.at[mine], swap_sem.at[k], sibling))
        swaps[k].start()
    for k in range(CHUNKS):
        swaps[k].wait_recv()
    wait_slot(wt_out, wc_sem, ha, n_ha, sibling)
    for k in range(CHUNKS):
        core[k].wait_send()
        rings[k][3]()
        ys[k].wait_send()
        swaps[k].wait_send()
    zring[3]()
    for cp in zys:
        cp.wait_send()
    back.wait()
    wait_send(wt_first, n_ha)
    wait_send(wt_second, n_wa)
    wait_send(wt_third, n_ha)


def reduce_all(wz, zh, wt, hw):
    width, chans = wz.shape[2], wz.shape[4]
    rows = zh.shape[2]
    half_w = width // 2
    span = half_w // CHUNKS
    vmem = pl.BlockSpec(memory_space=pltpu.VMEM)
    buf = lambda *s: pltpu.VMEM(s, F32)
    dma = lambda *s: pltpu.SemaphoreType.DMA(s)
    return pl.pallas_call(
        reduce_kernel,
        out_shape=(
            jax.ShapeDtypeStruct((width, 4, chans), F32),
            jax.ShapeDtypeStruct((rows // 2, 8, chans), F32),
            jax.ShapeDtypeStruct(wt.shape, F32),
            jax.ShapeDtypeStruct((hw.shape[0] // 2, chans), F32),
        ),
        in_specs=[vmem] * 4,
        out_specs=[vmem] * 4,
        scratch_shapes=[
            buf(2, 4, half_w, 8, chans),
            buf(CHUNKS, 2, span // 2, 8, chans),
            buf(CHUNKS, 2, span // 2, 8, chans),
            buf(CHUNKS, 2, 2, span, 8, chans),
            buf(2, half_w, 8, chans),
            buf(half_w, 8, chans),
            buf(half_w, 4, chans),
            buf(2, rows // 2, 8, chans),
            buf(2, rows // 2, 8, chans),
            buf(2, 2, rows, 8, chans),
            buf(2, rows, 8, chans),
            buf(3, rows // 2, 8, chans),
            buf(*wt.shape),
            buf(8, *wt.shape[1:]),
            dma(CHUNKS, 2), dma(CHUNKS, 2, 6), dma(CHUNKS, 2), dma(CHUNKS, 2), dma(2), dma(2, 6), dma(3, 2),
            dma(2, 16), dma(2, 8), dma(2, 16),
        ],
        compiler_params=pltpu.CompilerParams(
            collective_id=0, has_side_effects=True, vmem_limit_bytes=48 * 1024 * 1024),
    )(wz, zh, wt, hw)


def local(hw_plane, zh_plane, wz_plane, w_in, b_in, w_out, b_out, run_index, run_count, labels):
    rows, cols, chans = hw_plane.shape
    depth = zh_plane.shape[0]
    ncls = w_out.shape[1]
    zh_rows = jnp.transpose(zh_plane, (1, 0, 2))
    hw_rows = hw_plane.reshape(rows * cols, chans)
    idx, hwx, zh2, labx = exchange(run_index, hw_rows, zh_rows, labels[0])
    hw, zh, wz, wt = decode_runs(
        run_index, idx, run_count, hw_rows, hwx, zh2, wz_plane.reshape(cols // 2, 2 * depth, chans),
        labels[0], labx, w_in, b_in, w_out, b_out,
    )
    wz_grad, zh_grad, wt, back = reduce_all(
        wz.reshape(2, 4, cols, 8, chans), zh.reshape(2, 4, 2 * rows, 8, chans), wt.reshape(16, -1, chans), hw)
    hw_grad, wz_grad, zh_grad, gwi, gbi, gwo, gbo = finish(
        run_index, run_count, hw, back, wz_grad, zh_grad, wt.reshape(-1, chans), rows * cols, w_out.shape[0], ncls)
    return (hw_grad.reshape(rows, cols, chans), zh_grad, wz_grad, gwi, gbi[0], gwo, gbo[0])


def solution(mesh):
    placed = (
        P("ha", "wa", None),
        P(None, "ha", None),
        P("wa", None, None),
        P(),
        P(),
        P(),
        P(),
        P(("ha", "wa"), None),
        P(("ha", "wa")),
        P(("ha", "wa"), None, None),
    )
    return jax.shard_map(
        local,
        mesh=mesh,
        in_specs=placed,
        out_specs=(P("ha", "wa", None), P("wa", "ha", None), P("wa", "ha", None), P(), P(), P(), P()),
        check_vma=False,
    )
```

```python
import functools

import jax
import jax.numpy as jnp
from jax import lax
from jax.experimental import pallas as pl
from jax.experimental.pallas import tpu as pltpu
from jax.sharding import PartitionSpec as P

F32 = jnp.float32
BF16 = jnp.bfloat16
GRAD_SCALE = 0.25
GROUP = 32
CLS = 32
CHUNKS = 2
MESH = pl.DeviceIdType.MESH


def dotg(left, right, dims):
    return lax.dot_general(left, right, ((dims[0], dims[1]), ((), ())), preferred_element_type=F32)


def exchange_kernel(
    ids_ref, idrow_ref, hw_ref, zh_ref, labels_ref,
    ids_out, hw_out, zh_out, lab_out,
    hw32, rows32, rows16, lab16, sem, z_sem,
):
    ha, wa = lax.axis_index("ha"), lax.axis_index("wa")
    z, base = lax.rem(wa, 4), wa - lax.rem(wa, 4)
    cap = labels_ref.shape[0]
    half = cap // 2
    own_rows = zh_ref.shape[0]
    part = own_rows // 4
    across = (lax.rem(ha + 8, 16), wa)
    corner = (lax.rem(ha + 8, 16), lax.rem(wa + 4, 8))
    up, down, far = base + lax.rem(z + 1, 4), base + lax.rem(z + 3, 4), lax.rem(z + 2, 4)
    barrier = pltpu.get_barrier_semaphore()
    for to in (across, corner, (ha, up), (ha, down)):
        pl.semaphore_signal(barrier, inc=1, device_id=to, device_id_type=MESH)
    pl.semaphore_wait(barrier, 4)

    def send(source, dest, sems, to):
        return pltpu.make_async_remote_copy(
            src_ref=source, dst_ref=dest, send_sem=sems.at[0], recv_sem=sems.at[1],
            device_id=to, device_id_type=MESH)

    got = own_rows + z * part
    fetch = send(zh_ref.at[pl.ds(z * part, part)], zh_out.at[pl.ds(got, part)], z_sem.at[0], corner)
    fetch.start()
    keep = pltpu.make_async_copy(zh_ref, zh_out.at[pl.ds(0, own_rows)], sem.at[3, 0])
    keep.start()
    lab16[...] = labels_ref[half:].astype(F32).astype(BF16)
    to_lab = send(lab16, lab_out, sem.at[0], across)
    to_lab.start()
    to_ids = send(idrow_ref, ids_out, sem.at[1], across)
    to_ids.start()
    hw32[...] = hw_ref[...].astype(F32)

    def pick(i, carry):
        for k in range(8):
            s = i * 8 + k
            at = 2 * ids_ref[0, half + s]
            for p in range(2):
                rows32[pl.ds(2 * s + p, 1), :] = hw32[pl.ds(at + p, 1), :]
        return carry

    lax.fori_loop(0, half // 8, pick, 0)
    rows16[...] = rows32[...].astype(BF16)
    to_hw = send(rows16, hw_out, sem.at[2], across)
    to_hw.start()
    fetch.wait_recv()
    mine = zh_out.at[pl.ds(got, part)]
    to_up = send(mine, mine, z_sem.at[1], (ha, up))
    to_down = send(mine, mine, z_sem.at[2], (ha, down))
    to_up.start()
    to_down.start()
    from_down = own_rows + lax.rem(z + 3, 4) * part
    from_up = own_rows + lax.rem(z + 1, 4) * part
    to_up.wait_recv()
    piece = zh_out.at[pl.ds(from_down, part // 2)]
    on_up = send(piece, piece, z_sem.at[3], (ha, up))
    on_up.start()
    to_down.wait_recv()
    piece = zh_out.at[pl.ds(from_up + part // 2, part // 2)]
    on_down = send(piece, piece, z_sem.at[4], (ha, down))
    on_down.start()
    keep.wait()
    for cp in (to_lab, to_ids, to_hw, on_up, on_down):
        cp.wait()
    for cp in (fetch, to_up, to_down):
        cp.wait_send()


def exchange(ids, hw, zh, labels):
    vmem = pl.BlockSpec(memory_space=pltpu.VMEM)
    half = labels.shape[0] // 2
    dma = lambda *s: pltpu.SemaphoreType.DMA(s)
    return pl.pallas_call(
        exchange_kernel,
        out_shape=(
            jax.ShapeDtypeStruct(ids.shape, jnp.int32),
            jax.ShapeDtypeStruct((2 * half, hw.shape[1]), BF16),
            jax.ShapeDtypeStruct((2 * zh.shape[0],) + zh.shape[1:], BF16),
            jax.ShapeDtypeStruct((half, labels.shape[1]), BF16),
        ),
        in_specs=[pl.BlockSpec(memory_space=pltpu.SMEM)] + [vmem] * 4,
        out_specs=[vmem] * 4,
        scratch_shapes=[
            pltpu.VMEM(hw.shape, F32), pltpu.VMEM((2 * half, hw.shape[1]), F32),
            pltpu.VMEM((2 * half, hw.shape[1]), BF16), pltpu.VMEM((half, labels.shape[1]), BF16),
            dma(4, 2), dma(5, 2),
        ],
        compiler_params=pltpu.CompilerParams(
            collective_id=1, has_side_effects=True, vmem_limit_bytes=32 * 1024 * 1024),
    )(ids, ids, hw, zh, labels)


def decode_kernel(
    ids_ref, idx_ref, count_ref, hw_ref, hwx_ref, zh_ref, wz_ref, labels_ref, labx_ref, win_ref, bin_ref, wout_ref, bout_ref,
    hw_out, zh_out, wz_out, wt_out,
    hw32, labs, gwi_ref, gwo_ref, gbo_ref,
):
    rows, depth, chans = zh_ref.shape
    pairs = wz_ref.shape[0]
    half = labx_ref.shape[0]
    own_hw = hw_ref.shape[0]
    own_n = jnp.minimum(count_ref[0], half)
    hw32[:own_hw] = hw_ref[...].astype(F32)
    hw32[own_hw:] = hwx_ref[...].astype(F32)
    labs[:half] = labels_ref[:half]
    labs[half:] = labx_ref[...].astype(F32).astype(jnp.int32)
    hw_out[...] = jnp.zeros_like(hw_out)
    zh_out[...] = jnp.zeros_like(zh_out)
    wz_out[...] = jnp.zeros_like(wz_out)
    gwi_ref[...] = jnp.zeros_like(gwi_ref)
    gwo_ref[...] = jnp.zeros_like(gwo_ref)
    gbo_ref[...] = jnp.zeros_like(gbo_ref)
    samples = GROUP * 2 * depth
    run = 2 * depth

    def body(step, carry):
        base = step * GROUP
        spots = []
        parts = []
        for g in range(GROUP):
            i = base + g
            own = i < own_n
            j = jnp.maximum(i - own_n, 0)
            rid = jnp.where(own, ids_ref[0, i], idx_ref[0, half + j])
            row = rid // pairs + jnp.where(own, 0, rows // 2)
            pair = rid % pairs
            hw_at = jnp.where(own, 2 * rid, own_hw + 2 * j)
            slot = jnp.where(own, i, half + j)
            spots.append((slot, row, pair))
            zh = zh_ref[row].astype(F32)
            for p in range(2):
                hw = hw32[pl.ds(hw_at + p, 1), :]
                wz = wz_ref[pair, p * depth:(p + 1) * depth, :].astype(F32)
                parts.append(((hw + zh) + wz).astype(BF16))
        feats = jnp.concatenate(parts, axis=0)
        u = jnp.dot(feats, win_ref[...] * 0.5, preferred_element_type=F32) + bin_ref[...] * 0.5
        a = jnp.tanh(u) + 1.0
        h = u * a
        hid = h.astype(BF16)
        logits = dotg(wout_ref[...], hid, ((1,), (1,)))
        dparts = []
        for g in range(GROUP):
            lt = logits[:, g * run:(g + 1) * run] + bout_ref[...]
            top = jnp.max(lt, axis=0, keepdims=True)
            e = jnp.exp(lt - top)
            inv = GRAD_SCALE / jnp.sum(e, axis=0, keepdims=True)
            lab = labs[pl.ds(spots[g][0], 1), :]
            cls = lax.broadcasted_iota(jnp.int32, lt.shape, 0)
            hot = jnp.where(cls == lab, GRAD_SCALE, 0.0)
            dparts.append((e * inv - hot).astype(BF16))
        dlt = jnp.concatenate(dparts, axis=1)
        gwo_ref[...] += jnp.dot(dlt, hid, preferred_element_type=F32)
        tot = dparts[0].astype(F32)
        for g in range(1, GROUP):
            tot += dparts[g].astype(F32)
        gbo_ref[...] += tot
        dhh = dotg(dlt, wout_ref[...] * 0.5, ((0,), (0,)))
        q = (u + u + 1.0) - h
        dpre = (dhh * a * q).astype(BF16)
        lhs = jnp.concatenate([feats.T, jnp.ones((16, samples), BF16)], axis=0)
        gwi_ref[...] += jnp.dot(lhs, dpre, preferred_element_type=F32)
        df = dotg(dpre, win_ref[...], ((1,), (1,)))
        for g in range(GROUP):
            slot, row, pair = spots[g]
            d = df[g * run:(g + 1) * run]
            zh_out[:, row] += (d[:depth] + d[depth:]).reshape(depth // 8, 8, chans)
            for p in range(2):
                wz_out[:, 2 * pair + p] += d[p * depth:(p + 1) * depth].reshape(depth // 8, 8, chans)
                hw_out[pl.ds(2 * slot + p, 1), :] = jnp.sum(d[p * depth:(p + 1) * depth], axis=0, keepdims=True)
        return carry

    lax.fori_loop(0, half // GROUP, body, 0)
    top = chans + 16
    wt_out[0:top] = gwi_ref[:, :128]
    wt_out[top:2 * top] = gwi_ref[:, 128:]
    wt_out[2 * top:2 * top + CLS] = gwo_ref[:, :128]
    wt_out[2 * top + CLS:2 * top + 2 * CLS] = gwo_ref[:, 128:]
    wt_out[2 * top + 2 * CLS:] = gbo_ref[...]


def decode_runs(ids, idx, count, hw, hwx, zh, wz, labels, labx, w_in, b_in, w_out, b_out):
    rows, depth, chans = zh.shape
    pairs = wz.shape[0]
    hid, ncls = w_out.shape
    wout = jnp.pad(w_out.T, ((0, CLS - ncls), (0, 0)))
    bout = jnp.pad(b_out, (0, CLS - ncls), constant_values=-1e30).reshape(CLS, 1)
    smem = pl.BlockSpec(memory_space=pltpu.SMEM)
    vmem = pl.BlockSpec(memory_space=pltpu.VMEM)
    return pl.pallas_call(
        decode_kernel,
        out_shape=(
            jax.ShapeDtypeStruct((2 * labels.shape[0], chans), F32),
            jax.ShapeDtypeStruct((depth // 8, rows, 8, chans), F32),
            jax.ShapeDtypeStruct((depth // 8, 2 * pairs, 8, chans), F32),
            jax.ShapeDtypeStruct((2 * (chans + 16) + 3 * CLS, chans), F32),
        ),
        in_specs=[smem] * 3 + [vmem] * 10,
        out_specs=[vmem] * 4,
        scratch_shapes=[
            pltpu.VMEM((hw.shape[0] + hwx.shape[0], chans), F32),
            pltpu.VMEM(labels.shape, jnp.int32),
            pltpu.VMEM((chans + 16, hid), F32),
            pltpu.VMEM((CLS, hid), F32),
            pltpu.VMEM((CLS, 2 * depth), F32),
        ],
        compiler_params=pltpu.CompilerParams(vmem_limit_bytes=48 * 1024 * 1024),
    )(ids, idx, count, hw, hwx, zh, wz, labels, labx, w_in, b_in.reshape(1, hid), wout, bout)


def finish_kernel(
    ids_ref, count_ref, own_ref, back_ref, wz_ref, zh_ref, wt_ref,
    hw_out, wz_out, zh_out, gwi_out, gbi_out, gwo_out, gbo_out,
):
    cap = ids_ref.shape[1]
    half = cap // 2
    used = count_ref[0]
    chans = hw_out.shape[1]
    ncls = gwo_out.shape[1]
    hw_out[...] = jnp.zeros_like(hw_out)

    def put(source, start):
        def go(s, carry):
            for p in range(2):
                hw_out[pl.ds(2 * ids_ref[0, start + s] + p, 1), :] = source[pl.ds(2 * s + p, 1), :]
            return carry
        return go

    lax.fori_loop(0, jnp.minimum(used, half), put(own_ref, 0), 0)
    lax.fori_loop(0, jnp.maximum(used - half, 0), put(back_ref, half), 0)
    wz_out[...] = wz_ref[...]
    for i in range(8):
        zh_out[i] = zh_ref[:, i, :]
    top = chans + 16
    gwi_out[:, :128] = wt_ref[:chans]
    gwi_out[:, 128:] = wt_ref[top:top + chans]
    gbi_out[:, :128] = wt_ref[chans:chans + 1]
    gbi_out[:, 128:] = wt_ref[top + chans:top + chans + 1]
    at = 2 * top
    gwo_out[:128] = wt_ref[at:at + CLS].T[:, :ncls]
    gwo_out[128:] = wt_ref[at + CLS:at + 2 * CLS].T[:, :ncls]
    gbo_out[...] = jnp.sum(wt_ref[at + 2 * CLS:at + 3 * CLS].T, axis=0, keepdims=True)[:, :ncls]


def finish(ids, count, own, back, wz, zh, wt, hw_rows, hid, ncls):
    smem = pl.BlockSpec(memory_space=pltpu.SMEM)
    vmem = pl.BlockSpec(memory_space=pltpu.VMEM)
    chans = own.shape[1]
    return pl.pallas_call(
        finish_kernel,
        out_shape=(
            jax.ShapeDtypeStruct((hw_rows, chans), F32),
            jax.ShapeDtypeStruct(wz.shape, F32),
            jax.ShapeDtypeStruct((8, zh.shape[0], chans), F32),
            jax.ShapeDtypeStruct((chans, hid), F32),
            jax.ShapeDtypeStruct((1, hid), F32),
            jax.ShapeDtypeStruct((hid, ncls), F32),
            jax.ShapeDtypeStruct((1, ncls), F32),
        ),
        in_specs=[smem] * 2 + [vmem] * 5,
        out_specs=[vmem] * 7,
        compiler_params=pltpu.CompilerParams(vmem_limit_bytes=32 * 1024 * 1024),
    )(ids, count, own, back, wz, zh, wt)


def pack(v):
    most = jnp.maximum(jnp.max(jnp.abs(v), axis=1, keepdims=True), 1e-30)
    return jnp.round(v * (32766.0 / most)).astype(jnp.int32).astype(jnp.int16), most * (1.0 / 32766.0)


def unpack(q, scale):
    return q.astype(jnp.int32).astype(F32) * scale


class Coded:
    def __init__(self, out, out_scale, into, into_scale, sems, to):
        self.out, self.out_scale, self.into, self.into_scale = out, out_scale, into, into_scale
        self.copies = [
            pltpu.make_async_remote_copy(
                src_ref=a, dst_ref=b, send_sem=sems.at[0, i], recv_sem=sems.at[1, i], device_id=to, device_id_type=MESH)
            for i, (a, b) in enumerate(((out, into), (out_scale, into_scale)))
        ]

    def send(self, v):
        self.out[...], self.out_scale[...] = pack(v)
        for cp in self.copies:
            cp.start()

    def receive(self):
        for cp in self.copies:
            cp.wait_recv()
        return unpack(self.into[...], self.into_scale[...])

    def done(self):
        for cp in self.copies:
            cp.wait_send()


def coded_buffers(n, groups, rows, chans):
    return [
        pltpu.VMEM((n, groups, rows, chans), jnp.int16), pltpu.VMEM((n, groups, 1, chans), F32),
        pltpu.VMEM((n, groups, rows, chans), jnp.int16), pltpu.VMEM((n, groups, 1, chans), F32),
        pltpu.SemaphoreType.DMA((n, 2, 2)),
    ]


def coded(bufs, i, to):
    out, out_scale, into, into_scale, sems = bufs
    return Coded(out.at[i], out_scale.at[i], into.at[i], into_scale.at[i], sems.at[i], to)


class Ring:
    def __init__(self, src, bufs, first, axis, me, span, at):
        self.src, self.me, self.span = src, me, span
        self.plus, self.minus, self.far = lax.rem(me + 1, 4), lax.rem(me + 3, 4), lax.rem(me + 2, 4)
        self.lo, self.hi = pl.ds(at, span // 2), pl.ds(at + span // 2, span // 2)
        to = [axis(self.plus), axis(self.minus)]
        self.msgs = [coded(bufs, first + i, to[d]) for i, d in enumerate((0, 1, 1, 0, 0, 1))]

    def part(self, where, half):
        v = self.src[:, where, half]
        return v.reshape(v.shape[0], -1, v.shape[-1])

    def begin(self):
        self.msgs[0].send(self.part(self.far, self.lo))
        self.msgs[1].send(self.part(self.far, self.hi))
        self.msgs[2].send(self.part(self.minus, self.lo))
        self.msgs[3].send(self.part(self.plus, self.hi))

    def relay(self):
        self.msgs[4].send(self.msgs[0].receive() + self.part(self.plus, self.lo))
        self.msgs[5].send(self.msgs[1].receive() + self.part(self.minus, self.hi))

    def finish(self):
        lo = self.part(self.me, self.lo) + self.msgs[2].receive() + self.msgs[4].receive()
        hi = self.part(self.me, self.hi) + self.msgs[3].receive() + self.msgs[5].receive()
        return lo, hi

    def done(self):
        for m in self.msgs:
            m.done()


def reduce_kernel(
    wz_ref, zh_ref, wt_ref, hw_ref, wz_out, zh_out, wt_out, hw_out,
    wz_own, core_in, xsum, swap, zsum, wt_in, wt_mid,
    own_sem, core_sem, swap_sem, wa_sem, wb_sem, wc_sem, *bufs,
):
    xbufs, ybufs, zbufs, zybufs, hwbufs = (bufs[5 * i:5 * i + 5] for i in range(5))
    ha, wa = lax.axis_index("ha"), lax.axis_index("wa")
    yh, x, c = ha // 8, lax.rem(ha // 2, 4), lax.rem(ha, 2)
    yl, z = wa // 4, lax.rem(wa, 4)
    half_w = wz_ref.shape[2] // 2
    span = half_w // CHUNKS
    n_ha, n_wa = wt_ref.shape[0], 8

    def on_x(to):
        return (yh * 8 + to * 2 + c, wa)

    def on_z(to):
        return (ha, yl * 4 + to)

    sibling = (ha + 1 - 2 * c, wa)
    across = (lax.rem(ha + 8, 16), wa)
    beside = (ha, lax.rem(wa + 4, 8))
    corner = (lax.rem(ha + 8, 16), lax.rem(wa + 4, 8))
    rows_own = zh_ref.shape[2] // 2

    barrier = pltpu.get_barrier_semaphore()

    def greet_ha(i, carry):
        pl.semaphore_signal(barrier, inc=1, device_id=(lax.rem(ha + i, n_ha), wa), device_id_type=MESH)
        return carry

    def greet_wa(i, carry):
        pl.semaphore_signal(barrier, inc=1, device_id=(ha, lax.rem(wa + i, n_wa)), device_id_type=MESH)
        return carry

    load = pltpu.make_async_copy(wz_ref.at[:, :, pl.ds(c * half_w, half_w)], wz_own, own_sem.at[0])
    load.start()
    lax.fori_loop(1, n_ha, greet_ha, 0)
    lax.fori_loop(1, n_wa, greet_wa, 0)
    pl.semaphore_signal(barrier, inc=1, device_id=corner, device_id_type=MESH)
    pl.semaphore_wait(barrier, n_ha + n_wa - 1)

    def send(source, dest, sems, to):
        return pltpu.make_async_remote_copy(
            src_ref=source, dst_ref=dest, send_sem=sems.at[0], recv_sem=sems.at[1],
            device_id=to, device_id_type=MESH)

    core = [
        send(wz_ref.at[:, :, pl.ds((1 - c) * half_w + k * span, span)], core_in.at[:, :, pl.ds(k * span, span)],
             core_sem.at[k], sibling)
        for k in range(CHUNKS)
    ]
    for k in range(CHUNKS):
        core[k].start()
    zring = Ring(zh_ref, zbufs, 0, on_z, z, zh_ref.shape[2], 0)
    zring.begin()

    def wt_first(i):
        to = lax.rem(ha + i, n_ha)
        return pltpu.make_async_remote_copy(
            src_ref=wt_ref.at[to], dst_ref=wt_in.at[ha], send_sem=wa_sem.at[0, to], recv_sem=wa_sem.at[1, ha],
            device_id=(to, wa), device_id_type=MESH)

    def wt_second(i):
        to = lax.rem(wa + i, n_wa)
        return pltpu.make_async_remote_copy(
            src_ref=wt_mid.at[wa], dst_ref=wt_mid.at[wa], send_sem=wb_sem.at[0, to], recv_sem=wb_sem.at[1, wa],
            device_id=(ha, to), device_id_type=MESH)

    def wt_third(i):
        to = lax.rem(ha + i, n_ha)
        return pltpu.make_async_remote_copy(
            src_ref=wt_out.at[ha], dst_ref=wt_out.at[ha], send_sem=wc_sem.at[0, to], recv_sem=wc_sem.at[1, ha],
            device_id=(to, wa), device_id_type=MESH)

    def start(make, n):
        def go(i, carry):
            make(i).start()
            return carry
        lax.fori_loop(1, n, go, 0)

    def wait_send(make, n):
        def go(i, carry):
            make(i).wait_send()
            return carry
        lax.fori_loop(1, n, go, 0)

    def wait_slot(buf, sems, me, n, own):
        def go(i, carry):
            frm = lax.rem(me + i, n)
            pltpu.make_async_remote_copy(
                src_ref=buf.at[frm], dst_ref=buf.at[frm], send_sem=sems.at[0, frm], recv_sem=sems.at[1, frm],
                device_id=own, device_id_type=MESH).wait_recv()
            return carry
        lax.fori_loop(1, n, go, 0)

    start(wt_first, n_ha)
    chans = hw_ref.shape[1]
    back = coded(hwbufs, 0, across)
    back.send(hw_ref[hw_out.shape[0]:].reshape(-1, 128, chans))
    load.wait()
    rings = []
    for k in range(CHUNKS):
        rows = pl.ds(k * span, span)
        core[k].wait_recv()
        core_in[:, :, rows] += wz_own[:, :, rows]
        rings.append(Ring(core_in, xbufs, 6 * k, on_x, x, span, k * span))
        rings[k].begin()
    zring.relay()
    wait_slot(wt_in, wa_sem, ha, n_ha, sibling)
    wt_in[ha] = wt_ref[ha]
    tot = wt_in[0]
    for i in range(1, n_ha):
        tot += wt_in[i]
    wt_mid[wa] = tot
    start(wt_second, n_wa)
    for k in range(CHUNKS):
        rings[k].relay()
    zsum[0], zsum[1] = zring.finish()
    zys = [coded(zybufs, i, to) for i, to in enumerate((beside, corner, across))]
    zys[0].send(zsum[0, pl.ds(1 - yl, 1)])
    zys[1].send(zsum[1, pl.ds(1 - yl, 1)])
    zys[2].send(zsum[1, pl.ds(yl, 1)])
    ys = []
    for k in range(CHUNKS):
        rows = pl.ds(k * span, span)
        lo, hi = rings[k].finish()
        xsum[:, k, 0:span * 4], xsum[:, k, span * 4:] = lo, hi
        ys.append(coded(ybufs, k, across))
        ys[k].send(xsum[pl.ds(1 - yh, 1), k])
    wait_slot(wt_mid, wb_sem, wa, n_wa, beside)
    tot = wt_mid[0]
    for i in range(1, n_wa):
        tot += wt_mid[i]
    wt_out[ha] = tot
    start(wt_third, n_ha)
    total = zsum[0, pl.ds(yl, 1)]
    for m in zys:
        total += m.receive()
    zh_out[...] = total.reshape(zh_out.shape)
    swaps = []
    for k in range(CHUNKS):
        rows = pl.ds(k * span, span)
        r = (xsum[pl.ds(yh, 1), k] + ys[k].receive()).reshape(span, 8, chans)
        mine = pl.ds(c * half_w + k * span, span)
        wz_out[mine] = jnp.where(c == 0, r[:, :4], r[:, 4:])
        swap[rows] = jnp.where(c == 0, r[:, 4:], r[:, :4])
        swaps.append(send(swap.at[rows], wz_out.at[mine], swap_sem.at[k], sibling))
        swaps[k].start()
    hw_out[...] = back.receive().reshape(hw_out.shape)
    for k in range(CHUNKS):
        swaps[k].wait_recv()
    wait_slot(wt_out, wc_sem, ha, n_ha, sibling)
    for k in range(CHUNKS):
        core[k].wait_send()
        rings[k].done()
        ys[k].done()
        swaps[k].wait_send()
    zring.done()
    for m in zys + [back]:
        m.done()
    wait_send(wt_first, n_ha)
    wait_send(wt_second, n_wa)
    wait_send(wt_third, n_ha)


def reduce_all(wz, zh, wt, hw):
    width, chans = wz.shape[2], wz.shape[4]
    rows = zh.shape[2]
    half_w = width // 2
    span = half_w // CHUNKS
    vmem = pl.BlockSpec(memory_space=pltpu.VMEM)
    buf = lambda *s: pltpu.VMEM(s, F32)
    dma = lambda *s: pltpu.SemaphoreType.DMA(s)
    return pl.pallas_call(
        reduce_kernel,
        out_shape=(
            jax.ShapeDtypeStruct((width, 4, chans), F32),
            jax.ShapeDtypeStruct((rows // 2, 8, chans), F32),
            jax.ShapeDtypeStruct(wt.shape, F32),
            jax.ShapeDtypeStruct((hw.shape[0] // 2, chans), F32),
        ),
        in_specs=[pl.BlockSpec(memory_space=pl.ANY)] + [vmem] * 3,
        out_specs=[vmem] * 4,
        scratch_shapes=[
            buf(2, 4, half_w, 8, chans),
            buf(2, 4, half_w, 8, chans),
            buf(2, CHUNKS, span * 8, chans),
            buf(half_w, 4, chans),
            buf(2, 2, rows * 4, chans),
            buf(*wt.shape),
            buf(8, *wt.shape[1:]),
            dma(1), dma(CHUNKS, 2), dma(CHUNKS, 2), dma(2, 16), dma(2, 8), dma(2, 16),
            *coded_buffers(6 * CHUNKS, 2, span * 4, chans),
            *coded_buffers(CHUNKS, 1, span * 8, chans),
            *coded_buffers(6, 2, rows * 4, chans),
            *coded_buffers(3, 1, rows * 4, chans),
            *coded_buffers(1, hw.shape[0] // 256, 128, chans),
        ],
        compiler_params=pltpu.CompilerParams(
            collective_id=0, has_side_effects=True, vmem_limit_bytes=48 * 1024 * 1024),
    )(wz, zh, wt, hw)


def local(hw_plane, zh_plane, wz_plane, w_in, b_in, w_out, b_out, run_index, run_count, labels):
    rows, cols, chans = hw_plane.shape
    depth = zh_plane.shape[0]
    ncls = w_out.shape[1]
    zh_rows = jnp.transpose(zh_plane, (1, 0, 2))
    hw_rows = hw_plane.reshape(rows * cols, chans)
    idx, hwx, zh2, labx = exchange(run_index, hw_rows, zh_rows, labels[0])
    hw, zh, wz, wt = decode_runs(
        run_index, idx, run_count, hw_rows, hwx, zh2, wz_plane.reshape(cols // 2, 2 * depth, chans),
        labels[0], labx, w_in, b_in, w_out, b_out,
    )
    wz_grad, zh_grad, wt, back = reduce_all(
        wz.reshape(2, 4, cols, 8, chans), zh.reshape(2, 4, 2 * rows, 8, chans), wt.reshape(16, -1, chans), hw)
    hw_grad, wz_grad, zh_grad, gwi, gbi, gwo, gbo = finish(
        run_index, run_count, hw, back, wz_grad, zh_grad, wt.reshape(-1, chans), rows * cols, w_out.shape[0], ncls)
    return (hw_grad.reshape(rows, cols, chans), zh_grad, wz_grad, gwi, gbi[0], gwo, gbo[0])


def solution(mesh):
    placed = (
        P("ha", "wa", None),
        P(None, "ha", None),
        P("wa", None, None),
        P(),
        P(),
        P(),
        P(),
        P(("ha", "wa"), None),
        P(("ha", "wa")),
        P(("ha", "wa"), None, None),
    )
    return jax.shard_map(
        local,
        mesh=mesh,
        in_specs=placed,
        out_specs=(P("ha", "wa", None), P("wa", "ha", None), P("wa", "ha", None), P(), P(), P(), P()),
        check_vma=False,
    )
```

```python
import functools

import jax
import jax.numpy as jnp
from jax import lax
from jax.experimental import pallas as pl
from jax.experimental.pallas import tpu as pltpu
from jax.sharding import PartitionSpec as P

F32 = jnp.float32
BF16 = jnp.bfloat16
GRAD_SCALE = 0.25
GROUP = 32
CLS = 32
CHUNKS = 2
EXCHANGE_VMEM = 56 * 1024 * 1024
DECODE_VMEM = 40 * 1024 * 1024
REDUCE_VMEM = 32 * 1024 * 1024
MESH = pl.DeviceIdType.MESH


def dotg(left, right, dims):
    return lax.dot_general(left, right, ((dims[0], dims[1]), ((), ())), preferred_element_type=F32)


def exchange_kernel(
    ids_ref, idrow_ref, hw_ref, zh_ref, labels_ref,
    ids_out, hw_out, zh_out, lab_out,
    hwv, zhv, labv, hw32, zh32, rows32, rows16, lab16, load_sem, sem, z_sem,
):
    ha, wa = lax.axis_index("ha"), lax.axis_index("wa")
    z, base = lax.rem(wa, 4), wa - lax.rem(wa, 4)
    half = lab16.shape[0]
    own_rows = zh_ref.shape[1]
    part = own_rows // 4
    across = (lax.rem(ha + 8, 16), wa)
    corner = (lax.rem(ha + 8, 16), lax.rem(wa + 4, 8))
    ring = [(ha, base + lax.rem(z + k, 4)) for k in (1, 3, 2)]
    loads = [
        pltpu.make_async_copy(zh_ref, zhv, load_sem.at[0]),
        pltpu.make_async_copy(hw_ref, hwv, load_sem.at[1]),
        pltpu.make_async_copy(labels_ref.at[pl.ds(half, half)], labv, load_sem.at[2]),
    ]
    for cp in loads:
        cp.start()
    barrier = pltpu.get_barrier_semaphore()
    for to in [across, corner] + ring:
        pl.semaphore_signal(barrier, inc=1, device_id=to, device_id_type=MESH)

    def send(source, dest, sems, to):
        return pltpu.make_async_remote_copy(
            src_ref=source, dst_ref=dest, send_sem=sems.at[0], recv_sem=sems.at[1],
            device_id=to, device_id_type=MESH)

    def turn(q):
        at = pl.multiple_of(q * part, part)
        zh_out[pl.ds(at, part)] = jnp.swapaxes(zh32[:, pl.ds(at, part), :], 0, 1).astype(BF16)

    loads[0].wait()
    zh32[...] = zhv[...].astype(F32)
    turn(z)
    pl.semaphore_wait(barrier, 5)
    got = own_rows + z * part
    fetch = send(zh_out.at[pl.ds(z * part, part)], zh_out.at[pl.ds(got, part)], z_sem.at[0], corner)
    fetch.start()
    for k in (1, 2, 3):
        turn(lax.rem(z + k, 4))
    loads[2].wait()
    lab16[...] = labv[...].astype(F32).astype(BF16)
    loads[1].wait()
    hw32[...] = hwv[...].astype(F32)

    def pick(i, carry):
        for k in range(8):
            s = i * 8 + k
            at = 2 * ids_ref[0, half + s]
            for p in range(2):
                rows32[pl.ds(2 * s + p, 1), :] = hw32[pl.ds(at + p, 1), :]
        return carry

    lax.fori_loop(0, half // 8, pick, 0)
    rows16[...] = rows32[...].astype(BF16)
    fetch.wait_recv()
    mine = zh_out.at[pl.ds(got, part)]
    outs = [send(mine, mine, z_sem.at[1 + k], to) for k, to in enumerate(ring)]
    outs += [send(rows16, hw_out, sem.at[0], across), send(lab16, lab_out, sem.at[1], across),
             send(idrow_ref, ids_out, sem.at[2], across)]
    for cp in outs:
        cp.start()
    for cp in outs:
        cp.wait()
    fetch.wait_send()


def exchange(ids, hw, zh, labels):
    vmem = pl.BlockSpec(memory_space=pltpu.VMEM)
    hbm = pl.BlockSpec(memory_space=pl.ANY)
    half = labels.shape[0] // 2
    depth, rows, chans = zh.shape
    dma = lambda *s: pltpu.SemaphoreType.DMA(s)
    return pl.pallas_call(
        exchange_kernel,
        out_shape=(
            jax.ShapeDtypeStruct(ids.shape, jnp.int32),
            jax.ShapeDtypeStruct((2 * half, chans), BF16),
            jax.ShapeDtypeStruct((2 * rows, depth, chans), BF16),
            jax.ShapeDtypeStruct((half, labels.shape[1]), BF16),
        ),
        in_specs=[pl.BlockSpec(memory_space=pltpu.SMEM), vmem, hbm, hbm, hbm],
        out_specs=[vmem] * 4,
        scratch_shapes=[
            pltpu.VMEM(hw.shape, BF16), pltpu.VMEM(zh.shape, BF16), pltpu.VMEM((half, labels.shape[1]), jnp.int32),
            pltpu.VMEM(hw.shape, F32), pltpu.VMEM(zh.shape, F32), pltpu.VMEM((2 * half, chans), F32),
            pltpu.VMEM((2 * half, chans), BF16), pltpu.VMEM((half, labels.shape[1]), BF16),
            dma(3), dma(3, 2), dma(4, 2),
        ],
        compiler_params=pltpu.CompilerParams(
            collective_id=1, has_side_effects=True, vmem_limit_bytes=EXCHANGE_VMEM),
    )(ids, ids, hw, zh, labels)


def decode_kernel(
    ids_ref, idx_ref, count_ref, hw_ref, hwx_ref, zh_ref, wz_ref, labels_ref, labx_ref, win_ref, bin_ref, wout_ref, bout_ref,
    hw_out, zh_out, wz_out, wt_out,
    hw32, labs, wpad, wout_t, gwi_ref, gwo_ref, gbo_ref,
):
    rows, depth, chans = zh_ref.shape
    pairs = wz_ref.shape[0]
    half = labx_ref.shape[0]
    own_hw = hw_ref.shape[0]
    own_n = jnp.minimum(count_ref[0], half)
    hw32[:own_hw] = hw_ref[...].astype(F32)
    hw32[own_hw:] = hwx_ref[...].astype(F32)
    labs[:half] = labels_ref[:half]
    labs[half:] = labx_ref[...].astype(F32).astype(jnp.int32)
    hw_out[...] = jnp.zeros_like(hw_out)
    zh_out[...] = jnp.zeros_like(zh_out)
    wz_out[...] = jnp.zeros_like(wz_out)
    gwi_ref[...] = jnp.zeros_like(gwi_ref)
    gwo_ref[...] = jnp.zeros_like(gwo_ref)
    gbo_ref[...] = jnp.zeros_like(gbo_ref)
    ncls = wout_ref.shape[1]
    wpad[...] = jnp.zeros_like(wpad)
    wpad[:ncls] = wout_ref[...].astype(F32).T
    wout_t[...] = wpad[...].astype(BF16)
    at_row = lax.broadcasted_iota(jnp.int32, (CLS, ncls), 0)
    at_col = lax.broadcasted_iota(jnp.int32, (CLS, ncls), 1)
    bcol = jnp.sum(jnp.where(at_row == at_col, bout_ref[...], 0.0), axis=1, keepdims=True)
    bcol = jnp.where(lax.broadcasted_iota(jnp.int32, (CLS, 1), 0) < ncls, bcol, -1e30)
    samples = GROUP * 2 * depth
    low = lax.broadcasted_iota(jnp.int32, (depth // 8, 8, chans), 1) < 4
    run = 2 * depth

    def body(step, carry):
        base = step * GROUP
        spots = []
        parts = []
        for g in range(GROUP):
            i = base + g
            own = i < own_n
            j = jnp.maximum(i - own_n, 0)
            rid = jnp.where(own, ids_ref[0, i], idx_ref[0, half + j])
            row = rid // pairs + jnp.where(own, 0, rows // 2)
            pair = rid % pairs
            hw_at = jnp.where(own, 2 * rid, own_hw + 2 * j)
            slot = jnp.where(own, i, half + j)
            spots.append((slot, row, pair))
            zh = zh_ref[row].astype(F32)
            for p in range(2):
                hw = hw32[pl.ds(hw_at + p, 1), :]
                wz = wz_ref[pair, p * depth:(p + 1) * depth, :].astype(F32)
                parts.append(((hw + zh) + wz).astype(BF16))
        feats = jnp.concatenate(parts, axis=0)
        u = jnp.dot(feats, win_ref[...] * 0.5, preferred_element_type=F32) + bin_ref[...] * 0.5
        a = jnp.tanh(u) + 1.0
        h = u * a
        hid = h.astype(BF16)
        logits = dotg(wout_t[...], hid, ((1,), (1,)))
        dparts = []
        for g in range(GROUP):
            lt = logits[:, g * run:(g + 1) * run] + bcol
            top = jnp.max(lt, axis=0, keepdims=True)
            e = jnp.exp(lt - top)
            inv = GRAD_SCALE / jnp.sum(e, axis=0, keepdims=True)
            lab = labs[pl.ds(spots[g][0], 1), :]
            cls = lax.broadcasted_iota(jnp.int32, lt.shape, 0)
            hot = jnp.where(cls == lab, GRAD_SCALE, 0.0)
            dparts.append((e * inv - hot).astype(BF16))
        dlt = jnp.concatenate(dparts, axis=1)
        gwo_ref[...] += jnp.dot(dlt, hid, preferred_element_type=F32)
        tot = dparts[0].astype(F32)
        for g in range(1, GROUP):
            tot += dparts[g].astype(F32)
        gbo_ref[...] += tot
        dhh = dotg(dlt, wout_t[...] * 0.5, ((0,), (0,)))
        q = (u + u + 1.0) - h
        dpre = (dhh * a * q).astype(BF16)
        lhs = jnp.concatenate([feats.T, jnp.ones((16, samples), BF16)], axis=0)
        gwi_ref[...] += jnp.dot(lhs, dpre, preferred_element_type=F32)
        df = dotg(dpre, win_ref[...], ((1,), (1,)))
        for g in range(GROUP):
            slot, row, pair = spots[g]
            d = df[g * run:(g + 1) * run]
            zh_out[:, row] += (d[:depth] + d[depth:]).reshape(depth // 8, 8, chans)
            d0, d1 = d[:depth].reshape(depth // 8, 8, chans), d[depth:].reshape(depth // 8, 8, chans)
            wz_out[0, :, pair] += jnp.where(low, d0, pltpu.roll(d1, 4, 1))
            wz_out[1, :, pair] += jnp.where(low, pltpu.roll(d0, 4, 1), d1)
            for p in range(2):
                hw_out[pl.ds(2 * slot + p, 1), :] = jnp.sum(d[p * depth:(p + 1) * depth], axis=0, keepdims=True)
        return carry

    lax.fori_loop(0, half // GROUP, body, 0)
    top = chans + 16
    wt_out[0:top] = gwi_ref[:, :128]
    wt_out[top:2 * top] = gwi_ref[:, 128:]
    wt_out[2 * top:2 * top + CLS] = gwo_ref[:, :128]
    wt_out[2 * top + CLS:2 * top + 2 * CLS] = gwo_ref[:, 128:]
    wt_out[2 * top + 2 * CLS:] = gbo_ref[...]


def decode_runs(ids, idx, count, hw, hwx, zh, wz, labels, labx, w_in, b_in, w_out, b_out):
    rows, depth, chans = zh.shape
    pairs = wz.shape[0]
    hid, ncls = w_out.shape
    smem = pl.BlockSpec(memory_space=pltpu.SMEM)
    vmem = pl.BlockSpec(memory_space=pltpu.VMEM)
    return pl.pallas_call(
        decode_kernel,
        out_shape=(
            jax.ShapeDtypeStruct((2 * labels.shape[0], chans), F32),
            jax.ShapeDtypeStruct((depth // 8, rows, 8, chans), F32),
            jax.ShapeDtypeStruct((2, depth // 8, pairs, 8, chans), F32),
            jax.ShapeDtypeStruct((2 * (chans + 16) + 3 * CLS, chans), F32),
        ),
        in_specs=[smem] * 3 + [vmem] * 10,
        out_specs=[vmem] * 4,
        scratch_shapes=[
            pltpu.VMEM((hw.shape[0] + hwx.shape[0], chans), F32),
            pltpu.VMEM(labels.shape, jnp.int32),
            pltpu.VMEM((CLS, hid), F32),
            pltpu.VMEM((CLS, hid), BF16),
            pltpu.VMEM((chans + 16, hid), F32),
            pltpu.VMEM((CLS, hid), F32),
            pltpu.VMEM((CLS, 2 * depth), F32),
        ],
        compiler_params=pltpu.CompilerParams(vmem_limit_bytes=DECODE_VMEM),
    )(ids, idx, count, hw, hwx, zh, wz, labels, labx, w_in, b_in.reshape(1, hid), w_out, b_out.reshape(1, ncls))


def finish_kernel(
    ids_ref, count_ref, own_ref, back_ref, wz_ref, zh_ref, wt_ref,
    hw_out, wz_out, zh_out, gwi_out, gbi_out, gwo_out, gbo_out,
):
    cap = ids_ref.shape[1]
    half = cap // 2
    used = count_ref[0]
    chans = hw_out.shape[1]
    ncls = gwo_out.shape[1]
    hw_out[...] = jnp.zeros_like(hw_out)

    def put(source, start):
        def go(i, carry):
            for k in range(8):
                s = i * 8 + k
                at = 2 * ids_ref[0, start + s]
                for p in range(2):
                    hw_out[pl.ds(at + p, 1), :] = source[pl.ds(2 * s + p, 1), :]
            return carry
        return go

    lax.fori_loop(0, pl.cdiv(jnp.minimum(used, half), 8), put(own_ref, 0), 0)
    lax.fori_loop(0, pl.cdiv(jnp.maximum(used - half, 0), 8), put(back_ref, half), 0)
    wz_out[...] = wz_ref[...]
    for i in range(8):
        zh_out[i] = zh_ref[:, i, :]
    top = chans + 16
    gwi_out[:, :128] = wt_ref[:chans]
    gwi_out[:, 128:] = wt_ref[top:top + chans]
    gbi_out[:, :128] = wt_ref[chans:chans + 1]
    gbi_out[:, 128:] = wt_ref[top + chans:top + chans + 1]
    at = 2 * top
    gwo_out[:128] = wt_ref[at:at + CLS].T[:, :ncls]
    gwo_out[128:] = wt_ref[at + CLS:at + 2 * CLS].T[:, :ncls]
    gbo_out[...] = jnp.sum(wt_ref[at + 2 * CLS:at + 3 * CLS].T, axis=0, keepdims=True)[:, :ncls]


def finish(ids, count, own, back, wz, zh, wt, hw_rows, hid, ncls):
    smem = pl.BlockSpec(memory_space=pltpu.SMEM)
    vmem = pl.BlockSpec(memory_space=pltpu.VMEM)
    chans = own.shape[1]
    return pl.pallas_call(
        finish_kernel,
        out_shape=(
            jax.ShapeDtypeStruct((hw_rows, chans), F32),
            jax.ShapeDtypeStruct(wz.shape, F32),
            jax.ShapeDtypeStruct((8, zh.shape[0], chans), F32),
            jax.ShapeDtypeStruct((chans, hid), F32),
            jax.ShapeDtypeStruct((1, hid), F32),
            jax.ShapeDtypeStruct((hid, ncls), F32),
            jax.ShapeDtypeStruct((1, ncls), F32),
        ),
        in_specs=[smem] * 2 + [vmem] * 5,
        out_specs=[vmem] * 7,
        compiler_params=pltpu.CompilerParams(vmem_limit_bytes=32 * 1024 * 1024),
    )(ids, count, own, back, wz, zh, wt)


def pack(v):
    most = jnp.maximum(jnp.max(jnp.abs(v), axis=1, keepdims=True), 1e-30)
    return jnp.round(v * (32766.0 / most)).astype(jnp.int32).astype(jnp.int16), most * (1.0 / 32766.0)


def unpack(q, scale):
    return q.astype(jnp.int32).astype(F32) * scale


class Coded:
    def __init__(self, out, out_scale, into, into_scale, sems, to):
        self.out, self.out_scale, self.into, self.into_scale = out, out_scale, into, into_scale
        self.copies = [
            pltpu.make_async_remote_copy(
                src_ref=a, dst_ref=b, send_sem=sems.at[0, i], recv_sem=sems.at[1, i], device_id=to, device_id_type=MESH)
            for i, (a, b) in enumerate(((out, into), (out_scale, into_scale)))
        ]

    def send(self, v):
        self.out[...], self.out_scale[...] = pack(v)
        for cp in self.copies:
            cp.start()

    def receive(self):
        for cp in self.copies:
            cp.wait_recv()
        return unpack(self.into[...], self.into_scale[...])

    def done(self):
        for cp in self.copies:
            cp.wait_send()


def coded_buffers(n, groups, rows, chans):
    return [
        pltpu.VMEM((n, groups, rows, chans), jnp.int16), pltpu.VMEM((n, groups, 1, chans), F32),
        pltpu.VMEM((n, groups, rows, chans), jnp.int16), pltpu.VMEM((n, groups, 1, chans), F32),
        pltpu.SemaphoreType.DMA((n, 2, 2)),
    ]


def coded(bufs, i, to):
    out, out_scale, into, into_scale, sems = bufs
    return Coded(out.at[i], out_scale.at[i], into.at[i], into_scale.at[i], sems.at[i], to)


class Ring:
    def __init__(self, src, bufs, first, axis, me, span, at):
        self.src, self.me, self.span = src, me, span
        self.plus, self.minus, self.far = lax.rem(me + 1, 4), lax.rem(me + 3, 4), lax.rem(me + 2, 4)
        self.lo, self.hi = pl.ds(at, span // 2), pl.ds(at + span // 2, span // 2)
        to = [axis(self.plus), axis(self.minus)]
        self.msgs = [coded(bufs, first + i, to[d]) for i, d in enumerate((0, 1, 1, 0, 0, 1))]

    def part(self, where, half):
        v = self.src[:, where, half]
        return v.reshape(v.shape[0], -1, v.shape[-1])

    def begin(self):
        self.msgs[0].send(self.part(self.far, self.lo))
        self.msgs[1].send(self.part(self.far, self.hi))
        self.msgs[2].send(self.part(self.minus, self.lo))
        self.msgs[3].send(self.part(self.plus, self.hi))

    def relay(self):
        self.msgs[4].send(self.msgs[0].receive() + self.part(self.plus, self.lo))
        self.msgs[5].send(self.msgs[1].receive() + self.part(self.minus, self.hi))

    def finish(self):
        lo = self.part(self.me, self.lo) + self.msgs[2].receive() + self.msgs[4].receive()
        hi = self.part(self.me, self.hi) + self.msgs[3].receive() + self.msgs[5].receive()
        return lo, hi

    def done(self):
        for m in self.msgs:
            m.done()


def reduce_kernel(
    wz_ref, zh_ref, wt_ref, hw_ref, wz_out, zh_out, wt_out, hw_out,
    wz_own, core_in, xsum, zsum, wt_in, wt_mid,
    own_sem, core_sem, wa_sem, wb_sem, wc_sem, *bufs,
):
    xbufs, ybufs, zbufs, zybufs, hwbufs = (bufs[5 * i:5 * i + 5] for i in range(5))
    ha, wa = lax.axis_index("ha"), lax.axis_index("wa")
    yh, x, c = ha // 8, lax.rem(ha // 2, 4), lax.rem(ha, 2)
    yl, z = wa // 4, lax.rem(wa, 4)
    span = wz_ref.shape[3] // CHUNKS
    n_ha, n_wa = wt_ref.shape[0], 8

    def on_x(to):
        return (yh * 8 + to * 2 + c, wa)

    def on_z(to):
        return (ha, yl * 4 + to)

    sibling = (ha + 1 - 2 * c, wa)
    across = (lax.rem(ha + 8, 16), wa)
    beside = (ha, lax.rem(wa + 4, 8))
    corner = (lax.rem(ha + 8, 16), lax.rem(wa + 4, 8))
    rows_own = zh_ref.shape[2] // 2

    barrier = pltpu.get_barrier_semaphore()

    def greet_ha(i, carry):
        pl.semaphore_signal(barrier, inc=1, device_id=(lax.rem(ha + i, n_ha), wa), device_id_type=MESH)
        return carry

    def greet_wa(i, carry):
        pl.semaphore_signal(barrier, inc=1, device_id=(ha, lax.rem(wa + i, n_wa)), device_id_type=MESH)
        return carry

    load = pltpu.make_async_copy(wz_ref.at[c], wz_own, own_sem.at[0])
    load.start()
    lax.fori_loop(1, n_ha, greet_ha, 0)
    lax.fori_loop(1, n_wa, greet_wa, 0)
    pl.semaphore_signal(barrier, inc=1, device_id=corner, device_id_type=MESH)
    pl.semaphore_wait(barrier, n_ha + n_wa - 1)

    def send(source, dest, sems, to):
        return pltpu.make_async_remote_copy(
            src_ref=source, dst_ref=dest, send_sem=sems.at[0], recv_sem=sems.at[1],
            device_id=to, device_id_type=MESH)

    core = [
        send(wz_ref.at[1 - c, :, :, pl.ds(k * span, span)], core_in.at[:, :, pl.ds(k * span, span)],
             core_sem.at[k], sibling)
        for k in range(CHUNKS)
    ]
    for k in range(CHUNKS):
        core[k].start()
    zring = Ring(zh_ref, zbufs, 0, on_z, z, zh_ref.shape[2], 0)
    zring.begin()

    def wt_first(i):
        to = lax.rem(ha + i, n_ha)
        return pltpu.make_async_remote_copy(
            src_ref=wt_ref.at[to], dst_ref=wt_in.at[ha], send_sem=wa_sem.at[0, to], recv_sem=wa_sem.at[1, ha],
            device_id=(to, wa), device_id_type=MESH)

    def wt_second(i):
        to = lax.rem(wa + i, n_wa)
        return pltpu.make_async_remote_copy(
            src_ref=wt_mid.at[wa], dst_ref=wt_mid.at[wa], send_sem=wb_sem.at[0, to], recv_sem=wb_sem.at[1, wa],
            device_id=(ha, to), device_id_type=MESH)

    def wt_third(i):
        to = lax.rem(ha + i, n_ha)
        return pltpu.make_async_remote_copy(
            src_ref=wt_out.at[ha], dst_ref=wt_out.at[ha], send_sem=wc_sem.at[0, to], recv_sem=wc_sem.at[1, ha],
            device_id=(to, wa), device_id_type=MESH)

    def start(make, n):
        def go(i, carry):
            make(i).start()
            return carry
        lax.fori_loop(1, n, go, 0)

    def wait_send(make, n):
        def go(i, carry):
            make(i).wait_send()
            return carry
        lax.fori_loop(1, n, go, 0)

    def wait_slot(buf, sems, me, n, own):
        def go(i, carry):
            frm = lax.rem(me + i, n)
            pltpu.make_async_remote_copy(
                src_ref=buf.at[frm], dst_ref=buf.at[frm], send_sem=sems.at[0, frm], recv_sem=sems.at[1, frm],
                device_id=own, device_id_type=MESH).wait_recv()
            return carry
        lax.fori_loop(1, n, go, 0)

    start(wt_first, n_ha)
    chans = hw_ref.shape[1]
    back = coded(hwbufs, 0, across)
    back.send(hw_ref[hw_out.shape[0]:].reshape(-1, 128, chans))
    load.wait()
    rings = []
    for k in range(CHUNKS):
        rows = pl.ds(k * span, span)
        core[k].wait_recv()
        core_in[:, :, rows] += wz_own[:, :, rows]
        rings.append(Ring(core_in, xbufs, 6 * k, on_x, x, span, k * span))
        rings[k].begin()
    zring.relay()
    wait_slot(wt_in, wa_sem, ha, n_ha, sibling)
    wt_in[ha] = wt_ref[ha]
    tot = wt_in[0]
    for i in range(1, n_ha):
        tot += wt_in[i]
    wt_mid[wa] = tot
    start(wt_second, n_wa)
    for k in range(CHUNKS):
        rings[k].relay()
    wait_slot(wt_mid, wb_sem, wa, n_wa, beside)
    tot = wt_mid[0]
    for i in range(1, n_wa):
        tot += wt_mid[i]
    wt_out[ha] = tot
    start(wt_third, n_ha)
    zsum[0], zsum[1] = zring.finish()
    zys = [coded(zybufs, i, to) for i, to in enumerate((beside, corner, across))]
    zys[0].send(zsum[0, pl.ds(1 - yl, 1)])
    zys[1].send(zsum[1, pl.ds(1 - yl, 1)])
    zys[2].send(zsum[1, pl.ds(yl, 1)])
    ys = []
    for k in range(CHUNKS):
        rows = pl.ds(k * span, span)
        lo, hi = rings[k].finish()
        xsum[:, k, 0:span * 4], xsum[:, k, span * 4:] = lo, hi
        ys.append(coded(ybufs, k, across))
        ys[k].send(xsum[pl.ds(1 - yh, 1), k])
    total = zsum[0, pl.ds(yl, 1)]
    for m in zys:
        total += m.receive()
    zh_out[...] = total.reshape(zh_out.shape)
    for k in range(CHUNKS):
        rows = pl.ds(k * span, span)
        wz_out[pl.ds(k * span, span)] = (xsum[pl.ds(yh, 1), k] + ys[k].receive()).reshape(span, 8, chans)
    hw_out[...] = back.receive().reshape(hw_out.shape)
    wait_slot(wt_out, wc_sem, ha, n_ha, sibling)
    for k in range(CHUNKS):
        core[k].wait_send()
        rings[k].done()
        ys[k].done()
    zring.done()
    for m in zys + [back]:
        m.done()
    wait_send(wt_first, n_ha)
    wait_send(wt_second, n_wa)
    wait_send(wt_third, n_ha)


def reduce_all(wz, zh, wt, hw):
    half_w, chans = wz.shape[3], wz.shape[5]
    rows = zh.shape[2]
    span = half_w // CHUNKS
    vmem = pl.BlockSpec(memory_space=pltpu.VMEM)
    buf = lambda *s: pltpu.VMEM(s, F32)
    dma = lambda *s: pltpu.SemaphoreType.DMA(s)
    return pl.pallas_call(
        reduce_kernel,
        out_shape=(
            jax.ShapeDtypeStruct((half_w, 8, chans), F32),
            jax.ShapeDtypeStruct((rows // 2, 8, chans), F32),
            jax.ShapeDtypeStruct(wt.shape, F32),
            jax.ShapeDtypeStruct((hw.shape[0] // 2, chans), F32),
        ),
        in_specs=[pl.BlockSpec(memory_space=pl.ANY)] + [vmem] * 3,
        out_specs=[vmem] * 4,
        scratch_shapes=[
            buf(2, 4, half_w, 8, chans),
            buf(2, 4, half_w, 8, chans),
            buf(2, CHUNKS, span * 8, chans),
            buf(2, 2, rows * 4, chans),
            buf(*wt.shape),
            buf(8, *wt.shape[1:]),
            dma(1), dma(CHUNKS, 2), dma(2, 16), dma(2, 8), dma(2, 16),
            *coded_buffers(6 * CHUNKS, 2, span * 4, chans),
            *coded_buffers(CHUNKS, 1, span * 8, chans),
            *coded_buffers(6, 2, rows * 4, chans),
            *coded_buffers(3, 1, rows * 4, chans),
            *coded_buffers(1, hw.shape[0] // 256, 128, chans),
        ],
        compiler_params=pltpu.CompilerParams(
            collective_id=0, has_side_effects=True, vmem_limit_bytes=REDUCE_VMEM),
    )(wz, zh, wt, hw)


def local(hw_plane, zh_plane, wz_plane, w_in, b_in, w_out, b_out, run_index, run_count, labels):
    rows, cols, chans = hw_plane.shape
    depth = zh_plane.shape[0]
    ncls = w_out.shape[1]
    hw_rows = hw_plane.reshape(rows * cols, chans)
    idx, hwx, zh2, labx = exchange(run_index, hw_rows, zh_plane, labels[0])
    hw, zh, wz, wt = decode_runs(
        run_index, idx, run_count, hw_rows, hwx, zh2, wz_plane.reshape(cols // 2, 2 * depth, chans),
        labels[0], labx, w_in, b_in, w_out, b_out,
    )
    wz_grad, zh_grad, wt, back = reduce_all(
        wz.reshape(2, 2, 4, cols // 2, 8, chans), zh.reshape(2, 4, 2 * rows, 8, chans), wt.reshape(16, -1, chans), hw)
    hw_grad, wz_grad, zh_grad, gwi, gbi, gwo, gbo = finish(
        run_index, run_count, hw, back, wz_grad, zh_grad, wt.reshape(-1, chans), rows * cols, w_out.shape[0], ncls)
    return (hw_grad.reshape(rows, cols, chans), zh_grad, wz_grad.reshape(cols, 4, chans), gwi, gbi[0], gwo, gbo[0])


def solution(mesh):
    placed = (
        P("ha", "wa", None),
        P(None, "ha", None),
        P("wa", None, None),
        P(),
        P(),
        P(),
        P(),
        P(("ha", "wa"), None),
        P(("ha", "wa")),
        P(("ha", "wa"), None, None),
    )
    return jax.shard_map(
        local,
        mesh=mesh,
        in_specs=placed,
        out_specs=(P("ha", "wa", None), P("wa", "ha", None), P("wa", "ha", None), P(), P(), P(), P()),
        check_vma=False,
    )
```

```python
import functools

import jax
import jax.numpy as jnp
from jax import lax
from jax.experimental import pallas as pl
from jax.experimental.pallas import tpu as pltpu
from jax.sharding import PartitionSpec as P

F32 = jnp.float32
BF16 = jnp.bfloat16
GRAD_SCALE = 0.25
GROUP = 32
CLS = 32
CHUNKS = 2
EXCHANGE_VMEM = 58 * 1024 * 1024
FINISH_VMEM = 58 * 1024 * 1024
DECODE_VMEM = 58 * 1024 * 1024
REDUCE_VMEM = 58 * 1024 * 1024
MESH = pl.DeviceIdType.MESH


def dotg(left, right, dims):
    return lax.dot_general(left, right, ((dims[0], dims[1]), ((), ())), preferred_element_type=F32)


def exchange_kernel(
    ids_ref, idrow_ref, hw_ref, zh_ref, labels_ref,
    ids_out, hw_out, zh_out, lab_out,
    hwv, zhv, labv, hw32, zh32, rows32, rows16, lab16, load_sem, sem, z_sem,
):
    ha, wa = lax.axis_index("ha"), lax.axis_index("wa")
    z, base = lax.rem(wa, 4), wa - lax.rem(wa, 4)
    half = lab16.shape[0]
    own_rows = zh_ref.shape[1]
    part = own_rows // 4
    across = (lax.rem(ha + 8, 16), wa)
    corner = (lax.rem(ha + 8, 16), lax.rem(wa + 4, 8))
    ring = [(ha, base + lax.rem(z + k, 4)) for k in (1, 3, 2)]
    loads = [
        pltpu.make_async_copy(zh_ref, zhv, load_sem.at[0]),
        pltpu.make_async_copy(hw_ref, hwv, load_sem.at[1]),
        pltpu.make_async_copy(labels_ref.at[pl.ds(half, half)], labv, load_sem.at[2]),
    ]
    for cp in loads:
        cp.start()
    barrier = pltpu.get_barrier_semaphore()
    for to in [across, corner] + ring:
        pl.semaphore_signal(barrier, inc=1, device_id=to, device_id_type=MESH)

    def send(source, dest, sems, to):
        return pltpu.make_async_remote_copy(
            src_ref=source, dst_ref=dest, send_sem=sems.at[0], recv_sem=sems.at[1],
            device_id=to, device_id_type=MESH)

    def turn(q):
        at = pl.multiple_of(q * part, part)
        zh_out[pl.ds(at, part)] = jnp.swapaxes(zh32[:, pl.ds(at, part), :], 0, 1).astype(BF16)

    loads[0].wait()
    zh32[...] = zhv[...].astype(F32)
    turn(z)
    pl.semaphore_wait(barrier, 5)
    got = own_rows + z * part
    fetch = send(zh_out.at[pl.ds(z * part, part)], zh_out.at[pl.ds(got, part)], z_sem.at[0], corner)
    fetch.start()
    for k in (1, 2, 3):
        turn(lax.rem(z + k, 4))
    loads[2].wait()
    lab16[...] = labv[...].astype(F32).astype(BF16)
    loads[1].wait()
    hw32[...] = hwv[...].astype(F32)

    def pick(i, carry):
        for k in range(8):
            s = i * 8 + k
            at = 2 * ids_ref[0, half + s]
            for p in range(2):
                rows32[pl.ds(2 * s + p, 1), :] = hw32[pl.ds(at + p, 1), :]
        return carry

    lax.fori_loop(0, half // 8, pick, 0)
    rows16[...] = rows32[...].astype(BF16)
    fetch.wait_recv()
    mine = zh_out.at[pl.ds(got, part)]
    outs = [send(mine, mine, z_sem.at[1 + k], to) for k, to in enumerate(ring)]
    outs += [send(rows16, hw_out, sem.at[0], across), send(lab16, lab_out, sem.at[1], across),
             send(idrow_ref, ids_out, sem.at[2], across)]
    for cp in outs:
        cp.start()
    for cp in outs:
        cp.wait()
    fetch.wait_send()


def exchange(ids, hw, zh, labels):
    vmem = pl.BlockSpec(memory_space=pltpu.VMEM)
    hbm = pl.BlockSpec(memory_space=pl.ANY)
    half = labels.shape[0] // 2
    depth, rows, chans = zh.shape
    dma = lambda *s: pltpu.SemaphoreType.DMA(s)
    return pl.pallas_call(
        exchange_kernel,
        out_shape=(
            jax.ShapeDtypeStruct(ids.shape, jnp.int32),
            jax.ShapeDtypeStruct((2 * half, chans), BF16),
            jax.ShapeDtypeStruct((2 * rows, depth, chans), BF16),
            jax.ShapeDtypeStruct((half, labels.shape[1]), BF16),
        ),
        in_specs=[pl.BlockSpec(memory_space=pltpu.SMEM), vmem, hbm, hbm, hbm],
        out_specs=[vmem] * 4,
        scratch_shapes=[
            pltpu.VMEM(hw.shape, BF16), pltpu.VMEM(zh.shape, BF16), pltpu.VMEM((half, labels.shape[1]), jnp.int32),
            pltpu.VMEM(hw.shape, F32), pltpu.VMEM(zh.shape, F32), pltpu.VMEM((2 * half, chans), F32),
            pltpu.VMEM((2 * half, chans), BF16), pltpu.VMEM((half, labels.shape[1]), BF16),
            dma(3), dma(3, 2), dma(4, 2),
        ],
        compiler_params=pltpu.CompilerParams(
            collective_id=1, has_side_effects=True, vmem_limit_bytes=EXCHANGE_VMEM),
    )(ids, ids, hw, zh, labels)


def decode_kernel(
    ids_ref, idx_ref, count_ref, hw_ref, hwx_ref, zh_ref, wz_ref, labels_ref, labx_ref, win_ref, bin_ref, wout_ref, bout_ref,
    hw_out, zh_out, wz_out, wt_out,
    hw32, labs, wpad, wout_t, gwi_ref, gwo_ref, gbo_ref,
):
    rows, depth, chans = zh_ref.shape
    pairs = wz_ref.shape[0]
    half = labx_ref.shape[0]
    own_hw = hw_ref.shape[0]
    own_n = jnp.minimum(count_ref[0], half)
    hw32[:own_hw] = hw_ref[...].astype(F32)
    hw32[own_hw:] = hwx_ref[...].astype(F32)
    labs[:half] = labels_ref[:half]
    labs[half:] = labx_ref[...].astype(F32).astype(jnp.int32)
    hw_out[...] = jnp.zeros_like(hw_out)
    zh_out[...] = jnp.zeros_like(zh_out)
    wz_out[...] = jnp.zeros_like(wz_out)
    gwi_ref[...] = jnp.zeros_like(gwi_ref)
    gwo_ref[...] = jnp.zeros_like(gwo_ref)
    gbo_ref[...] = jnp.zeros_like(gbo_ref)
    ncls = wout_ref.shape[0]
    wpad[...] = jnp.zeros_like(wpad)
    wpad[:ncls] = wout_ref[...].astype(F32)
    wout_t[...] = wpad[...].astype(BF16)
    at_row = lax.broadcasted_iota(jnp.int32, (CLS, ncls), 0)
    at_col = lax.broadcasted_iota(jnp.int32, (CLS, ncls), 1)
    bcol = jnp.sum(jnp.where(at_row == at_col, bout_ref[...], 0.0), axis=1, keepdims=True)
    bcol = jnp.where(lax.broadcasted_iota(jnp.int32, (CLS, 1), 0) < ncls, bcol, -1e30)
    samples = GROUP * 2 * depth
    low = lax.broadcasted_iota(jnp.int32, (depth // 8, 8, chans), 1) < 4
    run = 2 * depth

    def body(step, carry):
        base = step * GROUP
        spots = []
        parts = []
        for g in range(GROUP):
            i = base + g
            own = i < own_n
            j = jnp.maximum(i - own_n, 0)
            rid = jnp.where(own, ids_ref[0, i], idx_ref[0, half + j])
            row = rid // pairs + jnp.where(own, 0, rows // 2)
            pair = rid % pairs
            hw_at = jnp.where(own, 2 * rid, own_hw + 2 * j)
            slot = jnp.where(own, i, half + j)
            spots.append((slot, row, pair))
            zh = zh_ref[row].astype(F32)
            for p in range(2):
                hw = hw32[pl.ds(hw_at + p, 1), :]
                wz = wz_ref[pair, p * depth:(p + 1) * depth, :].astype(F32)
                parts.append(((hw + zh) + wz).astype(BF16))
        feats = jnp.concatenate(parts, axis=0)
        u = jnp.dot(feats, win_ref[...] * 0.5, preferred_element_type=F32) + bin_ref[...] * 0.5
        a = jnp.tanh(u) + 1.0
        h = u * a
        hid = h.astype(BF16)
        logits = dotg(wout_t[...], hid, ((1,), (1,)))
        dparts = []
        for g in range(GROUP):
            lt = logits[:, g * run:(g + 1) * run] + bcol
            top = jnp.max(lt, axis=0, keepdims=True)
            e = jnp.exp(lt - top)
            inv = GRAD_SCALE / jnp.sum(e, axis=0, keepdims=True)
            lab = labs[pl.ds(spots[g][0], 1), :]
            cls = lax.broadcasted_iota(jnp.int32, lt.shape, 0)
            hot = jnp.where(cls == lab, GRAD_SCALE, 0.0)
            dparts.append((e * inv - hot).astype(BF16))
        dlt = jnp.concatenate(dparts, axis=1)
        gwo_ref[...] += jnp.dot(dlt, hid, preferred_element_type=F32)
        tot = dparts[0].astype(F32)
        for g in range(1, GROUP):
            tot += dparts[g].astype(F32)
        gbo_ref[...] += tot
        dhh = dotg(dlt, wout_t[...] * 0.5, ((0,), (0,)))
        q = (u + u + 1.0) - h
        dpre = (dhh * a * q).astype(BF16)
        lhs = jnp.concatenate([feats.T, jnp.ones((16, samples), BF16)], axis=0)
        gwi_ref[...] += jnp.dot(lhs, dpre, preferred_element_type=F32)
        df = dotg(dpre, win_ref[...], ((1,), (1,)))
        for g in range(GROUP):
            slot, row, pair = spots[g]
            d = df[g * run:(g + 1) * run]
            zh_out[:, row] += (d[:depth] + d[depth:]).reshape(depth // 8, 8, chans)
            d0, d1 = d[:depth].reshape(depth // 8, 8, chans), d[depth:].reshape(depth // 8, 8, chans)
            wz_out[0, :, pair] += jnp.where(low, d0, pltpu.roll(d1, 4, 1))
            wz_out[1, :, pair] += jnp.where(low, pltpu.roll(d0, 4, 1), d1)
            for p in range(2):
                hw_out[pl.ds(2 * slot + p, 1), :] = jnp.sum(d[p * depth:(p + 1) * depth], axis=0, keepdims=True)
        return carry

    lax.fori_loop(0, half // GROUP, body, 0)
    top = chans + 16
    wt_out[0:top] = gwi_ref[:, :128]
    wt_out[top:2 * top] = gwi_ref[:, 128:]
    wt_out[2 * top:2 * top + CLS] = gwo_ref[:, :128]
    wt_out[2 * top + CLS:2 * top + 2 * CLS] = gwo_ref[:, 128:]
    wt_out[2 * top + 2 * CLS:] = gbo_ref[...]


def decode_runs(ids, idx, count, hw, hwx, zh, wz, labels, labx, w_in, b_in, w_out, b_out):
    rows, depth, chans = zh.shape
    pairs = wz.shape[0]
    hid, ncls = w_out.shape
    smem = pl.BlockSpec(memory_space=pltpu.SMEM)
    vmem = pl.BlockSpec(memory_space=pltpu.VMEM)
    return pl.pallas_call(
        decode_kernel,
        out_shape=(
            jax.ShapeDtypeStruct((2 * labels.shape[0], chans), F32),
            jax.ShapeDtypeStruct((depth // 8, rows, 8, chans), F32),
            jax.ShapeDtypeStruct((2, depth // 8, pairs, 8, chans), F32),
            jax.ShapeDtypeStruct((2 * (chans + 16) + 3 * CLS, chans), F32),
        ),
        in_specs=[smem] * 3 + [vmem] * 10,
        out_specs=[vmem] * 4,
        scratch_shapes=[
            pltpu.VMEM((hw.shape[0] + hwx.shape[0], chans), F32),
            pltpu.VMEM(labels.shape, jnp.int32),
            pltpu.VMEM((CLS, hid), F32),
            pltpu.VMEM((CLS, hid), BF16),
            pltpu.VMEM((chans + 16, hid), F32),
            pltpu.VMEM((CLS, hid), F32),
            pltpu.VMEM((CLS, 2 * depth), F32),
        ],
        compiler_params=pltpu.CompilerParams(vmem_limit_bytes=DECODE_VMEM),
    )(ids, idx, count, hw, hwx, zh, wz, labels, labx, w_in, b_in.reshape(1, hid), w_out.T, b_out.reshape(1, ncls))


def finish_kernel(
    ids_ref, count_ref, own_ref, back_ref, wz_ref, zh_ref, wt_ref,
    hw_out, wz_out, zh_out, gwi_out, gbi_out, gwo_out, gbo_out,
):
    cap = ids_ref.shape[1]
    half = cap // 2
    used = count_ref[0]
    chans = hw_out.shape[1]
    ncls = gwo_out.shape[0]
    hw_out[...] = jnp.zeros_like(hw_out)

    def put(source, start):
        def go(i, carry):
            for k in range(8):
                s = i * 8 + k
                at = 2 * ids_ref[0, start + s]
                for p in range(2):
                    hw_out[pl.ds(at + p, 1), :] = source[pl.ds(2 * s + p, 1), :]
            return carry
        return go

    lax.fori_loop(0, pl.cdiv(jnp.minimum(used, half), 8), put(own_ref, 0), 0)
    lax.fori_loop(0, pl.cdiv(jnp.maximum(used - half, 0), 8), put(back_ref, half), 0)
    wz_out[...] = wz_ref[...]
    for i in range(8):
        zh_out[i] = zh_ref[:, i, :]
    top = chans + 16
    gwi_out[:, :128] = wt_ref[:chans]
    gwi_out[:, 128:] = wt_ref[top:top + chans]
    gbi_out[:, :128] = wt_ref[chans:chans + 1]
    gbi_out[:, 128:] = wt_ref[top + chans:top + chans + 1]
    at = 2 * top
    gwo_out[:, :128] = wt_ref[at:at + ncls]
    gwo_out[:, 128:] = wt_ref[at + CLS:at + CLS + ncls]
    gbo_out[...] = jnp.sum(wt_ref[at + 2 * CLS:at + 3 * CLS].T, axis=0, keepdims=True)[:, :ncls]


def finish(ids, count, own, back, wz, zh, wt, hw_rows, hid, ncls):
    smem = pl.BlockSpec(memory_space=pltpu.SMEM)
    vmem = pl.BlockSpec(memory_space=pltpu.VMEM)
    chans = own.shape[1]
    return pl.pallas_call(
        finish_kernel,
        out_shape=(
            jax.ShapeDtypeStruct((hw_rows, chans), F32),
            jax.ShapeDtypeStruct(wz.shape, F32),
            jax.ShapeDtypeStruct((8, zh.shape[0], chans), F32),
            jax.ShapeDtypeStruct((chans, hid), F32),
            jax.ShapeDtypeStruct((1, hid), F32),
            jax.ShapeDtypeStruct((ncls, hid), F32),
            jax.ShapeDtypeStruct((1, ncls), F32),
        ),
        in_specs=[smem] * 2 + [vmem] * 5,
        out_specs=[vmem] * 7,
        compiler_params=pltpu.CompilerParams(vmem_limit_bytes=FINISH_VMEM),
    )(ids, count, own, back, wz, zh, wt)


def pack(v):
    most = jnp.maximum(jnp.max(jnp.abs(v), axis=1, keepdims=True), 1e-30)
    return jnp.round(v * (32766.0 / most)).astype(jnp.int32).astype(jnp.int16), most * (1.0 / 32766.0)


def unpack(q, scale):
    return q.astype(jnp.int32).astype(F32) * scale


class Coded:
    def __init__(self, out, out_scale, into, into_scale, sems, to):
        self.out, self.out_scale, self.into, self.into_scale = out, out_scale, into, into_scale
        self.copies = [
            pltpu.make_async_remote_copy(
                src_ref=a, dst_ref=b, send_sem=sems.at[0, i], recv_sem=sems.at[1, i], device_id=to, device_id_type=MESH)
            for i, (a, b) in enumerate(((out, into), (out_scale, into_scale)))
        ]

    def send(self, v):
        self.out[...], self.out_scale[...] = pack(v)
        for cp in self.copies:
            cp.start()

    def receive(self):
        for cp in self.copies:
            cp.wait_recv()
        return unpack(self.into[...], self.into_scale[...])

    def done(self):
        for cp in self.copies:
            cp.wait_send()


def coded_buffers(n, groups, rows, chans):
    return [
        pltpu.VMEM((n, groups, rows, chans), jnp.int16), pltpu.VMEM((n, groups, 1, chans), F32),
        pltpu.VMEM((n, groups, rows, chans), jnp.int16), pltpu.VMEM((n, groups, 1, chans), F32),
        pltpu.SemaphoreType.DMA((n, 2, 2)),
    ]


def coded(bufs, i, to):
    out, out_scale, into, into_scale, sems = bufs
    return Coded(out.at[i], out_scale.at[i], into.at[i], into_scale.at[i], sems.at[i], to)


class Ring:
    def __init__(self, src, bufs, first, axis, me, span, at):
        self.src, self.me, self.span = src, me, span
        self.plus, self.minus, self.far = lax.rem(me + 1, 4), lax.rem(me + 3, 4), lax.rem(me + 2, 4)
        self.lo, self.hi = pl.ds(at, span // 2), pl.ds(at + span // 2, span // 2)
        to = [axis(self.plus), axis(self.minus)]
        self.msgs = [coded(bufs, first + i, to[d]) for i, d in enumerate((0, 1, 1, 0, 0, 1))]

    def part(self, where, half):
        v = self.src[:, where, half]
        return v.reshape(v.shape[0], -1, v.shape[-1])

    def begin(self):
        self.msgs[0].send(self.part(self.far, self.lo))
        self.msgs[1].send(self.part(self.far, self.hi))
        self.msgs[2].send(self.part(self.minus, self.lo))
        self.msgs[3].send(self.part(self.plus, self.hi))

    def relay(self):
        self.msgs[4].send(self.msgs[0].receive() + self.part(self.plus, self.lo))
        self.msgs[5].send(self.msgs[1].receive() + self.part(self.minus, self.hi))

    def finish(self):
        lo = self.part(self.me, self.lo) + self.msgs[2].receive() + self.msgs[4].receive()
        hi = self.part(self.me, self.hi) + self.msgs[3].receive() + self.msgs[5].receive()
        return lo, hi

    def done(self):
        for m in self.msgs:
            m.done()


def reduce_kernel(
    wz_ref, zh_hbm, wt_ref, hw_hbm, wz_out, zh_out, wt_out, hw_out,
    wz_own, zh_ref, hw_ref, core_in, xsum, zsum, wt_in, wt_mid,
    own_sem, core_sem, wa_sem, wb_sem, wc_sem, *bufs,
):
    xbufs, ybufs, zbufs, zybufs, hwbufs = (bufs[5 * i:5 * i + 5] for i in range(5))
    ha, wa = lax.axis_index("ha"), lax.axis_index("wa")
    yh, x, c = ha // 8, lax.rem(ha // 2, 4), lax.rem(ha, 2)
    yl, z = wa // 4, lax.rem(wa, 4)
    span = wz_ref.shape[3] // CHUNKS
    n_ha, n_wa = wt_ref.shape[0], 8

    def on_x(to):
        return (yh * 8 + to * 2 + c, wa)

    def on_z(to):
        return (ha, yl * 4 + to)

    sibling = (ha + 1 - 2 * c, wa)
    across = (lax.rem(ha + 8, 16), wa)
    beside = (ha, lax.rem(wa + 4, 8))
    corner = (lax.rem(ha + 8, 16), lax.rem(wa + 4, 8))
    rows_own = zh_ref.shape[2] // 2

    barrier = pltpu.get_barrier_semaphore()

    def greet_ha(i, carry):
        pl.semaphore_signal(barrier, inc=1, device_id=(lax.rem(ha + i, n_ha), wa), device_id_type=MESH)
        return carry

    def greet_wa(i, carry):
        pl.semaphore_signal(barrier, inc=1, device_id=(ha, lax.rem(wa + i, n_wa)), device_id_type=MESH)
        return carry

    loads = [
        pltpu.make_async_copy(zh_hbm, zh_ref, own_sem.at[0]),
        pltpu.make_async_copy(hw_hbm.at[pl.ds(hw_out.shape[0], hw_out.shape[0])], hw_ref, own_sem.at[1]),
        pltpu.make_async_copy(wz_ref.at[c], wz_own, own_sem.at[2]),
    ]
    for cp in loads:
        cp.start()
    lax.fori_loop(1, n_ha, greet_ha, 0)
    lax.fori_loop(1, n_wa, greet_wa, 0)
    pl.semaphore_signal(barrier, inc=1, device_id=corner, device_id_type=MESH)
    pl.semaphore_wait(barrier, n_ha + n_wa - 1)

    def send(source, dest, sems, to):
        return pltpu.make_async_remote_copy(
            src_ref=source, dst_ref=dest, send_sem=sems.at[0], recv_sem=sems.at[1],
            device_id=to, device_id_type=MESH)

    core = [
        send(wz_ref.at[1 - c, :, :, pl.ds(k * span, span)], core_in.at[:, :, pl.ds(k * span, span)],
             core_sem.at[k], sibling)
        for k in range(CHUNKS)
    ]
    for k in range(CHUNKS):
        core[k].start()
    zring = Ring(zh_ref, zbufs, 0, on_z, z, zh_ref.shape[2], 0)
    loads[0].wait()
    zring.begin()

    def wt_first(i):
        to = lax.rem(ha + i, n_ha)
        return pltpu.make_async_remote_copy(
            src_ref=wt_ref.at[to], dst_ref=wt_in.at[ha], send_sem=wa_sem.at[0, to], recv_sem=wa_sem.at[1, ha],
            device_id=(to, wa), device_id_type=MESH)

    def wt_second(i):
        to = lax.rem(wa + i, n_wa)
        return pltpu.make_async_remote_copy(
            src_ref=wt_mid.at[wa], dst_ref=wt_mid.at[wa], send_sem=wb_sem.at[0, to], recv_sem=wb_sem.at[1, wa],
            device_id=(ha, to), device_id_type=MESH)

    def wt_third(i):
        to = lax.rem(ha + i, n_ha)
        return pltpu.make_async_remote_copy(
            src_ref=wt_out.at[ha], dst_ref=wt_out.at[ha], send_sem=wc_sem.at[0, to], recv_sem=wc_sem.at[1, ha],
            device_id=(to, wa), device_id_type=MESH)

    def start(make, n):
        def go(i, carry):
            make(i).start()
            return carry
        lax.fori_loop(1, n, go, 0)

    def wait_send(make, n):
        def go(i, carry):
            make(i).wait_send()
            return carry
        lax.fori_loop(1, n, go, 0)

    def wait_slot(buf, sems, me, n, own):
        def go(i, carry):
            frm = lax.rem(me + i, n)
            pltpu.make_async_remote_copy(
                src_ref=buf.at[frm], dst_ref=buf.at[frm], send_sem=sems.at[0, frm], recv_sem=sems.at[1, frm],
                device_id=own, device_id_type=MESH).wait_recv()
            return carry
        lax.fori_loop(1, n, go, 0)

    start(wt_first, n_ha)
    chans = hw_ref.shape[1]
    back = coded(hwbufs, 0, across)
    loads[1].wait()
    back.send(hw_ref[...].reshape(-1, 128, chans))
    loads[2].wait()
    rings = []
    for k in range(CHUNKS):
        rows = pl.ds(k * span, span)
        core[k].wait_recv()
        core_in[:, :, rows] += wz_own[:, :, rows]
        rings.append(Ring(core_in, xbufs, 6 * k, on_x, x, span, k * span))
        rings[k].begin()
    zring.relay()
    wait_slot(wt_in, wa_sem, ha, n_ha, sibling)
    wt_in[ha] = wt_ref[ha]
    tot = wt_in[0]
    for i in range(1, n_ha):
        tot += wt_in[i]
    wt_mid[wa] = tot
    start(wt_second, n_wa)
    for k in range(CHUNKS):
        rings[k].relay()
    wait_slot(wt_mid, wb_sem, wa, n_wa, beside)
    tot = wt_mid[0]
    for i in range(1, n_wa):
        tot += wt_mid[i]
    wt_out[ha] = tot
    start(wt_third, n_ha)
    zsum[0], zsum[1] = zring.finish()
    zys = [coded(zybufs, i, to) for i, to in enumerate((beside, corner, across))]
    zys[0].send(zsum[0, pl.ds(1 - yl, 1)])
    zys[1].send(zsum[1, pl.ds(1 - yl, 1)])
    zys[2].send(zsum[1, pl.ds(yl, 1)])
    ys = []
    for k in range(CHUNKS):
        rows = pl.ds(k * span, span)
        lo, hi = rings[k].finish()
        xsum[:, k, 0:span * 4], xsum[:, k, span * 4:] = lo, hi
        ys.append(coded(ybufs, k, across))
        ys[k].send(xsum[pl.ds(1 - yh, 1), k])
    total = zsum[0, pl.ds(yl, 1)]
    for m in zys:
        total += m.receive()
    zh_out[...] = total.reshape(zh_out.shape)
    for k in range(CHUNKS):
        rows = pl.ds(k * span, span)
        wz_out[pl.ds(k * span, span)] = (xsum[pl.ds(yh, 1), k] + ys[k].receive()).reshape(span, 8, chans)
    hw_out[...] = back.receive().reshape(hw_out.shape)
    wait_slot(wt_out, wc_sem, ha, n_ha, sibling)
    for k in range(CHUNKS):
        core[k].wait_send()
        rings[k].done()
        ys[k].done()
    zring.done()
    for m in zys + [back]:
        m.done()
    wait_send(wt_first, n_ha)
    wait_send(wt_second, n_wa)
    wait_send(wt_third, n_ha)


def reduce_all(wz, zh, wt, hw):
    half_w, chans = wz.shape[3], wz.shape[5]
    rows = zh.shape[2]
    span = half_w // CHUNKS
    vmem = pl.BlockSpec(memory_space=pltpu.VMEM)
    hbm = pl.BlockSpec(memory_space=pl.ANY)
    buf = lambda *s: pltpu.VMEM(s, F32)
    dma = lambda *s: pltpu.SemaphoreType.DMA(s)
    return pl.pallas_call(
        reduce_kernel,
        out_shape=(
            jax.ShapeDtypeStruct((half_w, 8, chans), F32),
            jax.ShapeDtypeStruct((rows // 2, 8, chans), F32),
            jax.ShapeDtypeStruct(wt.shape, F32),
            jax.ShapeDtypeStruct((hw.shape[0] // 2, chans), F32),
        ),
        in_specs=[hbm, hbm, vmem, hbm],
        out_specs=[vmem] * 4,
        scratch_shapes=[
            buf(2, 4, half_w, 8, chans),
            buf(*zh.shape),
            buf(hw.shape[0] // 2, chans),
            buf(2, 4, half_w, 8, chans),
            buf(2, CHUNKS, span * 8, chans),
            buf(2, 2, rows * 4, chans),
            buf(*wt.shape),
            buf(8, *wt.shape[1:]),
            dma(3), dma(CHUNKS, 2), dma(2, 16), dma(2, 8), dma(2, 16),
            *coded_buffers(6 * CHUNKS, 2, span * 4, chans),
            *coded_buffers(CHUNKS, 1, span * 8, chans),
            *coded_buffers(6, 2, rows * 4, chans),
            *coded_buffers(3, 1, rows * 4, chans),
            *coded_buffers(1, hw.shape[0] // 256, 128, chans),
        ],
        compiler_params=pltpu.CompilerParams(
            collective_id=0, has_side_effects=True, vmem_limit_bytes=REDUCE_VMEM),
    )(wz, zh, wt, hw)


def local(hw_plane, zh_plane, wz_plane, w_in, b_in, w_out, b_out, run_index, run_count, labels):
    rows, cols, chans = hw_plane.shape
    depth = zh_plane.shape[0]
    ncls = w_out.shape[1]
    hw_rows = hw_plane.reshape(rows * cols, chans)
    idx, hwx, zh2, labx = exchange(run_index, hw_rows, zh_plane, labels[0])
    hw, zh, wz, wt = decode_runs(
        run_index, idx, run_count, hw_rows, hwx, zh2, wz_plane.reshape(cols // 2, 2 * depth, chans),
        labels[0], labx, w_in, b_in, w_out, b_out,
    )
    wz_grad, zh_grad, wt, back = reduce_all(
        wz.reshape(2, 2, 4, cols // 2, 8, chans), zh.reshape(2, 4, 2 * rows, 8, chans), wt.reshape(16, -1, chans), hw)
    hw_grad, wz_grad, zh_grad, gwi, gbi, gwo, gbo = finish(
        run_index, run_count, hw, back, wz_grad, zh_grad, wt.reshape(-1, chans), rows * cols, w_out.shape[0], ncls)
    return (hw_grad.reshape(rows, cols, chans), zh_grad, wz_grad.reshape(cols, 4, chans), gwi, gbi[0], gwo.T, gbo[0])


def solution(mesh):
    placed = (
        P("ha", "wa", None),
        P(None, "ha", None),
        P("wa", None, None),
        P(),
        P(),
        P(),
        P(),
        P(("ha", "wa"), None),
        P(("ha", "wa")),
        P(("ha", "wa"), None, None),
    )
    return jax.shard_map(
        local,
        mesh=mesh,
        in_specs=placed,
        out_specs=(P("ha", "wa", None), P("wa", "ha", None), P("wa", "ha", None), P(), P(), P(), P()),
        check_vma=False,
    )
```

```python
import functools

import jax
import jax.numpy as jnp
from jax import lax
from jax.experimental import pallas as pl
from jax.experimental.pallas import tpu as pltpu
from jax.sharding import PartitionSpec as P

F32 = jnp.float32
BF16 = jnp.bfloat16
GRAD_SCALE = 0.25
GROUP = 64
CLS = 32
CHUNKS = 2
EXCHANGE_VMEM = 58 * 1024 * 1024
FINISH_VMEM = 58 * 1024 * 1024
DECODE_VMEM = 58 * 1024 * 1024
REDUCE_VMEM = 58 * 1024 * 1024
MESH = pl.DeviceIdType.MESH


def dotg(left, right, dims):
    return lax.dot_general(left, right, ((dims[0], dims[1]), ((), ())), preferred_element_type=F32)


def exchange_kernel(
    ids_ref, idrow_ref, hw_ref, zh_ref, labels_ref,
    ids_out, hw_out, zh_out, lab_out,
    hwv, zhv, labv, hw32, zh32, rows32, rows16, lab16, load_sem, sem, z_sem,
):
    ha, wa = lax.axis_index("ha"), lax.axis_index("wa")
    z, base = lax.rem(wa, 4), wa - lax.rem(wa, 4)
    half = lab16.shape[0]
    own_rows = zh_ref.shape[1]
    part = own_rows // 4
    across = (lax.rem(ha + 8, 16), wa)
    corner = (lax.rem(ha + 8, 16), lax.rem(wa + 4, 8))
    ring = [(ha, base + lax.rem(z + k, 4)) for k in (1, 3, 2)]
    loads = [
        pltpu.make_async_copy(zh_ref, zhv, load_sem.at[0]),
        pltpu.make_async_copy(hw_ref, hwv, load_sem.at[1]),
        pltpu.make_async_copy(labels_ref.at[pl.ds(half, half)], labv, load_sem.at[2]),
    ]
    for cp in loads:
        cp.start()
    barrier = pltpu.get_barrier_semaphore()
    for to in [across, corner] + ring:
        pl.semaphore_signal(barrier, inc=1, device_id=to, device_id_type=MESH)

    def send(source, dest, sems, to):
        return pltpu.make_async_remote_copy(
            src_ref=source, dst_ref=dest, send_sem=sems.at[0], recv_sem=sems.at[1],
            device_id=to, device_id_type=MESH)

    def turn(q):
        at = pl.multiple_of(q * part, part)
        zh_out[pl.ds(at, part)] = jnp.swapaxes(zh32[:, pl.ds(at, part), :], 0, 1).astype(BF16)

    loads[0].wait()
    zh32[...] = zhv[...].astype(F32)
    turn(z)
    pl.semaphore_wait(barrier, 5)
    got = own_rows + z * part
    fetch = send(zh_out.at[pl.ds(z * part, part)], zh_out.at[pl.ds(got, part)], z_sem.at[0], corner)
    fetch.start()
    for k in (1, 2, 3):
        turn(lax.rem(z + k, 4))
    loads[2].wait()
    lab16[...] = labv[...].astype(F32).astype(BF16)
    loads[1].wait()
    hw32[...] = hwv[...].astype(F32)

    def pick(i, carry):
        for k in range(8):
            s = i * 8 + k
            at = 2 * ids_ref[0, half + s]
            for p in range(2):
                rows32[pl.ds(2 * s + p, 1), :] = hw32[pl.ds(at + p, 1), :]
        return carry

    lax.fori_loop(0, half // 8, pick, 0)
    rows16[...] = rows32[...].astype(BF16)
    fetch.wait_recv()
    mine = zh_out.at[pl.ds(got, part)]
    outs = [send(mine, mine, z_sem.at[1 + k], to) for k, to in enumerate(ring)]
    outs += [send(rows16, hw_out, sem.at[0], across), send(lab16, lab_out, sem.at[1], across),
             send(idrow_ref, ids_out, sem.at[2], across)]
    for cp in outs:
        cp.start()
    for cp in outs:
        cp.wait()
    fetch.wait_send()


def exchange(ids, hw, zh, labels):
    vmem = pl.BlockSpec(memory_space=pltpu.VMEM)
    hbm = pl.BlockSpec(memory_space=pl.ANY)
    half = labels.shape[0] // 2
    depth, rows, chans = zh.shape
    dma = lambda *s: pltpu.SemaphoreType.DMA(s)
    return pl.pallas_call(
        exchange_kernel,
        out_shape=(
            jax.ShapeDtypeStruct(ids.shape, jnp.int32),
            jax.ShapeDtypeStruct((2 * half, chans), BF16),
            jax.ShapeDtypeStruct((2 * rows, depth, chans), BF16),
            jax.ShapeDtypeStruct((half, labels.shape[1]), BF16),
        ),
        in_specs=[pl.BlockSpec(memory_space=pltpu.SMEM), vmem, hbm, hbm, hbm],
        out_specs=[vmem] * 4,
        scratch_shapes=[
            pltpu.VMEM(hw.shape, BF16), pltpu.VMEM(zh.shape, BF16), pltpu.VMEM((half, labels.shape[1]), jnp.int32),
            pltpu.VMEM(hw.shape, F32), pltpu.VMEM(zh.shape, F32), pltpu.VMEM((2 * half, chans), F32),
            pltpu.VMEM((2 * half, chans), BF16), pltpu.VMEM((half, labels.shape[1]), BF16),
            dma(3), dma(3, 2), dma(4, 2),
        ],
        compiler_params=pltpu.CompilerParams(
            collective_id=1, has_side_effects=True, vmem_limit_bytes=EXCHANGE_VMEM),
    )(ids, ids, hw, zh, labels)


def decode_kernel(
    ids_ref, idx_ref, count_ref, hw_ref, hwx_ref, zh_ref, wz_ref, labels_ref, labx_ref, win_ref, bin_ref, wout_ref, bout_ref,
    hw_out, zh_out, wz_out, wt_out,
    hw32, labs, wpad, wout_t, gwi_ref, gwo_ref, gbo_ref,
):
    rows, depth, chans = zh_ref.shape
    pairs = wz_ref.shape[0]
    half = labx_ref.shape[0]
    own_hw = hw_ref.shape[0]
    own_n = jnp.minimum(count_ref[0], half)
    hw32[:own_hw] = hw_ref[...].astype(F32)
    hw32[own_hw:] = hwx_ref[...].astype(F32)
    labs[:half] = labels_ref[:half]
    labs[half:] = labx_ref[...].astype(F32).astype(jnp.int32)
    hw_out[...] = jnp.zeros_like(hw_out)
    zh_out[...] = jnp.zeros_like(zh_out)
    wz_out[...] = jnp.zeros_like(wz_out)
    gwi_ref[...] = jnp.zeros_like(gwi_ref)
    gwo_ref[...] = jnp.zeros_like(gwo_ref)
    gbo_ref[...] = jnp.zeros_like(gbo_ref)
    ncls = wout_ref.shape[0]
    wpad[...] = jnp.zeros_like(wpad)
    wpad[:ncls] = wout_ref[...].astype(F32)
    wout_t[...] = wpad[...].astype(BF16)
    at_row = lax.broadcasted_iota(jnp.int32, (CLS, ncls), 0)
    at_col = lax.broadcasted_iota(jnp.int32, (CLS, ncls), 1)
    bcol = jnp.sum(jnp.where(at_row == at_col, bout_ref[...], 0.0), axis=1, keepdims=True)
    bcol = jnp.where(lax.broadcasted_iota(jnp.int32, (CLS, 1), 0) < ncls, bcol, -1e30)
    samples = GROUP * 2 * depth
    low = lax.broadcasted_iota(jnp.int32, (depth // 8, 8, chans), 1) < 4
    run = 2 * depth

    def body(step, carry):
        base = step * GROUP
        spots = []
        parts = []
        for g in range(GROUP):
            i = base + g
            own = i < own_n
            j = jnp.maximum(i - own_n, 0)
            rid = jnp.where(own, ids_ref[0, i], idx_ref[0, half + j])
            row = rid // pairs + jnp.where(own, 0, rows // 2)
            pair = rid % pairs
            hw_at = jnp.where(own, 2 * rid, own_hw + 2 * j)
            slot = jnp.where(own, i, half + j)
            spots.append((slot, row, pair))
            zh = zh_ref[row].astype(F32)
            for p in range(2):
                hw = hw32[pl.ds(hw_at + p, 1), :]
                wz = wz_ref[pair, p * depth:(p + 1) * depth, :].astype(F32)
                parts.append(((hw + zh) + wz).astype(BF16))
        feats = jnp.concatenate(parts, axis=0)
        u = jnp.dot(feats, win_ref[...] * 0.5, preferred_element_type=F32) + bin_ref[...] * 0.5
        a = jnp.tanh(u) + 1.0
        h = u * a
        hid = h.astype(BF16)
        logits = dotg(wout_t[...], hid, ((1,), (1,)))
        dparts = []
        for g in range(GROUP):
            lt = logits[:24, g * run:(g + 1) * run] + bcol[:24]
            top = jnp.max(lt, axis=0, keepdims=True)
            e = jnp.exp(lt - top)
            inv = GRAD_SCALE / jnp.sum(e, axis=0, keepdims=True)
            lab = labs[pl.ds(spots[g][0], 1), :]
            cls = lax.broadcasted_iota(jnp.int32, lt.shape, 0)
            hot = jnp.where(cls == lab, GRAD_SCALE, 0.0)
            dparts.append(jnp.concatenate([e * inv - hot, jnp.zeros((CLS - 24, run), F32)], axis=0).astype(BF16))
        dlt = jnp.concatenate(dparts, axis=1)
        gwo_ref[...] += jnp.dot(dlt, hid, preferred_element_type=F32)
        tot = dparts[0].astype(F32)
        for g in range(1, GROUP):
            tot += dparts[g].astype(F32)
        gbo_ref[...] += tot
        dhh = dotg(dlt, wout_t[...] * 0.5, ((0,), (0,)))
        q = (u + u + 1.0) - h
        dpre = (dhh * a * q).astype(BF16)
        lhs = jnp.concatenate([feats.T, jnp.ones((16, samples), BF16)], axis=0)
        df = dotg(dpre, win_ref[...], ((1,), (1,)))
        for g in range(GROUP):
            slot, row, pair = spots[g]
            d = df[g * run:(g + 1) * run]
            zh_out[:, row] += (d[:depth] + d[depth:]).reshape(depth // 8, 8, chans)
            d0, d1 = d[:depth].reshape(depth // 8, 8, chans), d[depth:].reshape(depth // 8, 8, chans)
            wz_out[0, :, pair] += jnp.where(low, d0, pltpu.roll(d1, 4, 1))
            wz_out[1, :, pair] += jnp.where(low, pltpu.roll(d0, 4, 1), d1)
            for p in range(2):
                hw_out[pl.ds(2 * slot + p, 1), :] = jnp.sum(d[p * depth:(p + 1) * depth], axis=0, keepdims=True)
        gwi_ref[...] += jnp.dot(lhs, dpre, preferred_element_type=F32)
        return carry

    lax.fori_loop(0, half // GROUP, body, 0)
    top = chans + 16
    wt_out[0:top] = gwi_ref[:, :128]
    wt_out[top:2 * top] = gwi_ref[:, 128:]
    wt_out[2 * top:2 * top + CLS] = gwo_ref[:, :128]
    wt_out[2 * top + CLS:2 * top + 2 * CLS] = gwo_ref[:, 128:]
    wt_out[2 * top + 2 * CLS:] = gbo_ref[...]


def decode_runs(ids, idx, count, hw, hwx, zh, wz, labels, labx, w_in, b_in, w_out, b_out):
    rows, depth, chans = zh.shape
    pairs = wz.shape[0]
    hid, ncls = w_out.shape
    smem = pl.BlockSpec(memory_space=pltpu.SMEM)
    vmem = pl.BlockSpec(memory_space=pltpu.VMEM)
    return pl.pallas_call(
        decode_kernel,
        out_shape=(
            jax.ShapeDtypeStruct((2 * labels.shape[0], chans), F32),
            jax.ShapeDtypeStruct((depth // 8, rows, 8, chans), F32),
            jax.ShapeDtypeStruct((2, depth // 8, pairs, 8, chans), F32),
            jax.ShapeDtypeStruct((2 * (chans + 16) + 3 * CLS, chans), F32),
        ),
        in_specs=[smem] * 3 + [vmem] * 10,
        out_specs=[vmem] * 4,
        scratch_shapes=[
            pltpu.VMEM((hw.shape[0] + hwx.shape[0], chans), F32),
            pltpu.VMEM(labels.shape, jnp.int32),
            pltpu.VMEM((CLS, hid), F32),
            pltpu.VMEM((CLS, hid), BF16),
            pltpu.VMEM((chans + 16, hid), F32),
            pltpu.VMEM((CLS, hid), F32),
            pltpu.VMEM((CLS, 2 * depth), F32),
        ],
        compiler_params=pltpu.CompilerParams(vmem_limit_bytes=DECODE_VMEM),
    )(ids, idx, count, hw, hwx, zh, wz, labels, labx, w_in, b_in.reshape(1, hid), w_out.T, b_out.reshape(1, ncls))


def finish_kernel(
    ids_ref, count_ref, own_ref, back_ref, wz_ref, zh_ref, wt_ref,
    hw_out, wz_out, zh_out, gwi_out, gbi_out, gwo_out, gbo_out,
):
    cap = ids_ref.shape[1]
    half = cap // 2
    used = count_ref[0]
    chans = hw_out.shape[1]
    ncls = gwo_out.shape[0]
    hw_out[...] = jnp.zeros_like(hw_out)

    def put(source, start):
        def go(i, carry):
            for k in range(8):
                s = i * 8 + k
                at = 2 * ids_ref[0, start + s]
                for p in range(2):
                    hw_out[pl.ds(at + p, 1), :] = source[pl.ds(2 * s + p, 1), :]
            return carry
        return go

    lax.fori_loop(0, pl.cdiv(jnp.minimum(used, half), 8), put(own_ref, 0), 0)
    lax.fori_loop(0, pl.cdiv(jnp.maximum(used - half, 0), 8), put(back_ref, half), 0)
    wz_out[...] = wz_ref[...]
    for i in range(8):
        zh_out[i] = zh_ref[:, i, :]
    top = chans + 16
    gwi_out[:, :128] = wt_ref[:chans]
    gwi_out[:, 128:] = wt_ref[top:top + chans]
    gbi_out[:, :128] = wt_ref[chans:chans + 1]
    gbi_out[:, 128:] = wt_ref[top + chans:top + chans + 1]
    at = 2 * top
    gwo_out[:, :128] = wt_ref[at:at + ncls]
    gwo_out[:, 128:] = wt_ref[at + CLS:at + CLS + ncls]
    gbo_out[...] = jnp.sum(wt_ref[at + 2 * CLS:at + 3 * CLS].T, axis=0, keepdims=True)[:, :ncls]


def finish(ids, count, own, back, wz, zh, wt, hw_rows, hid, ncls):
    smem = pl.BlockSpec(memory_space=pltpu.SMEM)
    vmem = pl.BlockSpec(memory_space=pltpu.VMEM)
    chans = own.shape[1]
    return pl.pallas_call(
        finish_kernel,
        out_shape=(
            jax.ShapeDtypeStruct((hw_rows, chans), F32),
            jax.ShapeDtypeStruct(wz.shape, F32),
            jax.ShapeDtypeStruct((8, zh.shape[0], chans), F32),
            jax.ShapeDtypeStruct((chans, hid), F32),
            jax.ShapeDtypeStruct((1, hid), F32),
            jax.ShapeDtypeStruct((ncls, hid), F32),
            jax.ShapeDtypeStruct((1, ncls), F32),
        ),
        in_specs=[smem] * 2 + [vmem] * 5,
        out_specs=[vmem] * 7,
        compiler_params=pltpu.CompilerParams(vmem_limit_bytes=FINISH_VMEM),
    )(ids, count, own, back, wz, zh, wt)


TAIL = 16


def pack(v):
    most = jnp.maximum(jnp.max(jnp.abs(v), axis=1, keepdims=True), 1e-30)
    power = jnp.ceil(jnp.log2(most))
    q = jnp.round(v * (jnp.exp2(-power) * 32600.0)).astype(jnp.int32).astype(jnp.int16)
    tail = jnp.broadcast_to(power, (v.shape[0], TAIL, v.shape[2])).astype(jnp.int32).astype(jnp.int16)
    return q, tail


def unpack(q, tail):
    power = tail.astype(jnp.int32).astype(F32)[:, :1]
    return q.astype(jnp.int32).astype(F32) * (jnp.exp2(power) * (1.0 / 32600.0))


class Coded:
    def __init__(self, out, into, sems, to):
        self.out, self.into, self.rows = out, into, out.shape[1] - TAIL
        self.copy = pltpu.make_async_remote_copy(
            src_ref=out, dst_ref=into, send_sem=sems.at[0], recv_sem=sems.at[1], device_id=to, device_id_type=MESH)

    def send(self, v):
        self.out[:, :self.rows], self.out[:, self.rows:] = pack(v)
        self.copy.start()

    def receive(self):
        self.copy.wait_recv()
        return unpack(self.into[:, :self.rows], self.into[:, self.rows:])

    def done(self):
        self.copy.wait_send()


def coded_buffers(n, groups, rows, chans):
    shape = (n, groups, rows + TAIL, chans)
    return [pltpu.VMEM(shape, jnp.int16), pltpu.VMEM(shape, jnp.int16), pltpu.SemaphoreType.DMA((n, 2))]


def coded(bufs, i, to):
    out, into, sems = bufs
    return Coded(out.at[i], into.at[i], sems.at[i], to)


class Ring:
    def __init__(self, src, bufs, first, axis, me, span, at):
        self.src, self.me, self.span = src, me, span
        self.plus, self.minus, self.far = lax.rem(me + 1, 4), lax.rem(me + 3, 4), lax.rem(me + 2, 4)
        self.lo, self.hi = pl.ds(at, span // 2), pl.ds(at + span // 2, span // 2)
        to = [axis(self.plus), axis(self.minus)]
        self.msgs = [coded(bufs, first + i, to[d]) for i, d in enumerate((0, 1, 1, 0, 0, 1))]

    def part(self, where, half):
        v = self.src[:, where, half]
        return v.reshape(v.shape[0], -1, v.shape[-1])

    def begin(self):
        self.msgs[0].send(self.part(self.far, self.lo))
        self.msgs[1].send(self.part(self.far, self.hi))
        self.msgs[2].send(self.part(self.minus, self.lo))
        self.msgs[3].send(self.part(self.plus, self.hi))

    def relay(self):
        self.msgs[4].send(self.msgs[0].receive() + self.part(self.plus, self.lo))
        self.msgs[5].send(self.msgs[1].receive() + self.part(self.minus, self.hi))

    def finish(self):
        lo = self.part(self.me, self.lo) + self.msgs[2].receive() + self.msgs[4].receive()
        hi = self.part(self.me, self.hi) + self.msgs[3].receive() + self.msgs[5].receive()
        return lo, hi

    def done(self):
        for m in self.msgs:
            m.done()


def reduce_kernel(
    wz_ref, zh_hbm, wt_ref, hw_hbm, wz_out, zh_out, wt_out, hw_out,
    wz_own, zh_ref, hw_ref, core_in, xsum, zsum, wt_in, wt_mid,
    own_sem, core_sem, wa_sem, wb_sem, wc_sem, *bufs,
):
    xbufs, ybufs, zbufs, zybufs, hwbufs = (bufs[3 * i:3 * i + 3] for i in range(5))
    ha, wa = lax.axis_index("ha"), lax.axis_index("wa")
    yh, x, c = ha // 8, lax.rem(ha // 2, 4), lax.rem(ha, 2)
    yl, z = wa // 4, lax.rem(wa, 4)
    span = wz_ref.shape[3] // CHUNKS
    n_ha, n_wa = wt_ref.shape[0], 8

    def on_x(to):
        return (yh * 8 + to * 2 + c, wa)

    def on_z(to):
        return (ha, yl * 4 + to)

    sibling = (ha + 1 - 2 * c, wa)
    across = (lax.rem(ha + 8, 16), wa)
    beside = (ha, lax.rem(wa + 4, 8))
    corner = (lax.rem(ha + 8, 16), lax.rem(wa + 4, 8))
    rows_own = zh_ref.shape[2] // 2

    barrier = pltpu.get_barrier_semaphore()

    def greet_ha(i, carry):
        pl.semaphore_signal(barrier, inc=1, device_id=(lax.rem(ha + i, n_ha), wa), device_id_type=MESH)
        return carry

    def greet_wa(i, carry):
        pl.semaphore_signal(barrier, inc=1, device_id=(ha, lax.rem(wa + i, n_wa)), device_id_type=MESH)
        return carry

    loads = [
        pltpu.make_async_copy(zh_hbm, zh_ref, own_sem.at[0]),
        pltpu.make_async_copy(hw_hbm.at[pl.ds(hw_out.shape[0], hw_out.shape[0])], hw_ref, own_sem.at[1]),
        pltpu.make_async_copy(wz_ref.at[c], wz_own, own_sem.at[2]),
    ]
    for cp in loads:
        cp.start()
    lax.fori_loop(1, n_ha, greet_ha, 0)
    lax.fori_loop(1, n_wa, greet_wa, 0)
    pl.semaphore_signal(barrier, inc=1, device_id=corner, device_id_type=MESH)
    pl.semaphore_wait(barrier, n_ha + n_wa - 1)

    def send(source, dest, sems, to):
        return pltpu.make_async_remote_copy(
            src_ref=source, dst_ref=dest, send_sem=sems.at[0], recv_sem=sems.at[1],
            device_id=to, device_id_type=MESH)

    core = [
        send(wz_ref.at[1 - c, :, :, pl.ds(k * span, span)], core_in.at[:, :, pl.ds(k * span, span)],
             core_sem.at[k], sibling)
        for k in range(CHUNKS)
    ]
    for k in range(CHUNKS):
        core[k].start()
    zring = Ring(zh_ref, zbufs, 0, on_z, z, zh_ref.shape[2], 0)
    loads[0].wait()
    zring.begin()

    def wt_first(i):
        to = lax.rem(ha + i, n_ha)
        return pltpu.make_async_remote_copy(
            src_ref=wt_ref.at[to], dst_ref=wt_in.at[ha], send_sem=wa_sem.at[0], recv_sem=wa_sem.at[1],
            device_id=(to, wa), device_id_type=MESH)

    def wt_second(i):
        to = lax.rem(wa + i, n_wa)
        return pltpu.make_async_remote_copy(
            src_ref=wt_mid.at[wa], dst_ref=wt_mid.at[wa], send_sem=wb_sem.at[0], recv_sem=wb_sem.at[1],
            device_id=(ha, to), device_id_type=MESH)

    def wt_third(i):
        to = lax.rem(ha + i, n_ha)
        return pltpu.make_async_remote_copy(
            src_ref=wt_out.at[ha], dst_ref=wt_out.at[ha], send_sem=wc_sem.at[0], recv_sem=wc_sem.at[1],
            device_id=(to, wa), device_id_type=MESH)

    def start(make, n):
        def go(i, carry):
            make(i).start()
            return carry
        lax.fori_loop(1, n, go, 0)

    def all_of(buf, sems, n, to):
        many = buf.at[pl.ds(0, n - 1)]
        return pltpu.make_async_remote_copy(
            src_ref=many, dst_ref=many, send_sem=sems.at[0], recv_sem=sems.at[1], device_id=to, device_id_type=MESH)

    first_all, second_all, third_all = (
        all_of(wt_in, wa_sem, n_ha, sibling), all_of(wt_mid, wb_sem, n_wa, beside), all_of(wt_out, wc_sem, n_ha, sibling))
    start(wt_first, n_ha)
    chans = hw_ref.shape[1]
    back = coded(hwbufs, 0, across)
    loads[1].wait()
    back.send(hw_ref[...].reshape(-1, 128, chans))
    loads[2].wait()
    rings = []
    for k in range(CHUNKS):
        rows = pl.ds(k * span, span)
        core[k].wait_recv()
        core_in[:, :, rows] += wz_own[:, :, rows]
        rings.append(Ring(core_in, xbufs, 6 * k, on_x, x, span, k * span))
        rings[k].begin()
    zring.relay()
    first_all.wait_recv()
    wt_in[ha] = wt_ref[ha]
    tot = wt_in[0]
    for i in range(1, n_ha):
        tot += wt_in[i]
    wt_mid[wa] = tot
    start(wt_second, n_wa)
    for k in range(CHUNKS):
        rings[k].relay()
    second_all.wait_recv()
    tot = wt_mid[0]
    for i in range(1, n_wa):
        tot += wt_mid[i]
    wt_out[ha] = tot
    start(wt_third, n_ha)
    zsum[0], zsum[1] = zring.finish()
    zys = [coded(zybufs, i, to) for i, to in enumerate((beside, corner, across))]
    zys[0].send(zsum[0, pl.ds(1 - yl, 1)])
    zys[1].send(zsum[1, pl.ds(1 - yl, 1)])
    zys[2].send(zsum[1, pl.ds(yl, 1)])
    ys = []
    for k in range(CHUNKS):
        rows = pl.ds(k * span, span)
        lo, hi = rings[k].finish()
        xsum[:, k, 0:span * 4], xsum[:, k, span * 4:] = lo, hi
        ys.append(coded(ybufs, k, across))
        ys[k].send(xsum[pl.ds(1 - yh, 1), k])
    total = zsum[0, pl.ds(yl, 1)]
    for m in zys:
        total += m.receive()
    zh_out[...] = total.reshape(zh_out.shape)
    for k in range(CHUNKS):
        rows = pl.ds(k * span, span)
        wz_out[pl.ds(k * span, span)] = (xsum[pl.ds(yh, 1), k] + ys[k].receive()).reshape(span, 8, chans)
    hw_out[...] = back.receive().reshape(hw_out.shape)
    third_all.wait_recv()
    for k in range(CHUNKS):
        core[k].wait_send()
        rings[k].done()
        ys[k].done()
    zring.done()
    for m in zys + [back]:
        m.done()
    for cp in (first_all, second_all, third_all):
        cp.wait_send()


def reduce_all(wz, zh, wt, hw):
    half_w, chans = wz.shape[3], wz.shape[5]
    rows = zh.shape[2]
    span = half_w // CHUNKS
    vmem = pl.BlockSpec(memory_space=pltpu.VMEM)
    hbm = pl.BlockSpec(memory_space=pl.ANY)
    buf = lambda *s: pltpu.VMEM(s, F32)
    dma = lambda *s: pltpu.SemaphoreType.DMA(s)
    return pl.pallas_call(
        reduce_kernel,
        out_shape=(
            jax.ShapeDtypeStruct((half_w, 8, chans), F32),
            jax.ShapeDtypeStruct((rows // 2, 8, chans), F32),
            jax.ShapeDtypeStruct(wt.shape, F32),
            jax.ShapeDtypeStruct((hw.shape[0] // 2, chans), F32),
        ),
        in_specs=[hbm, hbm, vmem, hbm],
        out_specs=[vmem] * 4,
        scratch_shapes=[
            buf(2, 4, half_w, 8, chans),
            buf(*zh.shape),
            buf(hw.shape[0] // 2, chans),
            buf(2, 4, half_w, 8, chans),
            buf(2, CHUNKS, span * 8, chans),
            buf(2, 2, rows * 4, chans),
            buf(*wt.shape),
            buf(8, *wt.shape[1:]),
            dma(3), dma(CHUNKS, 2), dma(2), dma(2), dma(2),
            *coded_buffers(6 * CHUNKS, 2, span * 4, chans),
            *coded_buffers(CHUNKS, 1, span * 8, chans),
            *coded_buffers(6, 2, rows * 4, chans),
            *coded_buffers(3, 1, rows * 4, chans),
            *coded_buffers(1, hw.shape[0] // 256, 128, chans),
        ],
        compiler_params=pltpu.CompilerParams(
            collective_id=0, has_side_effects=True, vmem_limit_bytes=REDUCE_VMEM),
    )(wz, zh, wt, hw)


def local(hw_plane, zh_plane, wz_plane, w_in, b_in, w_out, b_out, run_index, run_count, labels):
    rows, cols, chans = hw_plane.shape
    depth = zh_plane.shape[0]
    ncls = w_out.shape[1]
    hw_rows = hw_plane.reshape(rows * cols, chans)
    idx, hwx, zh2, labx = exchange(run_index, hw_rows, zh_plane, labels[0])
    hw, zh, wz, wt = decode_runs(
        run_index, idx, run_count, hw_rows, hwx, zh2, wz_plane.reshape(cols // 2, 2 * depth, chans),
        labels[0], labx, w_in, b_in, w_out, b_out,
    )
    wz_grad, zh_grad, wt, back = reduce_all(
        wz.reshape(2, 2, 4, cols // 2, 8, chans), zh.reshape(2, 4, 2 * rows, 8, chans), wt.reshape(16, -1, chans), hw)
    hw_grad, wz_grad, zh_grad, gwi, gbi, gwo, gbo = finish(
        run_index, run_count, hw, back, wz_grad, zh_grad, wt.reshape(-1, chans), rows * cols, w_out.shape[0], ncls)
    return (hw_grad.reshape(rows, cols, chans), zh_grad, wz_grad.reshape(cols, 4, chans), gwi, gbi[0], gwo.T, gbo[0])


def solution(mesh):
    placed = (
        P("ha", "wa", None),
        P(None, "ha", None),
        P("wa", None, None),
        P(),
        P(),
        P(),
        P(),
        P(("ha", "wa"), None),
        P(("ha", "wa")),
        P(("ha", "wa"), None, None),
    )
    return jax.shard_map(
        local,
        mesh=mesh,
        in_specs=placed,
        out_specs=(P("ha", "wa", None), P("wa", "ha", None), P("wa", "ha", None), P(), P(), P(), P()),
        check_vma=False,
    )
```

```python
import functools

import jax
import jax.numpy as jnp
from jax import lax
from jax.experimental import pallas as pl
from jax.experimental.pallas import tpu as pltpu
from jax.sharding import PartitionSpec as P

F32 = jnp.float32
BF16 = jnp.bfloat16
GRAD_SCALE = 0.25
GROUP = 64
CLS = 32
CHUNKS = 2
EXCHANGE_VMEM = 58 * 1024 * 1024
FINISH_VMEM = 58 * 1024 * 1024
DECODE_VMEM = 58 * 1024 * 1024
REDUCE_VMEM = 58 * 1024 * 1024
MESH = pl.DeviceIdType.MESH


def dotg(left, right, dims):
    return lax.dot_general(left, right, ((dims[0], dims[1]), ((), ())), preferred_element_type=F32)


def exchange_kernel(
    ids_ref, idrow_ref, hw_ref, zh_ref, labels_ref,
    ids_out, hw_out, zh_out, lab_out,
    hwv, zhv, labv, hw32, zh32, rows32, rows16, lab16, load_sem, sem, z_sem,
):
    ha, wa = lax.axis_index("ha"), lax.axis_index("wa")
    z, base = lax.rem(wa, 4), wa - lax.rem(wa, 4)
    half = lab16.shape[0]
    own_rows = zh_ref.shape[1]
    part = own_rows // 4
    across = (lax.rem(ha + 8, 16), wa)
    corner = (lax.rem(ha + 8, 16), lax.rem(wa + 4, 8))
    ring = [(ha, base + lax.rem(z + k, 4)) for k in (1, 3, 2)]
    loads = [
        pltpu.make_async_copy(zh_ref, zhv, load_sem.at[0]),
        pltpu.make_async_copy(hw_ref, hwv, load_sem.at[1]),
        pltpu.make_async_copy(labels_ref.at[pl.ds(half, half)], labv, load_sem.at[2]),
    ]
    for cp in loads:
        cp.start()
    barrier = pltpu.get_barrier_semaphore()
    for to in [across, corner] + ring:
        pl.semaphore_signal(barrier, inc=1, device_id=to, device_id_type=MESH)

    def send(source, dest, sems, to):
        return pltpu.make_async_remote_copy(
            src_ref=source, dst_ref=dest, send_sem=sems.at[0], recv_sem=sems.at[1],
            device_id=to, device_id_type=MESH)

    def turn(q):
        at = pl.multiple_of(q * part, part)
        zh_out[pl.ds(at, part)] = jnp.swapaxes(zh32[:, pl.ds(at, part), :], 0, 1).astype(BF16)

    loads[0].wait()
    zh32[...] = zhv[...].astype(F32)
    turn(z)
    pl.semaphore_wait(barrier, 5)
    got = own_rows + z * part
    fetch = send(zh_out.at[pl.ds(z * part, part)], zh_out.at[pl.ds(got, part)], z_sem.at[0], corner)
    fetch.start()
    for k in (1, 2, 3):
        turn(lax.rem(z + k, 4))
    loads[2].wait()
    lab16[...] = labv[...].astype(F32).astype(BF16)
    loads[1].wait()
    hw32[...] = hwv[...].astype(F32)

    def pick(i, carry):
        for k in range(8):
            s = i * 8 + k
            at = 2 * ids_ref[0, half + s]
            for p in range(2):
                rows32[pl.ds(2 * s + p, 1), :] = hw32[pl.ds(at + p, 1), :]
        return carry

    lax.fori_loop(0, half // 8, pick, 0)
    rows16[...] = rows32[...].astype(BF16)
    fetch.wait_recv()
    mine = zh_out.at[pl.ds(got, part)]
    outs = [send(mine, mine, z_sem.at[1 + k], to) for k, to in enumerate(ring)]
    outs += [send(rows16, hw_out, sem.at[0], across), send(lab16, lab_out, sem.at[1], across),
             send(idrow_ref, ids_out, sem.at[2], across)]
    for cp in outs:
        cp.start()
    for cp in outs:
        cp.wait()
    fetch.wait_send()


def exchange(ids, hw, zh, labels):
    vmem = pl.BlockSpec(memory_space=pltpu.VMEM)
    hbm = pl.BlockSpec(memory_space=pl.ANY)
    half = labels.shape[0] // 2
    depth, rows, chans = zh.shape
    dma = lambda *s: pltpu.SemaphoreType.DMA(s)
    return pl.pallas_call(
        exchange_kernel,
        out_shape=(
            jax.ShapeDtypeStruct(ids.shape, jnp.int32),
            jax.ShapeDtypeStruct((2 * half, chans), BF16),
            jax.ShapeDtypeStruct((2 * rows, depth, chans), BF16),
            jax.ShapeDtypeStruct((half, labels.shape[1]), BF16),
        ),
        in_specs=[pl.BlockSpec(memory_space=pltpu.SMEM), vmem, hbm, hbm, hbm],
        out_specs=[vmem] * 4,
        scratch_shapes=[
            pltpu.VMEM(hw.shape, BF16), pltpu.VMEM(zh.shape, BF16), pltpu.VMEM((half, labels.shape[1]), jnp.int32),
            pltpu.VMEM(hw.shape, F32), pltpu.VMEM(zh.shape, F32), pltpu.VMEM((2 * half, chans), F32),
            pltpu.VMEM((2 * half, chans), BF16), pltpu.VMEM((half, labels.shape[1]), BF16),
            dma(3), dma(3, 2), dma(4, 2),
        ],
        compiler_params=pltpu.CompilerParams(
            collective_id=1, has_side_effects=True, vmem_limit_bytes=EXCHANGE_VMEM),
    )(ids, ids, hw, zh, labels)


def decode_kernel(
    ids_ref, idx_ref, count_ref, hw_ref, hwx_ref, zh_ref, wz_ref, labels_ref, labx_ref, win_ref, bin_ref, wout_ref, bout_ref,
    hw_out, zh_out, wz_out, wt_out,
    hw32, labs, wpad, wout_t, gwi_ref, gwo_ref, gbo_ref,
):
    rows, depth, chans = zh_ref.shape
    pairs = wz_ref.shape[0]
    half = labx_ref.shape[0]
    own_hw = hw_ref.shape[0]
    own_n = jnp.minimum(count_ref[0], half)
    hw32[:own_hw] = hw_ref[...].astype(F32)
    hw32[own_hw:] = hwx_ref[...].astype(F32)
    labs[:half] = labels_ref[:half]
    labs[half:] = labx_ref[...].astype(F32).astype(jnp.int32)
    hw_out[...] = jnp.zeros_like(hw_out)
    zh_out[...] = jnp.zeros_like(zh_out)
    wz_out[...] = jnp.zeros_like(wz_out)
    gwi_ref[...] = jnp.zeros_like(gwi_ref)
    gwo_ref[...] = jnp.zeros_like(gwo_ref)
    gbo_ref[...] = jnp.zeros_like(gbo_ref)
    ncls = wout_ref.shape[0]
    wpad[...] = jnp.zeros_like(wpad)
    wpad[:ncls] = wout_ref[...].astype(F32)
    wout_t[...] = wpad[...].astype(BF16)
    at_row = lax.broadcasted_iota(jnp.int32, (CLS, ncls), 0)
    at_col = lax.broadcasted_iota(jnp.int32, (CLS, ncls), 1)
    bcol = jnp.sum(jnp.where(at_row == at_col, bout_ref[...], 0.0), axis=1, keepdims=True)
    bcol = jnp.where(lax.broadcasted_iota(jnp.int32, (CLS, 1), 0) < ncls, bcol, -1e30)
    samples = GROUP * 2 * depth
    low = lax.broadcasted_iota(jnp.int32, (depth // 8, 8, chans), 1) < 4
    run = 2 * depth

    def body(step, carry):
        base = step * GROUP
        spots = []
        parts = []
        for g in range(GROUP):
            i = base + g
            own = i < own_n
            j = jnp.maximum(i - own_n, 0)
            rid = jnp.where(own, ids_ref[0, i], idx_ref[0, half + j])
            row = rid // pairs + jnp.where(own, 0, rows // 2)
            pair = rid % pairs
            hw_at = jnp.where(own, 2 * rid, own_hw + 2 * j)
            slot = jnp.where(own, i, half + j)
            spots.append((slot, row, pair))
            zh = zh_ref[row].astype(F32)
            for p in range(2):
                hw = hw32[pl.ds(hw_at + p, 1), :]
                wz = wz_ref[pair, p * depth:(p + 1) * depth, :].astype(F32)
                parts.append(((hw + zh) + wz).astype(BF16))
        feats = jnp.concatenate(parts, axis=0)
        u = jnp.dot(feats, win_ref[...] * 0.5, preferred_element_type=F32) + bin_ref[...] * 0.5
        a = jnp.tanh(u) + 1.0
        h = u * a
        hid = h.astype(BF16)
        logits = dotg(wout_t[...], hid, ((1,), (1,)))
        dparts = []
        for g in range(GROUP):
            lt = logits[:24, g * run:(g + 1) * run] + bcol[:24]
            top = jnp.max(lt, axis=0, keepdims=True)
            e = jnp.exp(lt - top)
            inv = GRAD_SCALE / jnp.sum(e, axis=0, keepdims=True)
            lab = labs[pl.ds(spots[g][0], 1), :]
            cls = lax.broadcasted_iota(jnp.int32, lt.shape, 0)
            hot = jnp.where(cls == lab, GRAD_SCALE, 0.0)
            dparts.append(jnp.concatenate([e * inv - hot, jnp.zeros((CLS - 24, run), F32)], axis=0).astype(BF16))
        dlt = jnp.concatenate(dparts, axis=1)
        gwo_ref[...] += jnp.dot(dlt, hid, preferred_element_type=F32)
        tot = dparts[0].astype(F32)
        for g in range(1, GROUP):
            tot += dparts[g].astype(F32)
        gbo_ref[...] += tot
        dhh = dotg(dlt, wout_t[...] * 0.5, ((0,), (0,)))
        q = (u + u + 1.0) - h
        dpre = (dhh * a * q).astype(BF16)
        lhs = jnp.concatenate([feats.T, jnp.ones((16, samples), BF16)], axis=0)
        df = dotg(dpre, win_ref[...], ((1,), (1,)))
        for g in range(GROUP):
            slot, row, pair = spots[g]
            d = df[g * run:(g + 1) * run]
            zh_out[:, row] += (d[:depth] + d[depth:]).reshape(depth // 8, 8, chans)
            d0, d1 = d[:depth].reshape(depth // 8, 8, chans), d[depth:].reshape(depth // 8, 8, chans)
            wz_out[0, :, pair] += jnp.where(low, d0, pltpu.roll(d1, 4, 1))
            wz_out[1, :, pair] += jnp.where(low, pltpu.roll(d0, 4, 1), d1)
            for p in range(2):
                hw_out[pl.ds(2 * slot + p, 1), :] = jnp.sum(d[p * depth:(p + 1) * depth], axis=0, keepdims=True)
        gwi_ref[...] += jnp.dot(lhs, dpre, preferred_element_type=F32)
        return carry

    lax.fori_loop(0, half // GROUP, body, 0)
    top = chans + 16
    wt_out[0:top] = gwi_ref[:, :128]
    wt_out[top:2 * top] = gwi_ref[:, 128:]
    wt_out[2 * top:2 * top + CLS] = gwo_ref[:, :128]
    wt_out[2 * top + CLS:2 * top + 2 * CLS] = gwo_ref[:, 128:]
    wt_out[2 * top + 2 * CLS:] = gbo_ref[...]


def decode_runs(ids, idx, count, hw, hwx, zh, wz, labels, labx, w_in, b_in, w_out, b_out):
    rows, depth, chans = zh.shape
    pairs = wz.shape[0]
    hid, ncls = w_out.shape
    smem = pl.BlockSpec(memory_space=pltpu.SMEM)
    vmem = pl.BlockSpec(memory_space=pltpu.VMEM)
    return pl.pallas_call(
        decode_kernel,
        out_shape=(
            jax.ShapeDtypeStruct((2 * labels.shape[0], chans), F32),
            jax.ShapeDtypeStruct((depth // 8, rows, 8, chans), F32),
            jax.ShapeDtypeStruct((2, depth // 8, pairs, 8, chans), F32),
            jax.ShapeDtypeStruct((2 * (chans + 16) + 3 * CLS, chans), F32),
        ),
        in_specs=[smem] * 3 + [vmem] * 10,
        out_specs=[vmem] * 4,
        scratch_shapes=[
            pltpu.VMEM((hw.shape[0] + hwx.shape[0], chans), F32),
            pltpu.VMEM(labels.shape, jnp.int32),
            pltpu.VMEM((CLS, hid), F32),
            pltpu.VMEM((CLS, hid), BF16),
            pltpu.VMEM((chans + 16, hid), F32),
            pltpu.VMEM((CLS, hid), F32),
            pltpu.VMEM((CLS, 2 * depth), F32),
        ],
        compiler_params=pltpu.CompilerParams(vmem_limit_bytes=DECODE_VMEM),
    )(ids, idx, count, hw, hwx, zh, wz, labels, labx, w_in, b_in.reshape(1, hid), w_out.T, b_out.reshape(1, ncls))


def finish_kernel(
    ids_ref, count_ref, own_ref, back_ref, wz_ref, zh_ref, wt_ref,
    hw_out, wz_out, zh_out, gwi_out, gbi_out, gwo_out, gbo_out,
):
    cap = ids_ref.shape[1]
    half = cap // 2
    used = count_ref[0]
    chans = hw_out.shape[1]
    ncls = gwo_out.shape[0]
    hw_out[...] = jnp.zeros_like(hw_out)

    def put(source, start):
        def go(i, carry):
            for k in range(8):
                s = i * 8 + k
                at = 2 * ids_ref[0, start + s]
                for p in range(2):
                    hw_out[pl.ds(at + p, 1), :] = source[pl.ds(2 * s + p, 1), :]
            return carry
        return go

    lax.fori_loop(0, pl.cdiv(jnp.minimum(used, half), 8), put(own_ref, 0), 0)
    lax.fori_loop(0, pl.cdiv(jnp.maximum(used - half, 0), 8), put(back_ref, half), 0)
    wz_out[...] = wz_ref[...]
    for i in range(8):
        zh_out[i] = zh_ref[:, i, :]
    top = chans + 16
    gwi_out[:, :128] = wt_ref[:chans]
    gwi_out[:, 128:] = wt_ref[top:top + chans]
    gbi_out[:, :128] = wt_ref[chans:chans + 1]
    gbi_out[:, 128:] = wt_ref[top + chans:top + chans + 1]
    at = 2 * top
    gwo_out[:, :128] = wt_ref[at:at + ncls]
    gwo_out[:, 128:] = wt_ref[at + CLS:at + CLS + ncls]
    gbo_out[...] = jnp.sum(wt_ref[at + 2 * CLS:at + 3 * CLS].T, axis=0, keepdims=True)[:, :ncls]


def finish(ids, count, own, back, wz, zh, wt, hw_rows, hid, ncls):
    smem = pl.BlockSpec(memory_space=pltpu.SMEM)
    vmem = pl.BlockSpec(memory_space=pltpu.VMEM)
    chans = own.shape[1]
    return pl.pallas_call(
        finish_kernel,
        out_shape=(
            jax.ShapeDtypeStruct((hw_rows, chans), F32),
            jax.ShapeDtypeStruct(wz.shape, F32),
            jax.ShapeDtypeStruct((8, zh.shape[0], chans), F32),
            jax.ShapeDtypeStruct((chans, hid), F32),
            jax.ShapeDtypeStruct((1, hid), F32),
            jax.ShapeDtypeStruct((ncls, hid), F32),
            jax.ShapeDtypeStruct((1, ncls), F32),
        ),
        in_specs=[smem] * 2 + [vmem] * 5,
        out_specs=[vmem] * 7,
        compiler_params=pltpu.CompilerParams(vmem_limit_bytes=FINISH_VMEM),
    )(ids, count, own, back, wz, zh, wt)


TAIL = 16


def pack(v):
    most = jnp.maximum(jnp.max(jnp.abs(v), axis=1, keepdims=True), 1e-30)
    power = jnp.ceil(jnp.log2(most))
    q = jnp.round(v * (jnp.exp2(-power) * 32600.0)).astype(jnp.int32).astype(jnp.int16)
    tail = jnp.broadcast_to(power, (v.shape[0], TAIL, v.shape[2])).astype(jnp.int32).astype(jnp.int16)
    return q, tail


def unpack(q, tail):
    power = tail.astype(jnp.int32).astype(F32)[:, :1]
    return q.astype(jnp.int32).astype(F32) * (jnp.exp2(power) * (1.0 / 32600.0))


class Coded:
    def __init__(self, out, into, sems, to):
        self.out, self.into, self.rows = out, into, out.shape[1] - TAIL
        self.copy = pltpu.make_async_remote_copy(
            src_ref=out, dst_ref=into, send_sem=sems.at[0], recv_sem=sems.at[1], device_id=to, device_id_type=MESH)

    def send(self, v):
        self.out[:, :self.rows], self.out[:, self.rows:] = pack(v)
        self.copy.start()

    def receive(self):
        self.copy.wait_recv()
        return unpack(self.into[:, :self.rows], self.into[:, self.rows:])

    def done(self):
        self.copy.wait_send()


def coded_buffers(n, groups, rows, chans):
    shape = (n, groups, rows + TAIL, chans)
    return [pltpu.VMEM(shape, jnp.int16), pltpu.VMEM(shape, jnp.int16), pltpu.SemaphoreType.DMA((n, 2))]


def coded(bufs, i, to):
    out, into, sems = bufs
    return Coded(out.at[i], into.at[i], sems.at[i], to)


class Ring:
    def __init__(self, src, bufs, first, axis, me, span, at):
        self.src, self.me, self.span = src, me, span
        self.plus, self.minus, self.far = lax.rem(me + 1, 4), lax.rem(me + 3, 4), lax.rem(me + 2, 4)
        self.lo, self.hi = pl.ds(at, span // 2), pl.ds(at + span // 2, span // 2)
        to = [axis(self.plus), axis(self.minus)]
        self.msgs = [coded(bufs, first + i, to[d]) for i, d in enumerate((0, 1, 1, 0, 0, 1))]

    def part(self, where, half):
        v = self.src[:, where, half]
        return v.reshape(v.shape[0], -1, v.shape[-1])

    def begin(self):
        self.msgs[0].send(self.part(self.far, self.lo))
        self.msgs[1].send(self.part(self.far, self.hi))
        self.msgs[2].send(self.part(self.minus, self.lo))
        self.msgs[3].send(self.part(self.plus, self.hi))

    def relay(self):
        self.msgs[4].send(self.msgs[0].receive() + self.part(self.plus, self.lo))
        self.msgs[5].send(self.msgs[1].receive() + self.part(self.minus, self.hi))

    def finish(self):
        lo = self.part(self.me, self.lo) + self.msgs[2].receive() + self.msgs[4].receive()
        hi = self.part(self.me, self.hi) + self.msgs[3].receive() + self.msgs[5].receive()
        return lo, hi

    def done(self):
        for m in self.msgs:
            m.done()


def reduce_kernel(
    wz_ref, zh_hbm, wt_ref, hw_hbm, wz_out, zh_out, wt_out, hw_out,
    wz_own, zh_ref, hw_ref, core_in, xsum, zsum, wt_core, wt_in, wt_mid,
    own_sem, core_sem, wa_sem, wb_sem, wc_sem, wd_sem, we_sem, *bufs,
):
    xbufs, ybufs, zbufs, zybufs, hwbufs = (bufs[3 * i:3 * i + 3] for i in range(5))
    ha, wa = lax.axis_index("ha"), lax.axis_index("wa")
    yh, x, c = ha // 8, lax.rem(ha // 2, 4), lax.rem(ha, 2)
    yl, z = wa // 4, lax.rem(wa, 4)
    span = wz_ref.shape[3] // CHUNKS
    n_ha, n_wa = wt_ref.shape[0], 8

    def on_x(to):
        return (yh * 8 + to * 2 + c, wa)

    def on_z(to):
        return (ha, yl * 4 + to)

    sibling = (ha + 1 - 2 * c, wa)
    across = (lax.rem(ha + 8, 16), wa)
    beside = (ha, lax.rem(wa + 4, 8))
    corner = (lax.rem(ha + 8, 16), lax.rem(wa + 4, 8))
    rows_own = zh_ref.shape[2] // 2

    barrier = pltpu.get_barrier_semaphore()

    def greet_ha(i, carry):
        pl.semaphore_signal(barrier, inc=1, device_id=(lax.rem(ha + i, n_ha), wa), device_id_type=MESH)
        return carry

    def greet_wa(i, carry):
        pl.semaphore_signal(barrier, inc=1, device_id=(ha, lax.rem(wa + i, n_wa)), device_id_type=MESH)
        return carry

    loads = [
        pltpu.make_async_copy(zh_hbm, zh_ref, own_sem.at[0]),
        pltpu.make_async_copy(hw_hbm.at[pl.ds(hw_out.shape[0], hw_out.shape[0])], hw_ref, own_sem.at[1]),
        pltpu.make_async_copy(wz_ref.at[c], wz_own, own_sem.at[2]),
    ]
    for cp in loads:
        cp.start()
    lax.fori_loop(1, n_ha, greet_ha, 0)
    lax.fori_loop(1, n_wa, greet_wa, 0)
    pl.semaphore_signal(barrier, inc=1, device_id=corner, device_id_type=MESH)
    pl.semaphore_wait(barrier, n_ha + n_wa - 1)

    def send(source, dest, sems, to):
        return pltpu.make_async_remote_copy(
            src_ref=source, dst_ref=dest, send_sem=sems.at[0], recv_sem=sems.at[1],
            device_id=to, device_id_type=MESH)

    core = [
        send(wz_ref.at[1 - c, :, :, pl.ds(k * span, span)], core_in.at[:, :, pl.ds(k * span, span)],
             core_sem.at[k], sibling)
        for k in range(CHUNKS)
    ]
    peers = n_ha // 2
    group = ha // 2
    wt_own = pl.ds(c * peers, peers)
    wt_swap = send(wt_ref.at[pl.ds((1 - c) * peers, peers)], wt_core, wd_sem, sibling)
    wt_swap.start()
    for k in range(CHUNKS):
        core[k].start()
    zring = Ring(zh_ref, zbufs, 0, on_z, z, zh_ref.shape[2], 0)
    loads[0].wait()
    zring.begin()

    def wt_first(i):
        to = lax.rem(group + i, peers)
        return pltpu.make_async_remote_copy(
            src_ref=wt_core.at[to], dst_ref=wt_in.at[group], send_sem=wa_sem.at[0], recv_sem=wa_sem.at[1],
            device_id=(to * 2 + c, wa), device_id_type=MESH)

    def wt_second(i):
        to = lax.rem(wa + i, n_wa)
        return pltpu.make_async_remote_copy(
            src_ref=wt_mid.at[wa], dst_ref=wt_mid.at[wa], send_sem=wb_sem.at[0], recv_sem=wb_sem.at[1],
            device_id=(ha, to), device_id_type=MESH)

    def wt_third(i):
        to = lax.rem(group + i, peers)
        piece = wt_out.at[c * peers + group]
        return pltpu.make_async_remote_copy(
            src_ref=piece, dst_ref=piece, send_sem=wc_sem.at[0], recv_sem=wc_sem.at[1],
            device_id=(to * 2 + c, wa), device_id_type=MESH)

    def start(make, n):
        def go(i, carry):
            make(i).start()
            return carry
        lax.fori_loop(1, n, go, 0)

    def all_of(buf, sems, n, to):
        many = buf.at[pl.ds(0, n - 1)]
        return pltpu.make_async_remote_copy(
            src_ref=many, dst_ref=many, send_sem=sems.at[0], recv_sem=sems.at[1], device_id=to, device_id_type=MESH)

    first_all, second_all, third_all = (
        all_of(wt_in, wa_sem, peers, sibling), all_of(wt_mid, wb_sem, n_wa, beside), all_of(wt_out, wc_sem, peers, sibling))
    wt_swap.wait_recv()
    wt_core[...] += wt_ref[wt_own]
    start(wt_first, peers)
    chans = hw_ref.shape[1]
    back = coded(hwbufs, 0, across)
    loads[1].wait()
    back.send(hw_ref[...].reshape(-1, 128, chans))
    loads[2].wait()
    rings = []
    for k in range(CHUNKS):
        rows = pl.ds(k * span, span)
        core[k].wait_recv()
        core_in[:, :, rows] += wz_own[:, :, rows]
        rings.append(Ring(core_in, xbufs, 6 * k, on_x, x, span, k * span))
        rings[k].begin()
    zring.relay()
    first_all.wait_recv()
    wt_in[group] = wt_core[group]
    tot = wt_in[0]
    for i in range(1, peers):
        tot += wt_in[i]
    wt_mid[wa] = tot
    start(wt_second, n_wa)
    for k in range(CHUNKS):
        rings[k].relay()
    second_all.wait_recv()
    tot = wt_mid[0]
    for i in range(1, n_wa):
        tot += wt_mid[i]
    wt_out[c * peers + group] = tot
    start(wt_third, peers)
    zsum[0], zsum[1] = zring.finish()
    zys = [coded(zybufs, i, to) for i, to in enumerate((beside, corner, across))]
    zys[0].send(zsum[0, pl.ds(1 - yl, 1)])
    zys[1].send(zsum[1, pl.ds(1 - yl, 1)])
    zys[2].send(zsum[1, pl.ds(yl, 1)])
    ys = []
    for k in range(CHUNKS):
        rows = pl.ds(k * span, span)
        lo, hi = rings[k].finish()
        xsum[:, k, 0:span * 4], xsum[:, k, span * 4:] = lo, hi
        ys.append(coded(ybufs, k, across))
        ys[k].send(xsum[pl.ds(1 - yh, 1), k])
    third_all.wait_recv()
    wt_last = send(wt_out.at[wt_own], wt_out.at[wt_own], we_sem, sibling)
    wt_last.start()
    total = zsum[0, pl.ds(yl, 1)]
    for m in zys:
        total += m.receive()
    zh_out[...] = total.reshape(zh_out.shape)
    for k in range(CHUNKS):
        rows = pl.ds(k * span, span)
        wz_out[pl.ds(k * span, span)] = (xsum[pl.ds(yh, 1), k] + ys[k].receive()).reshape(span, 8, chans)
    hw_out[...] = back.receive().reshape(hw_out.shape)
    for k in range(CHUNKS):
        core[k].wait_send()
        rings[k].done()
        ys[k].done()
    zring.done()
    for m in zys + [back]:
        m.done()
    wt_last.wait()
    for cp in (wt_swap, first_all, second_all, third_all):
        cp.wait_send()


def reduce_all(wz, zh, wt, hw):
    half_w, chans = wz.shape[3], wz.shape[5]
    rows = zh.shape[2]
    span = half_w // CHUNKS
    vmem = pl.BlockSpec(memory_space=pltpu.VMEM)
    hbm = pl.BlockSpec(memory_space=pl.ANY)
    buf = lambda *s: pltpu.VMEM(s, F32)
    dma = lambda *s: pltpu.SemaphoreType.DMA(s)
    return pl.pallas_call(
        reduce_kernel,
        out_shape=(
            jax.ShapeDtypeStruct((half_w, 8, chans), F32),
            jax.ShapeDtypeStruct((rows // 2, 8, chans), F32),
            jax.ShapeDtypeStruct(wt.shape, F32),
            jax.ShapeDtypeStruct((hw.shape[0] // 2, chans), F32),
        ),
        in_specs=[hbm, hbm, vmem, hbm],
        out_specs=[vmem] * 4,
        scratch_shapes=[
            buf(2, 4, half_w, 8, chans),
            buf(*zh.shape),
            buf(hw.shape[0] // 2, chans),
            buf(2, 4, half_w, 8, chans),
            buf(2, CHUNKS, span * 8, chans),
            buf(2, 2, rows * 4, chans),
            buf(8, *wt.shape[1:]),
            buf(8, *wt.shape[1:]),
            buf(8, *wt.shape[1:]),
            dma(3), dma(CHUNKS, 2), dma(2), dma(2), dma(2), dma(2), dma(2),
            *coded_buffers(6 * CHUNKS, 2, span * 4, chans),
            *coded_buffers(CHUNKS, 1, span * 8, chans),
            *coded_buffers(6, 2, rows * 4, chans),
            *coded_buffers(3, 1, rows * 4, chans),
            *coded_buffers(1, hw.shape[0] // 256, 128, chans),
        ],
        compiler_params=pltpu.CompilerParams(
            collective_id=0, has_side_effects=True, vmem_limit_bytes=REDUCE_VMEM),
    )(wz, zh, wt, hw)


def local(hw_plane, zh_plane, wz_plane, w_in, b_in, w_out, b_out, run_index, run_count, labels):
    rows, cols, chans = hw_plane.shape
    depth = zh_plane.shape[0]
    ncls = w_out.shape[1]
    hw_rows = hw_plane.reshape(rows * cols, chans)
    idx, hwx, zh2, labx = exchange(run_index, hw_rows, zh_plane, labels[0])
    hw, zh, wz, wt = decode_runs(
        run_index, idx, run_count, hw_rows, hwx, zh2, wz_plane.reshape(cols // 2, 2 * depth, chans),
        labels[0], labx, w_in, b_in, w_out, b_out,
    )
    wz_grad, zh_grad, wt, back = reduce_all(
        wz.reshape(2, 2, 4, cols // 2, 8, chans), zh.reshape(2, 4, 2 * rows, 8, chans), wt.reshape(16, -1, chans), hw)
    hw_grad, wz_grad, zh_grad, gwi, gbi, gwo, gbo = finish(
        run_index, run_count, hw, back, wz_grad, zh_grad, wt.reshape(-1, chans), rows * cols, w_out.shape[0], ncls)
    return (hw_grad.reshape(rows, cols, chans), zh_grad, wz_grad.reshape(cols, 4, chans), gwi, gbi[0], gwo.T, gbo[0])


def solution(mesh):
    placed = (
        P("ha", "wa", None),
        P(None, "ha", None),
        P("wa", None, None),
        P(),
        P(),
        P(),
        P(),
        P(("ha", "wa"), None),
        P(("ha", "wa")),
        P(("ha", "wa"), None, None),
    )
    return jax.shard_map(
        local,
        mesh=mesh,
        in_specs=placed,
        out_specs=(P("ha", "wa", None), P("wa", "ha", None), P("wa", "ha", None), P(), P(), P(), P()),
        check_vma=False,
    )
```

```python
import functools

import jax
import jax.numpy as jnp
from jax import lax
from jax.experimental import pallas as pl
from jax.experimental.pallas import tpu as pltpu
from jax.sharding import PartitionSpec as P

F32 = jnp.float32
BF16 = jnp.bfloat16
GRAD_SCALE = 0.25
GROUP = 64
CLS = 32
CHUNKS = 1
EXCHANGE_VMEM = 58 * 1024 * 1024
FINISH_VMEM = 58 * 1024 * 1024
DECODE_VMEM = 58 * 1024 * 1024
REDUCE_VMEM = 58 * 1024 * 1024
MESH = pl.DeviceIdType.MESH


def dotg(left, right, dims):
    return lax.dot_general(left, right, ((dims[0], dims[1]), ((), ())), preferred_element_type=F32)


def exchange_kernel(
    ids_ref, idrow_ref, hw_ref, zh_ref, labels_ref,
    ids_out, hw_out, zh_out, lab_out,
    hwv, zhv, labv, hw32, zh32, rows32, rows16, lab16, load_sem, sem, z_sem,
):
    ha, wa = lax.axis_index("ha"), lax.axis_index("wa")
    z, base = lax.rem(wa, 4), wa - lax.rem(wa, 4)
    half = lab16.shape[0]
    own_rows = zh_ref.shape[1]
    part = own_rows // 4
    across = (lax.rem(ha + 8, 16), wa)
    corner = (lax.rem(ha + 8, 16), lax.rem(wa + 4, 8))
    ring = [(ha, base + lax.rem(z + k, 4)) for k in (1, 3, 2)]
    loads = [
        pltpu.make_async_copy(zh_ref, zhv, load_sem.at[0]),
        pltpu.make_async_copy(hw_ref, hwv, load_sem.at[1]),
        pltpu.make_async_copy(labels_ref.at[pl.ds(half, half)], labv, load_sem.at[2]),
    ]
    for cp in loads:
        cp.start()
    barrier = pltpu.get_barrier_semaphore()
    for to in [across, corner] + ring:
        pl.semaphore_signal(barrier, inc=1, device_id=to, device_id_type=MESH)

    def send(source, dest, sems, to):
        return pltpu.make_async_remote_copy(
            src_ref=source, dst_ref=dest, send_sem=sems.at[0], recv_sem=sems.at[1],
            device_id=to, device_id_type=MESH)

    def turn(q):
        at = pl.multiple_of(q * part, part)
        zh_out[pl.ds(at, part)] = jnp.swapaxes(zh32[:, pl.ds(at, part), :], 0, 1).astype(BF16)

    loads[0].wait()
    zh32[...] = zhv[...].astype(F32)
    turn(z)
    pl.semaphore_wait(barrier, 5)
    got = own_rows + z * part
    fetch = send(zh_out.at[pl.ds(z * part, part)], zh_out.at[pl.ds(got, part)], z_sem.at[0], corner)
    fetch.start()
    for k in (1, 2, 3):
        turn(lax.rem(z + k, 4))
    loads[2].wait()
    lab16[...] = labv[...].astype(F32).astype(BF16)
    loads[1].wait()
    hw32[...] = hwv[...].astype(F32)

    def pick(i, carry):
        for k in range(8):
            s = i * 8 + k
            at = 2 * ids_ref[0, half + s]
            for p in range(2):
                rows32[pl.ds(2 * s + p, 1), :] = hw32[pl.ds(at + p, 1), :]
        return carry

    lax.fori_loop(0, half // 8, pick, 0)
    rows16[...] = rows32[...].astype(BF16)
    fetch.wait_recv()
    mine = zh_out.at[pl.ds(got, part)]
    outs = [send(mine, mine, z_sem.at[1 + k], to) for k, to in enumerate(ring)]
    outs += [send(rows16, hw_out, sem.at[0], across), send(lab16, lab_out, sem.at[1], across),
             send(idrow_ref, ids_out, sem.at[2], across)]
    for cp in outs:
        cp.start()
    for cp in outs:
        cp.wait()
    fetch.wait_send()


def exchange(ids, hw, zh, labels):
    vmem = pl.BlockSpec(memory_space=pltpu.VMEM)
    hbm = pl.BlockSpec(memory_space=pl.ANY)
    half = labels.shape[0] // 2
    depth, rows, chans = zh.shape
    dma = lambda *s: pltpu.SemaphoreType.DMA(s)
    return pl.pallas_call(
        exchange_kernel,
        out_shape=(
            jax.ShapeDtypeStruct(ids.shape, jnp.int32),
            jax.ShapeDtypeStruct((2 * half, chans), BF16),
            jax.ShapeDtypeStruct((2 * rows, depth, chans), BF16),
            jax.ShapeDtypeStruct((half, labels.shape[1]), BF16),
        ),
        in_specs=[pl.BlockSpec(memory_space=pltpu.SMEM), vmem, hbm, hbm, hbm],
        out_specs=[vmem] * 4,
        scratch_shapes=[
            pltpu.VMEM(hw.shape, BF16), pltpu.VMEM(zh.shape, BF16), pltpu.VMEM((half, labels.shape[1]), jnp.int32),
            pltpu.VMEM(hw.shape, F32), pltpu.VMEM(zh.shape, F32), pltpu.VMEM((2 * half, chans), F32),
            pltpu.VMEM((2 * half, chans), BF16), pltpu.VMEM((half, labels.shape[1]), BF16),
            dma(3), dma(3, 2), dma(4, 2),
        ],
        compiler_params=pltpu.CompilerParams(
            collective_id=1, has_side_effects=True, vmem_limit_bytes=EXCHANGE_VMEM),
    )(ids, ids, hw, zh, labels)


def decode_kernel(
    ids_ref, idx_ref, count_ref, hw_ref, hwx_ref, zh_ref, wz_ref, labels_ref, labx_ref, win_ref, bin_ref, wout_ref, bout_ref,
    hw_out, zh_out, wz_out, wt_out,
    hw32, labs, wpad, wout_t, gwi_ref, gwo_ref, gbo_ref,
):
    rows, depth, chans = zh_ref.shape
    pairs = wz_ref.shape[0]
    half = labx_ref.shape[0]
    own_hw = hw_ref.shape[0]
    own_n = jnp.minimum(count_ref[0], half)
    hw32[:own_hw] = hw_ref[...].astype(F32)
    hw32[own_hw:] = hwx_ref[...].astype(F32)
    labs[:half] = labels_ref[:half]
    labs[half:] = labx_ref[...].astype(F32).astype(jnp.int32)
    hw_out[...] = jnp.zeros_like(hw_out)
    zh_out[...] = jnp.zeros_like(zh_out)
    wz_out[...] = jnp.zeros_like(wz_out)
    gwi_ref[...] = jnp.zeros_like(gwi_ref)
    gwo_ref[...] = jnp.zeros_like(gwo_ref)
    gbo_ref[...] = jnp.zeros_like(gbo_ref)
    ncls = wout_ref.shape[0]
    wpad[...] = jnp.zeros_like(wpad)
    wpad[:ncls] = wout_ref[...].astype(F32)
    wout_t[...] = wpad[...].astype(BF16)
    at_row = lax.broadcasted_iota(jnp.int32, (CLS, ncls), 0)
    at_col = lax.broadcasted_iota(jnp.int32, (CLS, ncls), 1)
    bcol = jnp.sum(jnp.where(at_row == at_col, bout_ref[...], 0.0), axis=1, keepdims=True)
    bcol = jnp.where(lax.broadcasted_iota(jnp.int32, (CLS, 1), 0) < ncls, bcol, -1e30)
    samples = GROUP * 2 * depth
    low = lax.broadcasted_iota(jnp.int32, (depth // 8, 8, chans), 1) < 4
    run = 2 * depth

    def body(step, carry):
        base = step * GROUP
        spots = []
        parts = []
        for g in range(GROUP):
            i = base + g
            own = i < own_n
            j = jnp.maximum(i - own_n, 0)
            rid = jnp.where(own, ids_ref[0, i], idx_ref[0, half + j])
            row = rid // pairs + jnp.where(own, 0, rows // 2)
            pair = rid % pairs
            hw_at = jnp.where(own, 2 * rid, own_hw + 2 * j)
            slot = jnp.where(own, i, half + j)
            spots.append((slot, row, pair))
            zh = zh_ref[row].astype(F32)
            for p in range(2):
                hw = hw32[pl.ds(hw_at + p, 1), :]
                wz = wz_ref[pair, p * depth:(p + 1) * depth, :].astype(F32)
                parts.append(((hw + zh) + wz).astype(BF16))
        feats = jnp.concatenate(parts, axis=0)
        u = jnp.dot(feats, win_ref[...] * 0.5, preferred_element_type=F32) + bin_ref[...] * 0.5
        a = jnp.tanh(u) + 1.0
        h = u * a
        hid = h.astype(BF16)
        logits = dotg(wout_t[...], hid, ((1,), (1,)))
        dparts = []
        for g in range(GROUP):
            lt = logits[:24, g * run:(g + 1) * run] + bcol[:24]
            top = jnp.max(lt, axis=0, keepdims=True)
            e = jnp.exp(lt - top)
            inv = GRAD_SCALE / jnp.sum(e, axis=0, keepdims=True)
            lab = labs[pl.ds(spots[g][0], 1), :]
            cls = lax.broadcasted_iota(jnp.int32, lt.shape, 0)
            hot = jnp.where(cls == lab, GRAD_SCALE, 0.0)
            dparts.append(jnp.concatenate([e * inv - hot, jnp.zeros((CLS - 24, run), F32)], axis=0).astype(BF16))
        dlt = jnp.concatenate(dparts, axis=1)
        gwo_ref[...] += jnp.dot(dlt, hid, preferred_element_type=F32)
        tot = dparts[0].astype(F32)
        for g in range(1, GROUP):
            tot += dparts[g].astype(F32)
        gbo_ref[...] += tot
        dhh = dotg(dlt, wout_t[...] * 0.5, ((0,), (0,)))
        q = (u + u + 1.0) - h
        dpre = (dhh * a * q).astype(BF16)
        lhs = jnp.concatenate([feats.T, jnp.ones((16, samples), BF16)], axis=0)
        df = dotg(dpre, win_ref[...], ((1,), (1,)))
        for g in range(GROUP):
            slot, row, pair = spots[g]
            d = df[g * run:(g + 1) * run]
            zh_out[:, row] += (d[:depth] + d[depth:]).reshape(depth // 8, 8, chans)
            d0, d1 = d[:depth].reshape(depth // 8, 8, chans), d[depth:].reshape(depth // 8, 8, chans)
            wz_out[0, :, pair] += jnp.where(low, d0, pltpu.roll(d1, 4, 1))
            wz_out[1, :, pair] += jnp.where(low, pltpu.roll(d0, 4, 1), d1)
            for p in range(2):
                hw_out[pl.ds(2 * slot + p, 1), :] = jnp.sum(d[p * depth:(p + 1) * depth], axis=0, keepdims=True)
        gwi_ref[...] += jnp.dot(lhs, dpre, preferred_element_type=F32)
        return carry

    lax.fori_loop(0, half // GROUP, body, 0)
    top = chans + 16
    wt_out[0:top] = gwi_ref[:, :128]
    wt_out[top:2 * top] = gwi_ref[:, 128:]
    wt_out[2 * top:2 * top + CLS] = gwo_ref[:, :128]
    wt_out[2 * top + CLS:2 * top + 2 * CLS] = gwo_ref[:, 128:]
    wt_out[2 * top + 2 * CLS:] = gbo_ref[...]


def decode_runs(ids, idx, count, hw, hwx, zh, wz, labels, labx, w_in, b_in, w_out, b_out):
    rows, depth, chans = zh.shape
    pairs = wz.shape[0]
    hid, ncls = w_out.shape
    smem = pl.BlockSpec(memory_space=pltpu.SMEM)
    vmem = pl.BlockSpec(memory_space=pltpu.VMEM)
    return pl.pallas_call(
        decode_kernel,
        out_shape=(
            jax.ShapeDtypeStruct((2 * labels.shape[0], chans), F32),
            jax.ShapeDtypeStruct((depth // 8, rows, 8, chans), F32),
            jax.ShapeDtypeStruct((2, depth // 8, pairs, 8, chans), F32),
            jax.ShapeDtypeStruct((2 * (chans + 16) + 3 * CLS, chans), F32),
        ),
        in_specs=[smem] * 3 + [vmem] * 10,
        out_specs=[vmem] * 4,
        scratch_shapes=[
            pltpu.VMEM((hw.shape[0] + hwx.shape[0], chans), F32),
            pltpu.VMEM(labels.shape, jnp.int32),
            pltpu.VMEM((CLS, hid), F32),
            pltpu.VMEM((CLS, hid), BF16),
            pltpu.VMEM((chans + 16, hid), F32),
            pltpu.VMEM((CLS, hid), F32),
            pltpu.VMEM((CLS, 2 * depth), F32),
        ],
        compiler_params=pltpu.CompilerParams(vmem_limit_bytes=DECODE_VMEM),
    )(ids, idx, count, hw, hwx, zh, wz, labels, labx, w_in, b_in.reshape(1, hid), w_out.T, b_out.reshape(1, ncls))


def finish_kernel(
    ids_ref, count_ref, own_ref, back_ref, wz_ref, zh_ref, wt_ref,
    hw_out, wz_out, zh_out, gwi_out, gbi_out, gwo_out, gbo_out,
):
    cap = ids_ref.shape[1]
    half = cap // 2
    used = count_ref[0]
    chans = hw_out.shape[1]
    ncls = gwo_out.shape[0]
    hw_out[...] = jnp.zeros_like(hw_out)

    def put(source, start):
        def go(i, carry):
            for k in range(8):
                s = i * 8 + k
                at = 2 * ids_ref[0, start + s]
                for p in range(2):
                    hw_out[pl.ds(at + p, 1), :] = source[pl.ds(2 * s + p, 1), :]
            return carry
        return go

    lax.fori_loop(0, pl.cdiv(jnp.minimum(used, half), 8), put(own_ref, 0), 0)
    lax.fori_loop(0, pl.cdiv(jnp.maximum(used - half, 0), 8), put(back_ref, half), 0)
    wz_out[...] = wz_ref[...]
    for i in range(8):
        zh_out[i] = zh_ref[:, i, :]
    top = chans + 16
    gwi_out[:, :128] = wt_ref[:chans]
    gwi_out[:, 128:] = wt_ref[top:top + chans]
    gbi_out[:, :128] = wt_ref[chans:chans + 1]
    gbi_out[:, 128:] = wt_ref[top + chans:top + chans + 1]
    at = 2 * top
    gwo_out[:, :128] = wt_ref[at:at + ncls]
    gwo_out[:, 128:] = wt_ref[at + CLS:at + CLS + ncls]
    gbo_out[...] = jnp.sum(wt_ref[at + 2 * CLS:at + 3 * CLS].T, axis=0, keepdims=True)[:, :ncls]


def finish(ids, count, own, back, wz, zh, wt, hw_rows, hid, ncls):
    smem = pl.BlockSpec(memory_space=pltpu.SMEM)
    vmem = pl.BlockSpec(memory_space=pltpu.VMEM)
    chans = own.shape[1]
    return pl.pallas_call(
        finish_kernel,
        out_shape=(
            jax.ShapeDtypeStruct((hw_rows, chans), F32),
            jax.ShapeDtypeStruct(wz.shape, F32),
            jax.ShapeDtypeStruct((8, zh.shape[0], chans), F32),
            jax.ShapeDtypeStruct((chans, hid), F32),
            jax.ShapeDtypeStruct((1, hid), F32),
            jax.ShapeDtypeStruct((ncls, hid), F32),
            jax.ShapeDtypeStruct((1, ncls), F32),
        ),
        in_specs=[smem] * 2 + [vmem] * 5,
        out_specs=[vmem] * 7,
        compiler_params=pltpu.CompilerParams(vmem_limit_bytes=FINISH_VMEM),
    )(ids, count, own, back, wz, zh, wt)


TAIL = 16


def pack(v):
    most = jnp.maximum(jnp.max(jnp.abs(v), axis=1, keepdims=True), 1e-30)
    power = jnp.ceil(jnp.log2(most))
    q = jnp.round(v * (jnp.exp2(-power) * 32600.0)).astype(jnp.int32).astype(jnp.int16)
    tail = jnp.broadcast_to(power, (v.shape[0], TAIL, v.shape[2])).astype(jnp.int32).astype(jnp.int16)
    return q, tail


def unpack(q, tail):
    power = tail.astype(jnp.int32).astype(F32)[:, :1]
    return q.astype(jnp.int32).astype(F32) * (jnp.exp2(power) * (1.0 / 32600.0))


class Coded:
    def __init__(self, out, into, sems, to):
        self.out, self.into, self.rows = out, into, out.shape[1] - TAIL
        self.copy = pltpu.make_async_remote_copy(
            src_ref=out, dst_ref=into, send_sem=sems.at[0], recv_sem=sems.at[1], device_id=to, device_id_type=MESH)

    def send(self, v):
        self.out[:, :self.rows], self.out[:, self.rows:] = pack(v)
        self.copy.start()

    def receive(self):
        self.copy.wait_recv()
        return unpack(self.into[:, :self.rows], self.into[:, self.rows:])

    def done(self):
        self.copy.wait_send()


def coded_buffers(n, groups, rows, chans):
    shape = (n, groups, rows + TAIL, chans)
    return [pltpu.VMEM(shape, jnp.int16), pltpu.VMEM(shape, jnp.int16), pltpu.SemaphoreType.DMA((n, 2))]


def coded(bufs, i, to):
    out, into, sems = bufs
    return Coded(out.at[i], into.at[i], sems.at[i], to)


class Ring:
    def __init__(self, src, bufs, first, axis, me, span, at):
        self.src, self.me, self.span = src, me, span
        self.plus, self.minus, self.far = lax.rem(me + 1, 4), lax.rem(me + 3, 4), lax.rem(me + 2, 4)
        self.lo, self.hi = pl.ds(at, span // 2), pl.ds(at + span // 2, span // 2)
        to = [axis(self.plus), axis(self.minus)]
        self.msgs = [coded(bufs, first + i, to[d]) for i, d in enumerate((0, 1, 1, 0, 0, 1))]

    def part(self, where, half):
        v = self.src[:, where, half]
        return v.reshape(v.shape[0], -1, v.shape[-1])

    def begin(self):
        self.msgs[0].send(self.part(self.far, self.lo))
        self.msgs[1].send(self.part(self.far, self.hi))
        self.msgs[2].send(self.part(self.minus, self.lo))
        self.msgs[3].send(self.part(self.plus, self.hi))

    def relay(self):
        self.msgs[4].send(self.msgs[0].receive() + self.part(self.plus, self.lo))
        self.msgs[5].send(self.msgs[1].receive() + self.part(self.minus, self.hi))

    def finish(self):
        lo = self.part(self.me, self.lo) + self.msgs[2].receive() + self.msgs[4].receive()
        hi = self.part(self.me, self.hi) + self.msgs[3].receive() + self.msgs[5].receive()
        return lo, hi

    def done(self):
        for m in self.msgs:
            m.done()


def reduce_kernel(
    wz_ref, zh_hbm, wt_ref, hw_hbm, wz_out, zh_out, wt_out, hw_out,
    wz_own, zh_ref, hw_ref, core_in, xsum, zsum, wt_core, wt_in, wt_mid,
    own_sem, core_sem, wa_sem, wb_sem, wc_sem, wd_sem, we_sem, *bufs,
):
    xbufs, ybufs, zbufs, zybufs, hwbufs = (bufs[3 * i:3 * i + 3] for i in range(5))
    ha, wa = lax.axis_index("ha"), lax.axis_index("wa")
    yh, x, c = ha // 8, lax.rem(ha // 2, 4), lax.rem(ha, 2)
    yl, z = wa // 4, lax.rem(wa, 4)
    span = wz_ref.shape[3] // CHUNKS
    n_ha, n_wa = wt_ref.shape[0], 8

    def on_x(to):
        return (yh * 8 + to * 2 + c, wa)

    def on_z(to):
        return (ha, yl * 4 + to)

    sibling = (ha + 1 - 2 * c, wa)
    across = (lax.rem(ha + 8, 16), wa)
    beside = (ha, lax.rem(wa + 4, 8))
    corner = (lax.rem(ha + 8, 16), lax.rem(wa + 4, 8))
    rows_own = zh_ref.shape[2] // 2

    barrier = pltpu.get_barrier_semaphore()

    def greet_ha(i, carry):
        pl.semaphore_signal(barrier, inc=1, device_id=(lax.rem(ha + i, n_ha), wa), device_id_type=MESH)
        return carry

    def greet_wa(i, carry):
        pl.semaphore_signal(barrier, inc=1, device_id=(ha, lax.rem(wa + i, n_wa)), device_id_type=MESH)
        return carry

    loads = [
        pltpu.make_async_copy(zh_hbm, zh_ref, own_sem.at[0]),
        pltpu.make_async_copy(hw_hbm.at[pl.ds(hw_out.shape[0], hw_out.shape[0])], hw_ref, own_sem.at[1]),
        pltpu.make_async_copy(wz_ref.at[c], wz_own, own_sem.at[2]),
    ]
    for cp in loads:
        cp.start()
    lax.fori_loop(1, n_ha, greet_ha, 0)
    lax.fori_loop(1, n_wa, greet_wa, 0)
    pl.semaphore_signal(barrier, inc=1, device_id=corner, device_id_type=MESH)
    pl.semaphore_wait(barrier, n_ha + n_wa - 1)

    def send(source, dest, sems, to):
        return pltpu.make_async_remote_copy(
            src_ref=source, dst_ref=dest, send_sem=sems.at[0], recv_sem=sems.at[1],
            device_id=to, device_id_type=MESH)

    core = [
        send(wz_ref.at[1 - c, :, :, pl.ds(k * span, span)], core_in.at[:, :, pl.ds(k * span, span)],
             core_sem.at[k], sibling)
        for k in range(CHUNKS)
    ]
    peers = n_ha // 2
    group = ha // 2
    wt_own = pl.ds(c * peers, peers)
    wt_swap = send(wt_ref.at[pl.ds((1 - c) * peers, peers)], wt_core, wd_sem, sibling)
    wt_swap.start()
    for k in range(CHUNKS):
        core[k].start()
    zring = Ring(zh_ref, zbufs, 0, on_z, z, zh_ref.shape[2], 0)
    loads[0].wait()
    zring.begin()

    def wt_first(i):
        to = lax.rem(group + i, peers)
        return pltpu.make_async_remote_copy(
            src_ref=wt_core.at[to], dst_ref=wt_in.at[group], send_sem=wa_sem.at[0], recv_sem=wa_sem.at[1],
            device_id=(to * 2 + c, wa), device_id_type=MESH)

    def wt_second(i):
        to = lax.rem(wa + i, n_wa)
        return pltpu.make_async_remote_copy(
            src_ref=wt_mid.at[wa], dst_ref=wt_mid.at[wa], send_sem=wb_sem.at[0], recv_sem=wb_sem.at[1],
            device_id=(ha, to), device_id_type=MESH)

    def wt_third(i):
        to = lax.rem(group + i, peers)
        piece = wt_out.at[c * peers + group]
        return pltpu.make_async_remote_copy(
            src_ref=piece, dst_ref=piece, send_sem=wc_sem.at[0], recv_sem=wc_sem.at[1],
            device_id=(to * 2 + c, wa), device_id_type=MESH)

    def start(make, n):
        def go(i, carry):
            make(i).start()
            return carry
        lax.fori_loop(1, n, go, 0)

    def all_of(buf, sems, n, to):
        many = buf.at[pl.ds(0, n - 1)]
        return pltpu.make_async_remote_copy(
            src_ref=many, dst_ref=many, send_sem=sems.at[0], recv_sem=sems.at[1], device_id=to, device_id_type=MESH)

    first_all, second_all, third_all = (
        all_of(wt_in, wa_sem, peers, sibling), all_of(wt_mid, wb_sem, n_wa, beside), all_of(wt_out, wc_sem, peers, sibling))
    wt_swap.wait_recv()
    wt_core[...] += wt_ref[wt_own]
    start(wt_first, peers)
    chans = hw_ref.shape[1]
    back = coded(hwbufs, 0, across)
    loads[1].wait()
    back.send(hw_ref[...].reshape(-1, 128, chans))
    loads[2].wait()
    rings = []
    for k in range(CHUNKS):
        rows = pl.ds(k * span, span)
        core[k].wait_recv()
        core_in[:, :, rows] += wz_own[:, :, rows]
        rings.append(Ring(core_in, xbufs, 6 * k, on_x, x, span, k * span))
        rings[k].begin()
    zring.relay()
    first_all.wait_recv()
    wt_in[group] = wt_core[group]
    tot = wt_in[0]
    for i in range(1, peers):
        tot += wt_in[i]
    wt_mid[wa] = tot
    start(wt_second, n_wa)
    for k in range(CHUNKS):
        rings[k].relay()
    second_all.wait_recv()
    tot = wt_mid[0]
    for i in range(1, n_wa):
        tot += wt_mid[i]
    wt_out[c * peers + group] = tot
    start(wt_third, peers)
    zsum[0], zsum[1] = zring.finish()
    zys = [coded(zybufs, i, to) for i, to in enumerate((beside, corner, across))]
    zys[0].send(zsum[0, pl.ds(1 - yl, 1)])
    zys[1].send(zsum[1, pl.ds(1 - yl, 1)])
    zys[2].send(zsum[1, pl.ds(yl, 1)])
    ys = []
    for k in range(CHUNKS):
        rows = pl.ds(k * span, span)
        lo, hi = rings[k].finish()
        xsum[:, k, 0:span * 4], xsum[:, k, span * 4:] = lo, hi
        ys.append(coded(ybufs, k, across))
        ys[k].send(xsum[pl.ds(1 - yh, 1), k])
    third_all.wait_recv()
    wt_last = send(wt_out.at[wt_own], wt_out.at[wt_own], we_sem, sibling)
    wt_last.start()
    total = zsum[0, pl.ds(yl, 1)]
    for m in zys:
        total += m.receive()
    zh_out[...] = total.reshape(zh_out.shape)
    for k in range(CHUNKS):
        rows = pl.ds(k * span, span)
        wz_out[pl.ds(k * span, span)] = (xsum[pl.ds(yh, 1), k] + ys[k].receive()).reshape(span, 8, chans)
    hw_out[...] = back.receive().reshape(hw_out.shape)
    for k in range(CHUNKS):
        core[k].wait_send()
        rings[k].done()
        ys[k].done()
    zring.done()
    for m in zys + [back]:
        m.done()
    wt_last.wait()
    for cp in (wt_swap, first_all, second_all, third_all):
        cp.wait_send()


def reduce_all(wz, zh, wt, hw):
    half_w, chans = wz.shape[3], wz.shape[5]
    rows = zh.shape[2]
    span = half_w // CHUNKS
    vmem = pl.BlockSpec(memory_space=pltpu.VMEM)
    hbm = pl.BlockSpec(memory_space=pl.ANY)
    buf = lambda *s: pltpu.VMEM(s, F32)
    dma = lambda *s: pltpu.SemaphoreType.DMA(s)
    return pl.pallas_call(
        reduce_kernel,
        out_shape=(
            jax.ShapeDtypeStruct((half_w, 8, chans), F32),
            jax.ShapeDtypeStruct((rows // 2, 8, chans), F32),
            jax.ShapeDtypeStruct(wt.shape, F32),
            jax.ShapeDtypeStruct((hw.shape[0] // 2, chans), F32),
        ),
        in_specs=[hbm, hbm, vmem, hbm],
        out_specs=[vmem] * 4,
        scratch_shapes=[
            buf(2, 4, half_w, 8, chans),
            buf(*zh.shape),
            buf(hw.shape[0] // 2, chans),
            buf(2, 4, half_w, 8, chans),
            buf(2, CHUNKS, span * 8, chans),
            buf(2, 2, rows * 4, chans),
            buf(8, *wt.shape[1:]),
            buf(8, *wt.shape[1:]),
            buf(8, *wt.shape[1:]),
            dma(3), dma(CHUNKS, 2), dma(2), dma(2), dma(2), dma(2), dma(2),
            *coded_buffers(6 * CHUNKS, 2, span * 4, chans),
            *coded_buffers(CHUNKS, 1, span * 8, chans),
            *coded_buffers(6, 2, rows * 4, chans),
            *coded_buffers(3, 1, rows * 4, chans),
            *coded_buffers(1, hw.shape[0] // 256, 128, chans),
        ],
        compiler_params=pltpu.CompilerParams(
            collective_id=0, has_side_effects=True, vmem_limit_bytes=REDUCE_VMEM),
    )(wz, zh, wt, hw)


def local(hw_plane, zh_plane, wz_plane, w_in, b_in, w_out, b_out, run_index, run_count, labels):
    rows, cols, chans = hw_plane.shape
    depth = zh_plane.shape[0]
    ncls = w_out.shape[1]
    hw_rows = hw_plane.reshape(rows * cols, chans)
    idx, hwx, zh2, labx = exchange(run_index, hw_rows, zh_plane, labels[0])
    hw, zh, wz, wt = decode_runs(
        run_index, idx, run_count, hw_rows, hwx, zh2, wz_plane.reshape(cols // 2, 2 * depth, chans),
        labels[0], labx, w_in, b_in, w_out, b_out,
    )
    wz_grad, zh_grad, wt, back = reduce_all(
        wz.reshape(2, 2, 4, cols // 2, 8, chans), zh.reshape(2, 4, 2 * rows, 8, chans), wt.reshape(16, -1, chans), hw)
    hw_grad, wz_grad, zh_grad, gwi, gbi, gwo, gbo = finish(
        run_index, run_count, hw, back, wz_grad, zh_grad, wt.reshape(-1, chans), rows * cols, w_out.shape[0], ncls)
    return (hw_grad.reshape(rows, cols, chans), zh_grad, wz_grad.reshape(cols, 4, chans), gwi, gbi[0], gwo.T, gbo[0])


def solution(mesh):
    placed = (
        P("ha", "wa", None),
        P(None, "ha", None),
        P("wa", None, None),
        P(),
        P(),
        P(),
        P(),
        P(("ha", "wa"), None),
        P(("ha", "wa")),
        P(("ha", "wa"), None, None),
    )
    return jax.shard_map(
        local,
        mesh=mesh,
        in_specs=placed,
        out_specs=(P("ha", "wa", None), P("wa", "ha", None), P("wa", "ha", None), P(), P(), P(), P()),
        check_vma=False,
    )
```
